256 devices in a mesh: own: 16 (over z, core), rep: 16 (over x, y).
Axes of the slice: x: 4, y: 4, z: 8, core: 2. Of those that a mesh axis runs over, the one named last changes fastest.
Arguments:
- histories: bfloat16 [8192, 64, 1024], P(('own', 'rep')), may hold values from -6 to 6
- lengths: int32 [8192], P(('own', 'rep')), may hold values from 1 to 64, as said below
- counts: int32 [4096], P(('own', 'rep')), may hold values from 0 to 2, as said below
- imp_user: int32 [65536], P(('own', 'rep')), may hold values from 0 to 511, as said below
- items: bfloat16 [65536, 1024], P(('own', 'rep')), may hold values from -0.8984375 to 0.8984375
- labels: int32 [65536], P(('own', 'rep')), may hold values 0 or 1
- w_uvqk: bfloat16 [1024, 2048], replicated, may hold values from -0.1875 to 0.1875
- w_out: bfloat16 [512, 1024], replicated, may hold values from -0.25 to 0.25
Outputs:
- logits: float32 [65536], P(('own', 'rep'))
- grad_out: bfloat16 [512, 1024], replicated
- grad_gate: bfloat16 [1024, 512], replicated
The draws below stay inside these ranges and needn't reach their ends.
Inputs may be any that keep to these rules, and one draw needn't show every extreme that they name: `counts`: on every data replica one owner receives 2 live slots from every shard; on every replica the first shard along own sends the first owner at least one live slot, and the last shard along own sends the last owner exactly 2 live slots. `lengths`: every shard has a live slot of length 64. `imp_user`: each impression names a live slot held by a shard of its own data replica; on every replica the smallest and the largest index are named.
All inputs are finite; a program needn't handle non-finite values. No bound on the sum of `labels` on one device may be relied on, other than what follows from the above.
Results may differ from the reference program's by a relative error of at most 0.017.
Values may be sent and summed in bfloat16 or wider, within the bound.
A program may use at most 128 MiB of HBM per device.

```python
import jax
import jax.numpy as jnp
from jax import lax

D = 1024
HEADS = 4
HEAD = 128
HIST = 64
CAP = 2
IMP_DEV = 256
SLOTS_ALL = 8192
IMPS = 65536
N_OWN = 16
N_REP = 16


def shared_counts(key):
    replica_full = jax.random.randint(jax.random.fold_in(key, 11), (N_REP,), 0, N_OWN)
    raw = jax.random.randint(jax.random.fold_in(key, 12), (N_OWN, N_REP, N_OWN), 0, CAP + 1)
    owners = jnp.arange(N_OWN, dtype=jnp.int32)
    filled = owners[None, None, :] == replica_full[None, :, None]
    table = jnp.where(filled, CAP, raw).astype(jnp.int32)
    table = table.at[0, :, 0].set(jnp.maximum(table[0, :, 0], 1))
    table = table.at[N_OWN - 1, :, N_OWN - 1].set(CAP)
    return (table.astype(jnp.int32), replica_full)


def draw_counts(key, part):
    table, _ = shared_counts(key)
    return table.reshape(-1)


def draw_lengths(key, part):
    table, replica_full = shared_counts(key)
    key = jax.random.fold_in(key, 2)
    raw = jax.random.randint(key, (N_OWN, N_REP, N_OWN, CAP), 1, HIST + 1)
    owners = jnp.arange(N_OWN, dtype=jnp.int32)
    first = (owners[None, None, :, None] == replica_full[None, :, None, None]) & (jnp.arange(CAP)[None, None, None, :] == 0)
    return jnp.where(first, HIST, raw).astype(jnp.int32).reshape(-1)


def draw_imp_user(key, part):
    table, _ = shared_counts(key)
    key = jax.random.fold_in(key, 3)
    live = (jnp.arange(CAP, dtype=jnp.int32)[None, None, None, :] < table[..., None]).astype(jnp.int32)
    live = jnp.transpose(live, (1, 2, 0, 3)).reshape(N_REP, N_OWN * N_OWN * CAP)
    cumul = jnp.cumsum(live, -1)
    totals = cumul[:, -1]
    picks = jax.random.randint(key, (N_OWN, N_REP, IMP_DEV), 0, 1048576)
    wanted = picks % totals[None, :, None]
    wanted = wanted.at[0, :, 0].set(0)
    wanted = wanted.at[N_OWN - 1, :, IMP_DEV - 1].set(totals - 1)
    chosen = jnp.sum((cumul[None, :, None, :] <= wanted[..., None]).astype(jnp.int32), -1)
    return chosen.reshape(-1).astype(jnp.int32)


def set_ends(entries, key, least, largest):
    index_at = [jax.random.randint(jax.random.fold_in(key, axis), (), 0, length) for axis, length in enumerate(entries.shape)]
    longest = entries.shape.index(max(entries.shape))
    neighbour = index_at[:longest] + [(index_at[longest] + 1) % entries.shape[longest]] + index_at[longest + 1:]
    return entries.at[tuple(index_at)].set(least).at[tuple(neighbour)].set(largest)


def block_scale(key, dims, cuts, low, high):
    loudness = 1.0
    for axis_at, parts in cuts:
        heights = jax.random.uniform(jax.random.fold_in(jax.random.fold_in(key, 6), axis_at), (parts,), jnp.float32, low / len(cuts), high / len(cuts))
        loudness = loudness * jnp.repeat(jnp.exp(heights), dims[axis_at] // parts).reshape((-1,) + (1,) * (len(dims) - 1 - axis_at))
    return loudness


def bell_draw(own_key, shape, scale, most, cuts=(), kind=jnp.bfloat16):
    gain = block_scale(own_key, shape, cuts, -0.22, 0.18) if cuts else 1.0
    values = jax.random.normal(own_key, shape, jnp.float32) * scale * gain
    return jnp.minimum(jnp.maximum(values, -most), most).astype(kind)


def setup_inputs(seed: int = 0) -> dict:
    key_list = jax.random.split(jax.random.key(seed), 9)
    return {
        "histories": bell_draw(key_list[0], (SLOTS_ALL, HIST, D), 1.0, 6.0, ((0, 256),)),
        "lengths": draw_lengths(jax.random.fold_in(key_list[8], 71), 0),
        "counts": draw_counts(jax.random.fold_in(key_list[8], 71), 0),
        "imp_user": draw_imp_user(jax.random.fold_in(key_list[8], 71), 0),
        "items": bell_draw(key_list[4], (IMPS, D), 0.15, 0.8984375, ((0, 256),)),
        "labels": set_ends((jax.random.randint(key_list[5], (IMPS,), 0, 2) < 1).astype(jnp.int32), jax.random.fold_in(key_list[5], 1), 0, 1),
        "w_uvqk": bell_draw(key_list[6], (D, 4 * HEADS * HEAD), D ** -0.5, 0.1875),
        "w_out": bell_draw(key_list[7], (HEADS * HEAD, D), (HEADS * HEAD) ** -0.5, 0.25),
    }


EPS_NORM = 1e-06
EPS_LAYER = 1e-05

def user_forward(block, spans, w_uvqk):
    width = HEADS * HEAD
    users = block.shape[0]
    feats = block.astype(jnp.float32)
    square = lax.optimization_barrier(jnp.mean(feats * feats, -1, keepdims=True))
    normed = (feats * lax.rsqrt(square + EPS_NORM)).astype(jnp.bfloat16)
    linear = jnp.dot(normed.reshape(-1, D), w_uvqk, preferred_element_type=jnp.float32).reshape(users, HIST, 4 * width)
    active = jax.nn.silu(linear)
    gate_act = active[..., :width]
    values = active[..., width:2 * width].astype(jnp.bfloat16).reshape(users, HIST, HEADS, HEAD)
    queries = active[..., 2 * width:3 * width].astype(jnp.bfloat16).reshape(users, HIST, HEADS, HEAD)
    keyset = active[..., 3 * width:].astype(jnp.bfloat16).reshape(users, HIST, HEADS, HEAD)
    scores = jnp.einsum('bqne,bkne->bnqk', queries.astype(jnp.float32), keyset.astype(jnp.float32)) * HEAD ** (-0.5)
    places = jnp.arange(HIST, dtype=jnp.int32)
    allowed = (places[None, :] <= places[:, None])[None, :, :] & (places[None, None, :] < spans[:, None, None])
    attn = (jax.nn.silu(scores) * allowed[:, None].astype(jnp.float32)).astype(jnp.bfloat16)
    attended = jnp.einsum('bnqk,bkne->bqne', attn.astype(jnp.float32), values.astype(jnp.float32)).reshape(users, HIST, width)
    center = lax.optimization_barrier(jnp.mean(attended, -1, keepdims=True))
    spread = lax.optimization_barrier(jnp.mean((attended - center) ** 2, -1, keepdims=True))
    normal_out = (attended - center) * lax.rsqrt(spread + EPS_LAYER)
    mixed = normal_out * gate_act
    validity = (places[None, :] < spans[:, None]).astype(jnp.float32)
    share = validity / jnp.maximum(spans, 1).astype(jnp.float32)[:, None]
    pooled_y = lax.optimization_barrier(jnp.sum(mixed * share[..., None], 1)).astype(jnp.bfloat16)
    pooled_x = lax.optimization_barrier(jnp.sum(feats * share[..., None], 1))
    gate_in = linear[..., :width]
    sigmoid_gate = jax.nn.sigmoid(gate_in)
    slope = normal_out * (sigmoid_gate + gate_in * sigmoid_gate * (1.0 - sigmoid_gate))
    return (pooled_y, pooled_x, normed, slope, share)

def reference(histories, lengths, counts, imp_user, items, labels, w_uvqk, w_out):
    width = HEADS * HEAD
    slots = N_OWN * CAP
    shards = N_OWN * N_REP
    ranks = jnp.arange(slots * shards, dtype=jnp.int32)
    alive = ranks % CAP < counts[ranks // CAP]
    spans = jnp.where(alive, lengths, 0).astype(jnp.int32)
    blocks = histories.reshape(shards, slots, HIST, D)
    span_blocks = spans.reshape(shards, slots)

    def forward_pool(pieces):
        result = user_forward(pieces[0], pieces[1], w_uvqk)
        return (result[0], result[1])
    pooled_y, pooled_x = lax.map(forward_pool, (blocks, span_blocks))
    pooled_y = pooled_y.reshape(-1, width)
    pooled_x = pooled_x.reshape(-1, D)
    embeds = (pooled_x + jnp.dot(pooled_y, w_out, preferred_element_type=jnp.float32)).astype(jnp.bfloat16)
    order = jnp.arange(imp_user.shape[0], dtype=jnp.int32)
    replica = order // IMP_DEV % N_REP
    owner_of = imp_user // slots
    source = imp_user % slots // CAP
    within = imp_user % CAP
    target = ((source * N_REP + replica) * slots + owner_of * CAP + within).astype(jnp.int32)
    user_rows = embeds[target].astype(jnp.float32)
    logits = lax.optimization_barrier(jnp.sum(user_rows * items.astype(jnp.float32), -1))
    weighted = (jax.nn.sigmoid(logits) - labels.astype(jnp.float32))[:, None] * items.astype(jnp.float32)
    grad_embed = jax.ops.segment_sum(weighted, target, num_segments=slots * shards).astype(jnp.bfloat16)
    grad_out = jnp.dot(pooled_y.T, grad_embed, preferred_element_type=jnp.float32).astype(jnp.bfloat16)
    grad_pool = jnp.dot(grad_embed, w_out.T, preferred_element_type=jnp.float32).astype(jnp.bfloat16)

    def accumulate(total, pieces):
        block, span_row, pool_row = pieces
        result = user_forward(block, span_row, w_uvqk)
        normed, slope, share = (result[2], result[3], result[4])
        grad_pre = (share[..., None] * pool_row[:, None, :].astype(jnp.float32) * slope).astype(jnp.bfloat16)
        term = jnp.dot(normed.reshape(-1, D).T, grad_pre.reshape(-1, width), preferred_element_type=jnp.float32)
        return (total + term, None)
    grad_gate, _ = lax.scan(accumulate, jnp.zeros((D, width), jnp.float32), (blocks, span_blocks, grad_pool.reshape(shards, slots, width)))
    return (logits, grad_out, grad_gate.astype(jnp.bfloat16))
```

```python
import jax
import jax.numpy as jnp
from jax import lax
from jax.experimental import pallas as pl
from jax.experimental.pallas import tpu as pltpu
from jax.sharding import PartitionSpec as P

D = 1024
HEADS = 4
HEAD = 128
HIST = 64
WIDTH = HEADS * HEAD
GROUP = 8
PAIR = 2 * HIST

EPS_NORM = 1e-06
EPS_LAYER = 1e-05


def sigmoid(v):
    return 0.5 * jnp.tanh(0.5 * v) + 0.5


def forward_kernel(spans, col_ref, h_ref, w_ref, px_ref, py_ref, slope_ref, lin):
    group = pl.program_id(0)
    tokens = GROUP * HIST
    x = h_ref[...].reshape(tokens, D)
    lin[...] = jnp.dot(x, w_ref[...], preferred_element_type=jnp.float32)
    span_col = col_ref[...]
    slot = lax.broadcasted_iota(jnp.int32, (GROUP, tokens), 0)
    place = lax.broadcasted_iota(jnp.int32, (GROUP, tokens), 1) - slot * HIST
    live = (place >= 0) & (place < span_col)
    inverse = 1.0 / jnp.maximum(span_col, 1).astype(jnp.float32)
    px_ref[...] = jnp.dot(live.astype(jnp.bfloat16), x, preferred_element_type=jnp.float32) * inverse

    def pair_step(p):
        rows = slice(p * PAIR, (p + 1) * PAIR)
        first = spans[group * GROUP + 2 * p]
        second = spans[group * GROUP + 2 * p + 1]
        feats = h_ref[2 * p : 2 * p + 2].reshape(PAIR, D).astype(jnp.float32)
        scale = lax.rsqrt(jnp.mean(feats * feats, -1, keepdims=True) + EPS_NORM)
        row = lax.broadcasted_iota(jnp.int32, (PAIR, PAIR), 0)
        col = lax.broadcasted_iota(jnp.int32, (PAIR, PAIR), 1)
        allowed = (
            (col <= row)
            & ((row < HIST) | (col >= HIST))
            & (col < jnp.where(col < HIST, first, HIST + second))
        )
        attended = []
        for h in range(HEADS):
            cols = [slice(k * WIDTH + h * HEAD, k * WIDTH + (h + 1) * HEAD) for k in (1, 2, 3)]
            raw = [lin[rows, c] * scale for c in cols]
            value, query, key = [(v * sigmoid(v)).astype(jnp.bfloat16) for v in raw]
            scores = lax.dot_general(
                query, key, (((1,), (1,)), ((), ())), preferred_element_type=jnp.float32
            ) * HEAD ** (-0.5)
            attn = jnp.where(allowed, scores * sigmoid(scores), 0.0).astype(jnp.bfloat16)
            attended.append(jnp.dot(attn, value, preferred_element_type=jnp.float32))
        center = sum(jnp.sum(a, -1, keepdims=True) for a in attended) / WIDTH
        moved = [a - center for a in attended]
        spread = sum(jnp.sum(a * a, -1, keepdims=True) for a in moved) / WIDTH
        norm = lax.rsqrt(spread + EPS_LAYER)
        spot = lax.broadcasted_iota(jnp.int32, (PAIR, 1), 0)
        valid = spot < jnp.where(spot < HIST, first, HIST + second)
        both = jnp.where(spot < HIST, first, second)
        share = jnp.where(valid, 1.0 / jnp.maximum(both, 1).astype(jnp.float32), 0.0)
        back = share * scale
        for h in range(HEADS):
            gate = lin[rows, h * HEAD : (h + 1) * HEAD] * scale
            sig = sigmoid(gate)
            act = gate * sig
            normal = moved[h] * norm
            mixed = normal * act * share
            for k in range(2):
                pooled = jnp.sum(mixed[k * HIST : (k + 1) * HIST], 0, keepdims=True)
                py_ref[2 * p + k : 2 * p + k + 1, h * HEAD : (h + 1) * HEAD] = pooled
            slope = back * normal * (sig + act * (1.0 - sig))
            slope_ref[h * HEAD : (h + 1) * HEAD, rows] = slope.T.astype(jnp.bfloat16)

    for p in range(GROUP // 2):
        pair_step(p)


def forward(histories, spans, w_uvqk):
    slots = histories.shape[0]
    steps = slots // GROUP
    return pl.pallas_call(
        forward_kernel,
        grid_spec=pltpu.PrefetchScalarGridSpec(
            num_scalar_prefetch=1,
            grid=(steps,),
            in_specs=[
                pl.BlockSpec((GROUP, 1), lambda i, s: (i, 0)),
                pl.BlockSpec((GROUP, HIST, D), lambda i, s: (i, 0, 0)),
                pl.BlockSpec((D, 4 * WIDTH), lambda i, s: (0, 0)),
            ],
            out_specs=[
                pl.BlockSpec((GROUP, D), lambda i, s: (i, 0)),
                pl.BlockSpec((GROUP, WIDTH), lambda i, s: (i, 0)),
                pl.BlockSpec((WIDTH, GROUP * HIST), lambda i, s: (0, i)),
            ],
            scratch_shapes=[pltpu.VMEM((GROUP * HIST, 4 * WIDTH), jnp.float32)],
        ),
        out_shape=[
            jax.ShapeDtypeStruct((slots, D), jnp.float32),
            jax.ShapeDtypeStruct((slots, WIDTH), jnp.float32),
            jax.ShapeDtypeStruct((WIDTH, slots * HIST), jnp.bfloat16),
        ],
        compiler_params=pltpu.CompilerParams(vmem_limit_bytes=48 * 1024 * 1024),
        name="forward",
    )(spans, spans[:, None], histories, w_uvqk)


def body(histories, lengths, counts, imp_user, items, labels, w_uvqk, w_out):
    slots = histories.shape[0]
    owners = lax.axis_size("own")
    capacity = slots // owners
    ranks = jnp.arange(slots, dtype=jnp.int32)
    alive = ranks % capacity < jnp.repeat(counts, capacity)
    spans = jnp.where(alive, lengths, 0)
    px, py, slope = forward(histories, spans, w_uvqk)
    px_all = lax.all_gather(px.astype(jnp.bfloat16), "own", axis=0, tiled=True)
    py_all = lax.all_gather(py.astype(jnp.bfloat16), "own", axis=0, tiled=True)
    place = (imp_user % slots) // capacity * slots + imp_user // slots * capacity + imp_user % capacity
    columns = jnp.arange(owners * slots, dtype=jnp.int32)
    select = place[:, None] == columns[None, :]
    item_w = lax.dot_general(items, w_out, (((1,), (1,)), ((), ())), preferred_element_type=jnp.float32)
    table = lax.dot_general(
        items, px_all, (((1,), (1,)), ((), ())), preferred_element_type=jnp.float32
    ) + lax.dot_general(
        item_w.astype(jnp.bfloat16), py_all, (((1,), (1,)), ((), ())), preferred_element_type=jnp.float32
    )
    logits = jnp.sum(jnp.where(select, table, 0.0), -1)
    error = (jax.nn.sigmoid(logits) - labels.astype(jnp.float32))[:, None]
    pick = select.astype(jnp.bfloat16)
    pool_part = lax.dot_general(
        pick, (error * item_w).astype(jnp.bfloat16), (((0,), (0,)), ((), ())), preferred_element_type=jnp.float32
    )
    pool = lax.psum_scatter(pool_part.astype(jnp.bfloat16), "own", scatter_dimension=0, tiled=True)
    rows = jnp.dot(pick, py_all, preferred_element_type=jnp.float32).astype(jnp.bfloat16)
    out_term = lax.dot_general(
        rows, (error * items.astype(jnp.float32)).astype(jnp.bfloat16), (((0,), (0,)), ((), ())),
        preferred_element_type=jnp.float32,
    )
    spread = jnp.repeat(pool.T.astype(jnp.float32), HIST, axis=1)
    grad_pre = (spread * slope.astype(jnp.float32)).astype(jnp.bfloat16)
    gate_term = jnp.dot(grad_pre, histories.reshape(-1, D), preferred_element_type=jnp.float32)
    out_sum, gate_sum = lax.psum(
        (out_term.astype(jnp.bfloat16), gate_term.astype(jnp.bfloat16)), ("own", "rep")
    )
    return (logits, out_sum, gate_sum.T)


def solution(mesh):
    return jax.shard_map(
        body,
        mesh=mesh,
        in_specs=(
            P(("own", "rep"), None, None),
            P(("own", "rep")),
            P(("own", "rep")),
            P(("own", "rep")),
            P(("own", "rep"), None),
            P(("own", "rep")),
            P(),
            P(),
        ),
        out_specs=(P(("own", "rep")), P(), P()),
        check_vma=False,
    )
```

```python
import functools

import jax
import jax.numpy as jnp
from jax import lax
from jax.experimental import pallas as pl
from jax.experimental.pallas import tpu as pltpu
from jax.sharding import PartitionSpec as P

D = 1024
HEADS = 4
HEAD = 128
HIST = 64
WIDTH = HEADS * HEAD
GROUP = 8
PAIR = 2 * HIST
CORES = 2
TILE = 16
LANES = 128
MESH = pl.DeviceIdType.MESH

EPS_NORM = 1e-06
EPS_LAYER = 1e-05


def sigmoid(v):
    return 0.5 * jnp.tanh(0.5 * v) + 0.5


def forward_kernel(spans, col_ref, h_ref, w_ref, px_ref, py_ref, slope_ref, lin):
    group = pl.program_id(0)
    tokens = GROUP * HIST
    x = h_ref[...].reshape(tokens, D)
    lin[...] = jnp.dot(x, w_ref[...], preferred_element_type=jnp.float32)
    span_col = col_ref[...]
    slot = lax.broadcasted_iota(jnp.int32, (GROUP, tokens), 0)
    place = lax.broadcasted_iota(jnp.int32, (GROUP, tokens), 1) - slot * HIST
    live = (place >= 0) & (place < span_col)
    inverse = 1.0 / jnp.maximum(span_col, 1).astype(jnp.float32)
    px_ref[...] = jnp.dot(live.astype(jnp.bfloat16), x, preferred_element_type=jnp.float32) * inverse

    def pair_step(p):
        rows = slice(p * PAIR, (p + 1) * PAIR)
        first = spans[group * GROUP + 2 * p]
        second = spans[group * GROUP + 2 * p + 1]
        feats = h_ref[2 * p : 2 * p + 2].reshape(PAIR, D).astype(jnp.float32)
        scale = lax.rsqrt(jnp.mean(feats * feats, -1, keepdims=True) + EPS_NORM)
        row = lax.broadcasted_iota(jnp.int32, (PAIR, PAIR), 0)
        col = lax.broadcasted_iota(jnp.int32, (PAIR, PAIR), 1)
        allowed = (
            (col <= row)
            & ((row < HIST) | (col >= HIST))
            & (col < jnp.where(col < HIST, first, HIST + second))
        )
        attended = []
        for h in range(HEADS):
            cols = [slice(k * WIDTH + h * HEAD, k * WIDTH + (h + 1) * HEAD) for k in (1, 2, 3)]
            raw = [lin[rows, c] * scale for c in cols]
            value, query, key = [(v * sigmoid(v)).astype(jnp.bfloat16) for v in raw]
            scores = lax.dot_general(
                query, key, (((1,), (1,)), ((), ())), preferred_element_type=jnp.float32
            ) * HEAD ** (-0.5)
            attn = jnp.where(allowed, scores * sigmoid(scores), 0.0).astype(jnp.bfloat16)
            attended.append(jnp.dot(attn, value, preferred_element_type=jnp.float32))
        center = sum(jnp.sum(a, -1, keepdims=True) for a in attended) / WIDTH
        moved = [a - center for a in attended]
        spread = sum(jnp.sum(a * a, -1, keepdims=True) for a in moved) / WIDTH
        norm = lax.rsqrt(spread + EPS_LAYER)
        spot = lax.broadcasted_iota(jnp.int32, (PAIR, 1), 0)
        valid = spot < jnp.where(spot < HIST, first, HIST + second)
        both = jnp.where(spot < HIST, first, second)
        share = jnp.where(valid, 1.0 / jnp.maximum(both, 1).astype(jnp.float32), 0.0)
        back = share * scale
        for h in range(HEADS):
            gate = lin[rows, h * HEAD : (h + 1) * HEAD] * scale
            sig = sigmoid(gate)
            act = gate * sig
            normal = moved[h] * norm
            mixed = normal * act * share
            for k in range(2):
                pooled = jnp.sum(mixed[k * HIST : (k + 1) * HIST], 0, keepdims=True)
                py_ref[2 * p + k : 2 * p + k + 1, h * HEAD : (h + 1) * HEAD] = pooled
            slope = back * normal * (sig + act * (1.0 - sig))
            slope_ref[h * HEAD : (h + 1) * HEAD, rows] = slope.T.astype(jnp.bfloat16)

    for p in range(GROUP // 2):
        pair_step(p)


def forward(histories, spans, w_uvqk):
    slots = histories.shape[0]
    steps = slots // GROUP
    return pl.pallas_call(
        forward_kernel,
        grid_spec=pltpu.PrefetchScalarGridSpec(
            num_scalar_prefetch=1,
            grid=(steps,),
            in_specs=[
                pl.BlockSpec((GROUP, 1), lambda i, s: (i, 0)),
                pl.BlockSpec((GROUP, HIST, D), lambda i, s: (i, 0, 0)),
                pl.BlockSpec((D, 4 * WIDTH), lambda i, s: (0, 0)),
            ],
            out_specs=[
                pl.BlockSpec((GROUP, D), lambda i, s: (i, 0)),
                pl.BlockSpec((GROUP, WIDTH), lambda i, s: (i, 0)),
                pl.BlockSpec((WIDTH, GROUP * HIST), lambda i, s: (0, i)),
            ],
            scratch_shapes=[pltpu.VMEM((GROUP * HIST, 4 * WIDTH), jnp.float32)],
        ),
        out_shape=[
            jax.ShapeDtypeStruct((slots, D), jnp.float32),
            jax.ShapeDtypeStruct((slots, WIDTH), jnp.float32),
            jax.ShapeDtypeStruct((WIDTH, slots * HIST), jnp.bfloat16),
        ],
        compiler_params=pltpu.CompilerParams(vmem_limit_bytes=48 * 1024 * 1024),
        name="forward",
    )(spans, spans[:, None], histories, w_uvqk)


def dot(a, b):
    return jnp.dot(a, b, preferred_element_type=jnp.float32)


def dot_t(a, b):
    return lax.dot_general(a, b, (((1,), (1,)), ((), ())), preferred_element_type=jnp.float32)


def exchange_kernel(
    nz, nr, user_ref, label_ref, px_ref, py_ref, items_hbm, w_hbm, slope_hbm, hist_hbm,
    logit_ref, out_ref, gate_ref,
    items, w_out, slope, hist, users, pool_send, pool_core, pool_mine, pool_z, pool_got,
    pre, mine, core_send, core_got, half, plane_got, row_sum, piece_got,
    load_sem, user_send, user_recv, relay_send, relay_recv, pcore_sem, pz_send, pz_recv,
    core_sem, plane_send, plane_recv, piece_send, piece_recv, back_send, back_recv,
    wide_send, wide_recv, last_send, last_recv,
):
    own = lax.axis_index("own")
    rep = lax.axis_index("rep")
    z, c = own // CORES, own % CORES
    other = 1 - c
    slots = px_ref.shape[0]
    side = nz * slots
    block = WIDTH // nr
    half_w = D // CORES
    grads = (out_ref, gate_ref)

    loads = [
        pltpu.make_async_copy(source, target, load_sem.at[k])
        for k, (source, target) in enumerate(
            ((items_hbm, items), (w_hbm, w_out), (slope_hbm, slope), (hist_hbm, hist))
        )
    ]
    for load in loads:
        load.start()

    def z_id(k):
        return ((z + k) % nz * CORES + c, rep)

    def plane_id(k):
        return (own, (rep + k) % nr)

    sibling = (z * CORES + other, rep)

    def copy(source, target, send, recv, device):
        return pltpu.make_async_remote_copy(
            src_ref=source, dst_ref=target, send_sem=send, recv_sem=recv,
            device_id=device, device_id_type=MESH,
        )

    def each(count, step):
        def run(k, carry):
            step(k)
            return carry
        lax.fori_loop(1, count, run, 0)

    barrier = pltpu.get_barrier_semaphore()
    each(nz, lambda k: pl.semaphore_signal(barrier, inc=1, device_id=z_id(k), device_id_type=MESH))
    each(nr, lambda k: pl.semaphore_signal(barrier, inc=1, device_id=plane_id(k), device_id_type=MESH))
    pl.semaphore_signal(barrier, inc=1, device_id=sibling, device_id_type=MESH)
    pl.semaphore_wait(barrier, nz - 1 + nr - 1 + 1)

    at = c * nz + z
    users[at, :, 0:D] = px_ref[...].astype(jnp.bfloat16)
    users[at, :, D : D + WIDTH] = py_ref[...].astype(jnp.bfloat16)

    def user_copy(k):
        return copy(users.at[at], users.at[at], user_send.at[k], user_recv.at[z], z_id(k))

    def user_relay(zz):
        spot = users.at[c * nz + zz]
        return copy(spot, spot, relay_send.at[zz], relay_recv.at[zz], sibling)

    def user_wait(zz):
        spot = users.at[c * nz + zz]
        copy(spot, spot, user_send.at[0], user_recv.at[zz], sibling).wait_recv()

    def relay_wait(zz):
        spot = users.at[other * nz + zz]
        copy(spot, spot, relay_send.at[zz], relay_recv.at[zz], sibling).wait_recv()

    each(nz, lambda k: user_copy(k).start())
    user_relay(z).start()

    loads[0].wait()
    loads[1].wait()
    item_w = dot_t(items[...], w_out[...]).astype(jnp.bfloat16)

    def pass_on(k):
        zz = (z + k) % nz
        user_wait(zz)
        user_relay(zz).start()

    each(nz, pass_on)
    relay_wait(z)
    each(nz, lambda k: relay_wait((z + k) % nz))

    index = user_ref[...]
    source = (index % slots) // 2
    place = (source % CORES) * side + (source // CORES) * slots + index // slots * 2 + index % 2
    table = dot_t(users[:, :, 0:D].reshape(2 * side, D), items[...]) + dot_t(
        users[:, :, D : D + WIDTH].reshape(2 * side, WIDTH), item_w
    )
    imps = index.shape[1]
    picked = lax.broadcasted_iota(jnp.int32, (2 * side, imps), 0) == place
    logits = jnp.sum(jnp.where(picked, table, 0.0), 0, keepdims=True)
    logit_ref[...] = logits
    error = sigmoid(logits) - label_ref[...].astype(jnp.float32)

    line = lax.broadcasted_iota(jnp.int32, (side, imps), 0)

    def pool_side(core):
        weight = jnp.where(line + core * side == place, error, 0.0).astype(jnp.bfloat16)
        return dot(weight, item_w)

    pool_send[...] = pool_side(other).astype(jnp.bfloat16).reshape(nz, slots, WIDTH)
    pool_copy = copy(pool_send, pool_core, pcore_sem.at[0], pcore_sem.at[1], sibling)
    pool_copy.start()
    pool_mine[...] = pool_side(c).reshape(nz, slots, WIDTH)

    turned = users[:, :, D : D + WIDTH].reshape(2 * side, WIDTH).astype(jnp.float32).T.astype(jnp.bfloat16)
    chosen = dot(turned, picked.astype(jnp.bfloat16))
    chosen = (chosen * error).astype(jnp.bfloat16)

    def columns(core, k=0, size=half_w):
        return pl.ds(pl.multiple_of(core * half_w + k * size, size), size)

    def core_copy(a):
        return copy(core_send.at[a], core_got.at[a], core_sem.at[a, 0], core_sem.at[a, 1], sibling)

    core_send[0] = dot(chosen, items[:, columns(other)]).astype(jnp.bfloat16)
    core_copy(0).start()
    pool_copy.wait()
    pool_z[...] = (pool_mine[...] + pool_core[...].astype(jnp.float32)).astype(jnp.bfloat16)

    def pool_out(k):
        zz = (z + k) % nz
        return copy(pool_z.at[zz], pool_got.at[z], pz_send.at[k], pz_recv.at[z], z_id(k))

    each(nz, lambda k: pool_out(k).start())
    mine[0] = dot(chosen, items[:, columns(c)])

    def plane_rows(k):
        return pl.ds(pl.multiple_of((rep + k) % nr * block, block), block)

    def plane_copy(a, k):
        return copy(
            half.at[a, plane_rows(k)], plane_got.at[a, rep], plane_send.at[a, k], plane_recv.at[a, rep], plane_id(k)
        )

    def core_end(a):
        core_copy(a).wait()
        half[a] = (mine[a] + core_got[a].astype(jnp.float32)).astype(jnp.bfloat16)
        each(nr, lambda k: plane_copy(a, k).start())

    def piece_spot(zz):
        return (
            pl.multiple_of(zz // 4 * TILE, TILE),
            pl.multiple_of(zz % 4 * LANES, LANES),
        )

    def piece_copy(a, k):
        down, across = piece_spot((z + k) % nz)
        return copy(
            row_sum.at[a, pl.ds(down, TILE), pl.ds(across, LANES)], piece_got.at[a, z],
            piece_send.at[a, k], piece_recv.at[a, z], z_id(k),
        )

    def plane_end(a):
        def add(k, total):
            rr = (rep + k) % nr
            spot = plane_got.at[a, rr]
            copy(spot, spot, plane_send.at[a, 0], plane_recv.at[a, rr], sibling).wait_recv()
            return total + spot[...].astype(jnp.float32)
        total = half[a, plane_rows(0)].astype(jnp.float32)
        row_sum[a] = lax.fori_loop(1, nr, add, total).astype(jnp.bfloat16)
        each(nz, lambda k: piece_copy(a, k).start())

    def final_spot(a, zz):
        down, across = piece_spot(zz)
        rows = pl.ds(pl.multiple_of(rep * block + down, TILE), TILE)
        return grads[a].at[rows, pl.ds(pl.multiple_of(c * half_w + across, LANES), LANES)]

    def back_copy(a, k):
        spot = final_spot(a, z)
        return copy(spot, spot, back_send.at[a, k], back_recv.at[a, z], z_id(k))

    def piece_end(a):
        down, across = piece_spot(z)
        def add(k, total):
            zz = (z + k) % nz
            spot = piece_got.at[a, zz]
            copy(spot, spot, piece_send.at[a, 0], piece_recv.at[a, zz], sibling).wait_recv()
            return total + spot[...].astype(jnp.float32)
        total = row_sum[a, pl.ds(down, TILE), pl.ds(across, LANES)].astype(jnp.float32)
        final_spot(a, z)[...] = lax.fori_loop(1, nz, add, total).astype(jnp.bfloat16)
        each(nz, lambda k: back_copy(a, k).start())

    def wide_spot(a, core, k):
        return grads[a].at[plane_rows(k), columns(core)]

    def wide_copy(a, k):
        spot = wide_spot(a, c, 0)
        return copy(spot, spot, wide_send.at[a, k], wide_recv.at[a, rep], plane_id(k))

    def last_copy(a, k):
        spot = wide_spot(a, c, k)
        rr = (rep + k) % nr
        return copy(spot, spot, last_send.at[a, rr], last_recv.at[a, rr], sibling)

    def back_end(a):
        def wait(k):
            zz = (z + k) % nz
            spot = final_spot(a, zz)
            copy(spot, spot, back_send.at[a, 0], back_recv.at[a, zz], sibling).wait_recv()
        each(nz, wait)
        each(nr, lambda k: wide_copy(a, k).start())
        last_copy(a, 0).start()

    def wide_end(a):
        def step(k):
            rr = (rep + k) % nr
            spot = wide_spot(a, c, k)
            copy(spot, spot, wide_send.at[a, 0], wide_recv.at[a, rr], sibling).wait_recv()
            last_copy(a, k).start()
        each(nr, step)

    def last_end(a):
        def step(k):
            rr = (rep + k) % nr
            spot = wide_spot(a, other, k)
            copy(spot, spot, last_send.at[a, 0], last_recv.at[a, rr], sibling).wait_recv()
        step(0)
        each(nr, step)

    core_end(0)

    def pool_add(k, total):
        zz = (z + k) % nz
        spot = pool_got.at[zz]
        copy(spot, spot, pz_send.at[0], pz_recv.at[zz], sibling).wait_recv()
        return total + spot[...].astype(jnp.float32)

    loads[2].wait()
    loads[3].wait()
    pool = lax.fori_loop(1, nz, pool_add, pool_z[z].astype(jnp.float32))
    pool_t = pool.astype(jnp.bfloat16).astype(jnp.float32).T.astype(jnp.bfloat16)
    tokens = slots * HIST
    slot = lax.broadcasted_iota(jnp.int32, (slots, tokens), 0)
    event = lax.broadcasted_iota(jnp.int32, (slots, tokens), 1)
    holds = (event // HIST == slot).astype(jnp.bfloat16)
    pre[...] = (dot(pool_t, holds) * slope[...].astype(jnp.float32)).astype(jnp.bfloat16)

    quarter = half_w // 2

    def gate_part(core, k):
        return dot(pre[...], hist[:, columns(core, k, quarter)])

    core_send[1, :, 0:quarter] = gate_part(other, 0).astype(jnp.bfloat16)
    core_send[1, :, quarter:half_w] = gate_part(other, 1).astype(jnp.bfloat16)
    core_copy(1).start()
    plane_end(0)
    mine[1, :, 0:quarter] = gate_part(c, 0)
    mine[1, :, quarter:half_w] = gate_part(c, 1)
    piece_end(0)
    core_end(1)
    back_end(0)
    plane_end(1)
    piece_end(1)
    wide_end(0)
    back_end(1)
    wide_end(1)
    last_end(0)
    last_end(1)

    def sent(k):
        user_copy(k).wait_send()
        pool_out(k).wait_send()
        user_relay((z + k) % nz).wait_send()
        for a in range(2):
            piece_copy(a, k).wait_send()
            back_copy(a, k).wait_send()

    def sent_plane(k):
        for a in range(2):
            plane_copy(a, k).wait_send()
            wide_copy(a, k).wait_send()
            last_copy(a, k).wait_send()

    each(nz, sent)
    each(nr, sent_plane)
    user_relay(z).wait_send()
    for a in range(2):
        last_copy(a, 0).wait_send()


def exchange(imp_user, labels, px, py, items, w_out, slope, hist):
    nz = lax.axis_size("own") // CORES
    nr = lax.axis_size("rep")
    slots = px.shape[0]
    imps = imp_user.shape[0]
    half_w = D // CORES
    bf16, f32 = jnp.bfloat16, jnp.float32
    vmem = pl.BlockSpec(memory_space=pltpu.VMEM)
    hbm = pl.BlockSpec(memory_space=pl.ANY)
    dma = pltpu.SemaphoreType.DMA
    return pl.pallas_call(
        functools.partial(exchange_kernel, nz, nr),
        in_specs=[vmem] * 4 + [hbm] * 4,
        out_specs=[vmem] * 3,
        out_shape=[
            jax.ShapeDtypeStruct((1, imps), f32),
            jax.ShapeDtypeStruct((WIDTH, D), bf16),
            jax.ShapeDtypeStruct((WIDTH, D), bf16),
        ],
        scratch_shapes=[
            pltpu.VMEM(items.shape, bf16),
            pltpu.VMEM(w_out.shape, bf16),
            pltpu.VMEM(slope.shape, bf16),
            pltpu.VMEM(hist.shape, bf16),
            pltpu.VMEM((CORES * nz, slots, D + WIDTH), bf16),
            pltpu.VMEM((nz, slots, WIDTH), bf16),
            pltpu.VMEM((nz, slots, WIDTH), bf16),
            pltpu.VMEM((nz, slots, WIDTH), f32),
            pltpu.VMEM((nz, slots, WIDTH), bf16),
            pltpu.VMEM((nz, slots, WIDTH), bf16),
            pltpu.VMEM(slope.shape, bf16),
            pltpu.VMEM((2, WIDTH, half_w), f32),
            pltpu.VMEM((2, WIDTH, half_w), bf16),
            pltpu.VMEM((2, WIDTH, half_w), bf16),
            pltpu.VMEM((2, WIDTH, half_w), bf16),
            pltpu.VMEM((2, nr, WIDTH // nr, half_w), bf16),
            pltpu.VMEM((2, WIDTH // nr, half_w), bf16),
            pltpu.VMEM((2, nz, TILE, LANES), bf16),
            dma((4,)),
            dma((nz,)), dma((nz,)), dma((nz,)), dma((nz,)),
            dma((2,)),
            dma((nz,)), dma((nz,)),
            dma((2, 2)),
            dma((2, nr)), dma((2, nr)),
            dma((2, nz)), dma((2, nz)), dma((2, nz)), dma((2, nz)),
            dma((2, nr)), dma((2, nr)), dma((2, nr)), dma((2, nr)),
        ],
        compiler_params=pltpu.CompilerParams(
            collective_id=0, has_side_effects=True, vmem_limit_bytes=48 * 1024 * 1024
        ),
        name="exchange",
    )(imp_user[None], labels[None], px, py, items, w_out, slope, hist)


def body(histories, lengths, counts, imp_user, items, labels, w_uvqk, w_out):
    slots = histories.shape[0]
    capacity = slots // lax.axis_size("own")
    ranks = jnp.arange(slots, dtype=jnp.int32)
    alive = ranks % capacity < jnp.repeat(counts, capacity)
    spans = jnp.where(alive, lengths, 0)
    px, py, slope = forward(histories, spans, w_uvqk)
    logits, grad_out, grad_gate = exchange(
        imp_user, labels, px, py, items, w_out, slope, histories.reshape(-1, D)
    )
    return (logits[0], grad_out, grad_gate.T)


def solution(mesh):
    return jax.shard_map(
        body,
        mesh=mesh,
        in_specs=(
            P(("own", "rep"), None, None),
            P(("own", "rep")),
            P(("own", "rep")),
            P(("own", "rep")),
            P(("own", "rep"), None),
            P(("own", "rep")),
            P(),
            P(),
        ),
        out_specs=(P(("own", "rep")), P(), P()),
        check_vma=False,
    )
```

```python
import functools

import jax
import jax.numpy as jnp
from jax import lax
from jax.experimental import pallas as pl
from jax.experimental.pallas import tpu as pltpu
from jax.sharding import PartitionSpec as P

D = 1024
HEADS = 4
HEAD = 128
HIST = 64
WIDTH = HEADS * HEAD
BIN = 128
CHUNK = 256
CORES = 2
TILE = 16
LANES = 128
PARTS = 4
MESH = pl.DeviceIdType.MESH

EPS_NORM = 1e-06
EPS_LAYER = 1e-05


def sigmoid(v):
    return 0.5 * jnp.tanh(0.5 * v) + 0.5


def dot(a, b):
    return jnp.dot(a, b, preferred_element_type=jnp.float32)


def dot_t(a, b):
    return lax.dot_general(a, b, (((1,), (1,)), ((), ())), preferred_element_type=jnp.float32)


def forward_kernel(
    lengths, counts, h_hbm, w_hbm, user_ref, slope_ref, packed_ref, holds_ref,
    hist, w, heads_in, gate_act, gate_slope, sum_x, sum_y,
    spans, free, unit_source, unit_start, unit_span, unit_slot, load_sem,
):
    slots = user_ref.shape[0]
    bins = slots * HIST // BIN
    per_bin = BIN // TILE
    loads = [
        pltpu.make_async_copy(h_hbm, hist, load_sem.at[0]),
        pltpu.make_async_copy(w_hbm, w, load_sem.at[1]),
    ]
    for load in loads:
        load.start()
    sum_x[...] = jnp.zeros_like(sum_x)
    sum_y[...] = jnp.zeros_like(sum_y)

    def clear(u, carry):
        unit_source[u] = 0
        unit_start[u] = 0
        unit_span[u] = 0
        unit_slot[u] = 0
        return carry

    def clear_bin(b, carry):
        free[b] = per_bin
        return carry

    lax.fori_loop(0, bins * per_bin, clear, 0)
    lax.fori_loop(0, bins, clear_bin, 0)

    def size_of(s):
        return (spans[s] + TILE - 1) // TILE

    def put(s, b):
        size = size_of(s)
        used = per_bin - free[b]
        for j in range(HIST // TILE):
            @pl.when(j < size)
            def _():
                u = b * per_bin + used + j
                unit_source[u] = s * (HIST // TILE) + j
                unit_start[u] = used * TILE
                unit_span[u] = spans[s]
                unit_slot[u] = s
        free[b] = free[b] - size

    def large(s, count):
        live = s % 2 < counts[s // 2]
        spans[s] = jnp.where(live, lengths[s], 0)
        fits = size_of(s) > 2

        @pl.when(fits)
        def _():
            put(s, count // 2)
        return count + fits.astype(jnp.int32)

    used_bins = (lax.fori_loop(0, slots, large, jnp.int32(0)) + 1) // 2

    def small(size):
        def step(s, carry):
            def place(carry):
                at, top = carry
                at = lax.while_loop(lambda b: (b < bins - 1) & (free[b] < size), lambda b: b + 1, at)
                put(s, at)
                return at, jnp.maximum(top, at + 1)
            return lax.cond(size_of(s) == size, place, lambda carry: carry, carry)
        return step

    for size in (2, 1):
        used_bins = lax.fori_loop(0, slots, small(size), (jnp.int32(0), used_bins))[1]
    steps = (used_bins + 1) // 2

    for load in loads:
        load.wait()

    def block(i, carry):
        base = pl.multiple_of(i * 2 * BIN, 2 * BIN)
        for j in range(2 * per_bin):
            packed_ref[pl.ds(base + j * TILE, TILE), :] = hist[unit_source[i * 2 * per_bin + j]]
        x = packed_ref[pl.ds(base, 2 * BIN), :]
        feats = x.astype(jnp.float32)
        scale = lax.rsqrt(jnp.mean(feats * feats, -1, keepdims=True) + EPS_NORM)
        for j in range(4 * WIDTH // CHUNK):
            linear = dot(x, w[:, j * CHUNK : (j + 1) * CHUNK]) * scale
            sig = sigmoid(linear)
            act = linear * sig
            if j < WIDTH // CHUNK:
                gate_act[:, j * CHUNK : (j + 1) * CHUNK] = act
                gate_slope[:, j * CHUNK : (j + 1) * CHUNK] = sig + act * (1.0 - sig)
            else:
                heads_in[:, j * CHUNK - WIDTH : (j + 1) * CHUNK - WIDTH] = act.astype(jnp.bfloat16)
        row = lax.broadcasted_iota(jnp.int32, (BIN, BIN), 0)
        col = lax.broadcasted_iota(jnp.int32, (BIN, BIN), 1)
        spot = lax.broadcasted_iota(jnp.int32, (BIN, 1), 0)
        lane = lax.broadcasted_iota(jnp.int32, (1, BIN), 1)
        slot = lax.broadcasted_iota(jnp.int32, (slots, BIN), 0)
        for k in range(2):
            rows = slice(k * BIN, (k + 1) * BIN)
            units = [(i * 2 + k) * per_bin + j for j in range(per_bin)]

            def down(table):
                return jnp.concatenate([jnp.full((TILE, 1), table[u], jnp.int32) for u in units], 0)

            start = down(unit_start)
            span = down(unit_span)
            end = start + span
            allowed = (col >= start) & (col <= row) & (col < end)
            share = jnp.where(spot < end, 1.0 / jnp.maximum(span, 1).astype(jnp.float32), 0.0)
            back = share * scale[rows]
            name = jnp.full((1, BIN), -1, jnp.int32)
            stop = jnp.zeros((1, BIN), jnp.int32)
            for j, u in enumerate(units):
                here = lane // TILE == j
                name = jnp.where(here, unit_slot[u], name)
                stop = jnp.where(here, unit_start[u] + unit_span[u], stop)
            member = ((slot == name) & (lane < stop)).astype(jnp.bfloat16)
            place = pl.ds(pl.multiple_of(base + k * BIN, BIN), BIN)
            holds_ref[:, place] = member
            sum_x[...] += dot(member, x[rows])
            attended = []
            for h in range(HEADS):
                value, query, key = [
                    heads_in[rows, m * WIDTH + h * HEAD : m * WIDTH + (h + 1) * HEAD] for m in range(3)
                ]
                scores = dot_t(query, key) * HEAD ** (-0.5)
                attn = jnp.where(allowed, scores * sigmoid(scores), 0.0).astype(jnp.bfloat16)
                attended.append(dot(attn, value))
            center = sum(jnp.sum(a, -1, keepdims=True) for a in attended) / WIDTH
            moved = [a - center for a in attended]
            spread = sum(jnp.sum(a * a, -1, keepdims=True) for a in moved) / WIDTH
            norm = lax.rsqrt(spread + EPS_LAYER)
            for h in range(HEADS):
                cols = slice(h * HEAD, (h + 1) * HEAD)
                normal = moved[h] * norm
                mixed = normal * gate_act[rows, cols]
                high = mixed.astype(jnp.bfloat16)
                low = (mixed - high.astype(jnp.float32)).astype(jnp.bfloat16)
                sum_y[:, cols] += dot(member, high) + dot(member, low)
                slope = back * normal * gate_slope[rows, cols]
                slope_ref[cols, place] = slope.T.astype(jnp.bfloat16)
        return carry

    def blank(i, carry):
        place = pl.ds(pl.multiple_of(i * 2 * BIN, 2 * BIN), 2 * BIN)
        packed_ref[place, :] = jnp.zeros((2 * BIN, D), jnp.bfloat16)
        slope_ref[:, place] = jnp.zeros((WIDTH, 2 * BIN), jnp.bfloat16)
        holds_ref[:, place] = jnp.zeros((slots, 2 * BIN), jnp.bfloat16)
        return carry

    lax.fori_loop(0, steps, block, 0)
    lax.fori_loop(steps, bins // 2, blank, 0)
    which = lax.broadcasted_iota(jnp.int32, (slots, 1), 0)
    span = jnp.ones((slots, 1), jnp.int32)
    for s in range(slots):
        span = jnp.where(which == s, jnp.maximum(spans[s], 1), span)
    inverse = 1.0 / span.astype(jnp.float32)
    user_ref[:, 0:D] = (sum_x[...] * inverse).astype(jnp.bfloat16)
    user_ref[:, D : D + WIDTH] = (sum_y[...] * inverse).astype(jnp.bfloat16)


def forward(histories, lengths, counts, w_uvqk):
    slots = histories.shape[0]
    tokens = slots * HIST
    units = tokens // TILE
    bf16, f32 = jnp.bfloat16, jnp.float32
    vmem = pl.BlockSpec(memory_space=pltpu.VMEM)
    smem = pl.BlockSpec(memory_space=pltpu.SMEM)
    hbm = pl.BlockSpec(memory_space=pl.ANY)
    return pl.pallas_call(
        forward_kernel,
        in_specs=[smem, smem, hbm, hbm],
        out_specs=[vmem] * 4,
        out_shape=[
            jax.ShapeDtypeStruct((slots, D + WIDTH), bf16),
            jax.ShapeDtypeStruct((WIDTH, tokens), bf16),
            jax.ShapeDtypeStruct((tokens, D), bf16),
            jax.ShapeDtypeStruct((slots, tokens), bf16),
        ],
        scratch_shapes=[
            pltpu.VMEM((units, TILE, D), bf16),
            pltpu.VMEM(w_uvqk.shape, bf16),
            pltpu.VMEM((2 * BIN, 3 * WIDTH), bf16),
            pltpu.VMEM((2 * BIN, WIDTH), f32),
            pltpu.VMEM((2 * BIN, WIDTH), f32),
            pltpu.VMEM((slots, D), f32),
            pltpu.VMEM((slots, WIDTH), f32),
            pltpu.SMEM((slots,), jnp.int32),
            pltpu.SMEM((tokens // BIN,), jnp.int32),
            pltpu.SMEM((units,), jnp.int32),
            pltpu.SMEM((units,), jnp.int32),
            pltpu.SMEM((units,), jnp.int32),
            pltpu.SMEM((units,), jnp.int32),
            pltpu.SemaphoreType.DMA((2,)),
        ],
        compiler_params=pltpu.CompilerParams(vmem_limit_bytes=40 * 1024 * 1024),
        name="forward",
    )(lengths, counts, histories.reshape(units, TILE, D), w_uvqk)


def exchange_kernel(
    nz, nr, user_ref, label_ref, mine_ref, items, w_out, slope, packed, holds,
    logit_ref, out_ref, gate_ref,
    users, pool_send, pool_core, pool_mine, pool_z, pool_got,
    pre, mine, core_send, core_got, half, plane_got, row_sum, piece_got,
    user_send, user_recv, relay_send, relay_recv, pcore_sem, pz_send, pz_recv,
    core_sem, plane_send, plane_recv, piece_send, piece_recv, back_send, back_recv,
    wide_send, wide_recv, last_send, last_recv,
):
    own = lax.axis_index("own")
    rep = lax.axis_index("rep")
    z, c = own // CORES, own % CORES
    other = 1 - c
    slots = mine_ref.shape[0]
    side = nz * slots
    block = WIDTH // nr
    half_w = D // CORES
    grads = (out_ref, gate_ref)

    def z_id(k):
        return ((z + k) % nz * CORES + c, rep)

    def plane_id(k):
        return (own, (rep + k) % nr)

    sibling = (z * CORES + other, rep)

    def copy(source, target, send, recv, device):
        return pltpu.make_async_remote_copy(
            src_ref=source, dst_ref=target, send_sem=send, recv_sem=recv,
            device_id=device, device_id_type=MESH,
        )

    def each(count, step):
        def run(k, carry):
            step(k)
            return carry
        lax.fori_loop(1, count, run, 0)

    barrier = pltpu.get_barrier_semaphore()
    each(nz, lambda k: pl.semaphore_signal(barrier, inc=1, device_id=z_id(k), device_id_type=MESH))
    each(nr, lambda k: pl.semaphore_signal(barrier, inc=1, device_id=plane_id(k), device_id_type=MESH))
    pl.semaphore_signal(barrier, inc=1, device_id=sibling, device_id_type=MESH)
    pl.semaphore_wait(barrier, nz - 1 + nr - 1 + 1)

    at = c * nz + z
    users[at] = mine_ref[...]

    reach = nz // 2
    width = (D + WIDTH) // PARTS
    ends = (z_id(1), z_id(nz - 1))

    def origin(way, step):
        return (z + nz - step if way == 0 else z + step) % nz

    def hop(way, step, part):
        spot = users.at[c * nz + origin(way, step), :, part * width : (part + 1) * width]
        flag = (way * reach + step) * PARTS + part
        return copy(spot, spot, user_send.at[flag], user_recv.at[flag], ends[way])

    def landed(way, step, part):
        spot = users.at[c * nz + origin(way, step + 1), :, part * width : (part + 1) * width]
        flag = (way * reach + step) * PARTS + part
        copy(spot, spot, user_send.at[flag], user_recv.at[flag], ends[way]).wait_recv()

    def goes(way, step, part):
        return step < reach - 1 or part % 2 == way

    hops = [
        (way, step, part)
        for step in range(reach) for part in range(PARTS) for way in range(2) if goes(way, step, part)
    ]

    def user_relay(zz):
        spot = users.at[c * nz + zz]
        return copy(spot, spot, relay_send.at[zz], relay_recv.at[zz], sibling)

    def relay_wait(zz):
        spot = users.at[other * nz + zz]
        copy(spot, spot, relay_send.at[zz], relay_recv.at[zz], sibling).wait_recv()

    for part in range(PARTS):
        for way in range(2):
            hop(way, 0, part).start()
    user_relay(z).start()

    item_w = dot_t(items[...], w_out[...]).astype(jnp.bfloat16)

    for step in range(reach):
        for part in range(PARTS):
            for way in range(2):
                if goes(way, step, part):
                    landed(way, step, part)
                if step + 1 < reach and goes(way, step + 1, part):
                    hop(way, step + 1, part).start()
        user_relay(origin(0, step + 1)).start()
        if step + 1 < reach:
            user_relay(origin(1, step + 1)).start()
    relay_wait(z)
    each(nz, lambda k: relay_wait((z + k) % nz))

    index = user_ref[...]
    source = (index % slots) // 2
    place = (source % CORES) * side + (source // CORES) * slots + index // slots * 2 + index % 2
    table = dot_t(users[:, :, 0:D].reshape(2 * side, D), items[...]) + dot_t(
        users[:, :, D : D + WIDTH].reshape(2 * side, WIDTH), item_w
    )
    imps = index.shape[1]
    picked = lax.broadcasted_iota(jnp.int32, (2 * side, imps), 0) == place
    logits = jnp.sum(jnp.where(picked, table, 0.0), 0, keepdims=True)
    logit_ref[...] = logits
    error = sigmoid(logits) - label_ref[...].astype(jnp.float32)

    line = lax.broadcasted_iota(jnp.int32, (side, imps), 0)

    def pool_side(core):
        weight = jnp.where(line + core * side == place, error, 0.0).astype(jnp.bfloat16)
        return dot(weight, item_w)

    pool_send[...] = pool_side(other).astype(jnp.bfloat16).reshape(nz, slots, WIDTH)
    pool_copy = copy(pool_send, pool_core, pcore_sem.at[0], pcore_sem.at[1], sibling)
    pool_copy.start()
    pool_mine[...] = pool_side(c).reshape(nz, slots, WIDTH)

    turned = users[:, :, D : D + WIDTH].reshape(2 * side, WIDTH).astype(jnp.float32).T.astype(jnp.bfloat16)

    pool_copy.wait()
    pool_z[...] = (pool_mine[...] + pool_core[...].astype(jnp.float32)).astype(jnp.bfloat16)

    def pool_out(k):
        zz = (z + k) % nz
        return copy(pool_z.at[zz], pool_got.at[z], pz_send.at[k], pz_recv.at[z], z_id(k))

    each(nz, lambda k: pool_out(k).start())

    chosen = dot(turned, picked.astype(jnp.bfloat16))
    chosen = (chosen * error).astype(jnp.bfloat16)

    def columns(core, k=0, size=half_w):
        return pl.ds(pl.multiple_of(core * half_w + k * size, size), size)

    def core_copy(a):
        return copy(core_send.at[a], core_got.at[a], core_sem.at[a, 0], core_sem.at[a, 1], sibling)

    core_send[0] = dot(chosen, items[:, columns(other)]).astype(jnp.bfloat16)
    core_copy(0).start()
    mine[0] = dot(chosen, items[:, columns(c)])

    def plane_rows(k):
        return pl.ds(pl.multiple_of((rep + k) % nr * block, block), block)

    def plane_copy(a, k):
        return copy(
            half.at[a, plane_rows(k)], plane_got.at[a, rep], plane_send.at[a, k], plane_recv.at[a, rep], plane_id(k)
        )

    def core_end(a):
        core_copy(a).wait()
        half[a] = (mine[a] + core_got[a].astype(jnp.float32)).astype(jnp.bfloat16)
        each(nr, lambda k: plane_copy(a, k).start())

    def piece_spot(zz):
        return (
            pl.multiple_of(zz // 4 * TILE, TILE),
            pl.multiple_of(zz % 4 * LANES, LANES),
        )

    def piece_copy(a, k):
        down, across = piece_spot((z + k) % nz)
        return copy(
            row_sum.at[a, pl.ds(down, TILE), pl.ds(across, LANES)], piece_got.at[a, z],
            piece_send.at[a, k], piece_recv.at[a, z], z_id(k),
        )

    def plane_end(a):
        def add(k, total):
            rr = (rep + k) % nr
            spot = plane_got.at[a, rr]
            copy(spot, spot, plane_send.at[a, 0], plane_recv.at[a, rr], sibling).wait_recv()
            return total + spot[...].astype(jnp.float32)
        total = half[a, plane_rows(0)].astype(jnp.float32)
        row_sum[a] = lax.fori_loop(1, nr, add, total).astype(jnp.bfloat16)
        each(nz, lambda k: piece_copy(a, k).start())

    def final_spot(a, zz):
        down, across = piece_spot(zz)
        rows = pl.ds(pl.multiple_of(rep * block + down, TILE), TILE)
        return grads[a].at[rows, pl.ds(pl.multiple_of(c * half_w + across, LANES), LANES)]

    def back_copy(a, k):
        spot = final_spot(a, z)
        return copy(spot, spot, back_send.at[a, k], back_recv.at[a, z], z_id(k))

    def piece_end(a):
        down, across = piece_spot(z)
        def add(k, total):
            zz = (z + k) % nz
            spot = piece_got.at[a, zz]
            copy(spot, spot, piece_send.at[a, 0], piece_recv.at[a, zz], sibling).wait_recv()
            return total + spot[...].astype(jnp.float32)
        total = row_sum[a, pl.ds(down, TILE), pl.ds(across, LANES)].astype(jnp.float32)
        final_spot(a, z)[...] = lax.fori_loop(1, nz, add, total).astype(jnp.bfloat16)
        each(nz, lambda k: back_copy(a, k).start())

    def wide_spot(a, core, k):
        return grads[a].at[plane_rows(k), columns(core)]

    def wide_copy(a, k):
        spot = wide_spot(a, c, 0)
        return copy(spot, spot, wide_send.at[a, k], wide_recv.at[a, rep], plane_id(k))

    def last_copy(a, k):
        spot = wide_spot(a, c, k)
        rr = (rep + k) % nr
        return copy(spot, spot, last_send.at[a, rr], last_recv.at[a, rr], sibling)

    def back_end(a):
        def wait(k):
            zz = (z + k) % nz
            spot = final_spot(a, zz)
            copy(spot, spot, back_send.at[a, 0], back_recv.at[a, zz], sibling).wait_recv()
        each(nz, wait)
        each(nr, lambda k: wide_copy(a, k).start())
        last_copy(a, 0).start()

    def wide_end(a):
        def step(k):
            rr = (rep + k) % nr
            spot = wide_spot(a, c, k)
            copy(spot, spot, wide_send.at[a, 0], wide_recv.at[a, rr], sibling).wait_recv()
            last_copy(a, k).start()
        each(nr, step)

    def last_end(a):
        def step(k):
            rr = (rep + k) % nr
            spot = wide_spot(a, other, k)
            copy(spot, spot, last_send.at[a, 0], last_recv.at[a, rr], sibling).wait_recv()
        step(0)
        each(nr, step)

    core_end(0)

    def pool_add(k, total):
        zz = (z + k) % nz
        spot = pool_got.at[zz]
        copy(spot, spot, pz_send.at[0], pz_recv.at[zz], sibling).wait_recv()
        return total + spot[...].astype(jnp.float32)

    pool = lax.fori_loop(1, nz, pool_add, pool_z[z].astype(jnp.float32))
    pool_t = pool.astype(jnp.bfloat16).astype(jnp.float32).T.astype(jnp.bfloat16)
    pre[...] = (dot(pool_t, holds[...]) * slope[...].astype(jnp.float32)).astype(jnp.bfloat16)

    quarter = half_w // 2

    def gate_part(core, k):
        return dot(pre[...], packed[:, columns(core, k, quarter)])

    core_send[1, :, 0:quarter] = gate_part(other, 0).astype(jnp.bfloat16)
    core_send[1, :, quarter:half_w] = gate_part(other, 1).astype(jnp.bfloat16)
    core_copy(1).start()
    plane_end(0)
    mine[1, :, 0:quarter] = gate_part(c, 0)
    mine[1, :, quarter:half_w] = gate_part(c, 1)
    piece_end(0)
    core_end(1)
    plane_end(1)
    back_end(0)
    piece_end(1)
    wide_end(0)
    back_end(1)
    wide_end(1)
    last_end(0)
    last_end(1)

    def sent(k):
        pool_out(k).wait_send()
        user_relay((z + k) % nz).wait_send()
        for a in range(2):
            piece_copy(a, k).wait_send()
            back_copy(a, k).wait_send()

    def sent_plane(k):
        for a in range(2):
            plane_copy(a, k).wait_send()
            wide_copy(a, k).wait_send()
            last_copy(a, k).wait_send()

    each(nz, sent)
    each(nr, sent_plane)
    user_relay(z).wait_send()
    for way, step, part in hops:
        hop(way, step, part).wait_send()
    for a in range(2):
        last_copy(a, 0).wait_send()


def exchange(imp_user, labels, users, items, w_out, slope, packed, holds):
    nz = lax.axis_size("own") // CORES
    nr = lax.axis_size("rep")
    slots = users.shape[0]
    imps = imp_user.shape[0]
    half_w = D // CORES
    bf16, f32 = jnp.bfloat16, jnp.float32
    vmem = pl.BlockSpec(memory_space=pltpu.VMEM)
    dma = pltpu.SemaphoreType.DMA
    return pl.pallas_call(
        functools.partial(exchange_kernel, nz, nr),
        in_specs=[vmem] * 8,
        out_specs=[vmem] * 3,
        out_shape=[
            jax.ShapeDtypeStruct((1, imps), f32),
            jax.ShapeDtypeStruct((WIDTH, D), bf16),
            jax.ShapeDtypeStruct((WIDTH, D), bf16),
        ],
        scratch_shapes=[
            pltpu.VMEM((CORES * nz, slots, D + WIDTH), bf16),
            pltpu.VMEM((nz, slots, WIDTH), bf16),
            pltpu.VMEM((nz, slots, WIDTH), bf16),
            pltpu.VMEM((nz, slots, WIDTH), f32),
            pltpu.VMEM((nz, slots, WIDTH), bf16),
            pltpu.VMEM((nz, slots, WIDTH), bf16),
            pltpu.VMEM(slope.shape, bf16),
            pltpu.VMEM((2, WIDTH, half_w), f32),
            pltpu.VMEM((2, WIDTH, half_w), bf16),
            pltpu.VMEM((2, WIDTH, half_w), bf16),
            pltpu.VMEM((2, WIDTH, half_w), bf16),
            pltpu.VMEM((2, nr, WIDTH // nr, half_w), bf16),
            pltpu.VMEM((2, WIDTH // nr, half_w), bf16),
            pltpu.VMEM((2, nz, TILE, LANES), bf16),
            dma((nz * PARTS,)), dma((nz * PARTS,)), dma((nz,)), dma((nz,)),
            dma((2,)),
            dma((nz,)), dma((nz,)),
            dma((2, 2)),
            dma((2, nr)), dma((2, nr)),
            dma((2, nz)), dma((2, nz)), dma((2, nz)), dma((2, nz)),
            dma((2, nr)), dma((2, nr)), dma((2, nr)), dma((2, nr)),
        ],
        compiler_params=pltpu.CompilerParams(
            collective_id=0, has_side_effects=True, vmem_limit_bytes=48 * 1024 * 1024
        ),
        name="exchange",
    )(imp_user[None], labels[None], users, items, w_out, slope, packed, holds)


def body(histories, lengths, counts, imp_user, items, labels, w_uvqk, w_out):
    users, slope, packed, holds = forward(histories, lengths, counts, w_uvqk)
    logits, grad_out, grad_gate = exchange(
        imp_user, labels, users, items, w_out, slope, packed, holds
    )
    return (logits[0], grad_out, grad_gate.T)


def solution(mesh):
    return jax.shard_map(
        body,
        mesh=mesh,
        in_specs=(
            P(("own", "rep"), None, None),
            P(("own", "rep")),
            P(("own", "rep")),
            P(("own", "rep")),
            P(("own", "rep"), None),
            P(("own", "rep")),
            P(),
            P(),
        ),
        out_specs=(P(("own", "rep")), P(), P()),
        check_vma=False,
    )
```

```python
import functools

import jax
import jax.numpy as jnp
from jax import lax
from jax.experimental import pallas as pl
from jax.experimental.pallas import tpu as pltpu
from jax.sharding import PartitionSpec as P

D = 1024
HEADS = 4
HEAD = 128
HIST = 64
WIDTH = HEADS * HEAD
BIN = 128
CHUNK = 256
CORES = 2
TILE = 16
LANES = 128
PARTS = 4
MESH = pl.DeviceIdType.MESH

EPS_NORM = 1e-06
EPS_LAYER = 1e-05


def sigmoid(v):
    return 0.5 * jnp.tanh(0.5 * v) + 0.5


def dot(a, b):
    return jnp.dot(a, b, preferred_element_type=jnp.float32)


def dot_t(a, b):
    return lax.dot_general(a, b, (((1,), (1,)), ((), ())), preferred_element_type=jnp.float32)


def forward_kernel(
    lengths_hbm, counts_hbm, h_hbm, w_hbm, user_ref, slope_hbm, packed_hbm, holds_hbm,
    slope_ref, packed_ref, holds_ref, w, heads_in, gate_act, gate_slope, sum_x, sum_y,
    lengths, counts, spans, free, unit_source, unit_start, unit_stop, unit_slot, load_sem, unit_sem, out_sem,
):
    slots = user_ref.shape[0]
    bins = slots * HIST // BIN
    per_bin = BIN // TILE
    per_step = 2 * per_bin
    loads = [
        pltpu.make_async_copy(source, target, load_sem.at[k])
        for k, (source, target) in enumerate(((lengths_hbm, lengths), (counts_hbm, counts), (w_hbm, w)))
    ]
    for load in loads:
        load.start()
    sum_x[...] = jnp.zeros_like(sum_x)
    sum_y[...] = jnp.zeros_like(sum_y)

    def clear_bin(b, carry):
        free[b] = per_bin
        return carry

    lax.fori_loop(0, bins, clear_bin, 0)
    loads[0].wait()
    loads[1].wait()

    def size_of(s):
        return (spans[s] + TILE - 1) // TILE

    def put(s, b):
        size = size_of(s)
        used = per_bin - free[b]
        first = b * per_bin + used

        def fill(j, carry):
            unit_source[first + j] = s * (HIST // TILE) + j
            unit_start[first + j] = used * TILE
            unit_stop[first + j] = used * TILE + spans[s]
            unit_slot[first + j] = s
            return carry

        lax.fori_loop(0, size, fill, 0)
        free[b] = free[b] - size

    def large(s, count):
        live = s % 2 < counts[s // 2]
        spans[s] = jnp.where(live, lengths[s], 0)
        fits = size_of(s) > 2

        @pl.when(fits)
        def _():
            put(s, count // 2)
        return count + fits.astype(jnp.int32)

    used_bins = (lax.fori_loop(0, slots, large, jnp.int32(0)) + 1) // 2

    def small(size):
        def step(s, carry):
            def place(carry):
                at, top = carry
                at = lax.while_loop(lambda b: (b < bins - 1) & (free[b] < size), lambda b: b + 1, at)
                put(s, at)
                return at, jnp.maximum(top, at + 1)
            return lax.cond(size_of(s) == size, place, lambda carry: carry, carry)
        return step

    for size in (2, 1):
        used_bins = lax.fori_loop(0, slots, small(size), (jnp.int32(0), used_bins))[1]
    steps = (used_bins + 1) // 2

    def pad(b, carry):
        def fill(u, carry):
            unit_source[u] = 0
            unit_start[u] = 0
            unit_stop[u] = 0
            unit_slot[u] = 0
            return carry
        lax.fori_loop((b + 1) * per_bin - free[b], (b + 1) * per_bin, fill, 0)
        return carry

    lax.fori_loop(0, 2 * steps, pad, 0)

    def tile_copy(u):
        row = pl.ds(pl.multiple_of(u * TILE, TILE), TILE)
        return pltpu.make_async_copy(h_hbm.at[unit_source[u]], packed_ref.at[row], unit_sem.at[u])

    def fetch(u, carry):
        tile_copy(u).start()
        return carry

    lax.fori_loop(0, steps * per_step, fetch, 0)

    def packed_out(i):
        place = pl.ds(pl.multiple_of(i * 2 * BIN, 2 * BIN), 2 * BIN)
        return pltpu.make_async_copy(packed_ref.at[place], packed_hbm.at[place], out_sem.at[0, i])

    def rest_out(i):
        place = pl.ds(pl.multiple_of(i * 2 * BIN, 2 * BIN), 2 * BIN)
        return [
            pltpu.make_async_copy(slope_ref.at[:, place], slope_hbm.at[:, place], out_sem.at[1, i]),
            pltpu.make_async_copy(holds_ref.at[:, place], holds_hbm.at[:, place], out_sem.at[2, i]),
        ]

    def blank(i, carry):
        place = pl.ds(pl.multiple_of(i * 2 * BIN, 2 * BIN), 2 * BIN)
        packed_ref[place, :] = jnp.zeros((2 * BIN, D), jnp.bfloat16)
        slope_ref[:, place] = jnp.zeros((WIDTH, 2 * BIN), jnp.bfloat16)
        holds_ref[:, place] = jnp.zeros((slots, 2 * BIN), jnp.bfloat16)
        packed_out(i).start()
        for done in rest_out(i):
            done.start()
        return carry

    lax.fori_loop(steps, bins // 2, blank, 0)
    loads[2].wait()

    def block(i, carry):
        base = pl.multiple_of(i * 2 * BIN, 2 * BIN)
        for j in range(per_step):
            tile_copy(i * per_step + j).wait()
        packed_out(i).start()
        x = packed_ref[pl.ds(base, 2 * BIN), :]
        feats = x.astype(jnp.float32)
        scale = lax.rsqrt(jnp.mean(feats * feats, -1, keepdims=True) + EPS_NORM)
        half_scale = 0.5 * scale
        for j in range(4 * WIDTH // CHUNK):
            half = dot(x, w[:, j * CHUNK : (j + 1) * CHUNK]) * half_scale
            t = jnp.tanh(half)
            act = half * t + half
            if j < WIDTH // CHUNK:
                gate_act[:, j * CHUNK : (j + 1) * CHUNK] = act
                gate_slope[:, j * CHUNK : (j + 1) * CHUNK] = (1.0 + t) * (1.0 + half * (1.0 - t))
            else:
                heads_in[:, j * CHUNK - WIDTH : (j + 1) * CHUNK - WIDTH] = act.astype(jnp.bfloat16)
        row = lax.broadcasted_iota(jnp.int32, (BIN, BIN), 0)
        col = lax.broadcasted_iota(jnp.int32, (BIN, BIN), 1)
        lane = lax.broadcasted_iota(jnp.int32, (1, BIN), 1)
        slot = lax.broadcasted_iota(jnp.int32, (slots, BIN), 0)
        for k in range(2):
            rows = slice(k * BIN, (k + 1) * BIN)
            units = [(i * 2 + k) * per_bin + j for j in range(per_bin)]

            def down(values):
                return jnp.concatenate([jnp.full((TILE, BIN), v, jnp.int32) for v in values], 0)

            start = down([unit_start[u] for u in units])
            stop = down([unit_stop[u] for u in units])
            allowed = (col >= start) & (col <= row) & (col < stop)
            span = jnp.maximum(stop - start, 1).astype(jnp.float32)
            back = jnp.where(row < stop, half_scale[rows] / span, 0.0)
            name = jnp.full((1, BIN), -1, jnp.int32)
            limit = jnp.zeros((1, BIN), jnp.int32)
            for j, u in enumerate(units):
                here = lane // TILE == j
                name = jnp.where(here, unit_slot[u], name)
                limit = jnp.where(here, unit_stop[u], limit)
            member = ((slot == name) & (lane < limit)).astype(jnp.bfloat16)
            place = pl.ds(pl.multiple_of(base + k * BIN, BIN), BIN)
            holds_ref[:, place] = member
            sum_x[...] += dot(member, x[rows])
            attended = []
            for h in range(HEADS):
                value, query, key = [
                    heads_in[rows, m * WIDTH + h * HEAD : m * WIDTH + (h + 1) * HEAD] for m in range(3)
                ]
                half = dot_t(query, key) * (0.5 * HEAD ** (-0.5))
                attn = jnp.where(allowed, half * jnp.tanh(half) + half, 0.0).astype(jnp.bfloat16)
                attended.append(dot(attn, value))
            center = jnp.sum(sum(attended), -1, keepdims=True) / WIDTH
            moved = [a - center for a in attended]
            spread = jnp.sum(sum(a * a for a in moved), -1, keepdims=True) / WIDTH
            norm = lax.rsqrt(spread + EPS_LAYER)
            for h in range(HEADS):
                cols = slice(h * HEAD, (h + 1) * HEAD)
                normal = moved[h] * norm
                mixed = (normal * gate_act[rows, cols]).astype(jnp.bfloat16)
                sum_y[:, cols] += dot(member, mixed)
                slope = back * normal * gate_slope[rows, cols]
                slope_ref[cols, place] = slope.T.astype(jnp.bfloat16)
        for done in rest_out(i):
            done.start()
        return carry

    lax.fori_loop(0, steps, block, 0)
    which = lax.broadcasted_iota(jnp.int32, (slots, 1), 0)
    span = jnp.ones((slots, 1), jnp.int32)
    for s in range(slots):
        span = jnp.where(which == s, jnp.maximum(spans[s], 1), span)
    inverse = 1.0 / span.astype(jnp.float32)
    user_ref[:, 0:D] = (sum_x[...] * inverse).astype(jnp.bfloat16)
    user_ref[:, D : D + WIDTH] = (sum_y[...] * inverse).astype(jnp.bfloat16)

    def finish(i, carry):
        packed_out(i).wait()
        for done in rest_out(i):
            done.wait()
        return carry

    lax.fori_loop(0, bins // 2, finish, 0)


def forward(histories, lengths, counts, w_uvqk):
    slots = histories.shape[0]
    tokens = slots * HIST
    units = tokens // TILE
    bf16, f32 = jnp.bfloat16, jnp.float32
    vmem = pl.BlockSpec(memory_space=pltpu.VMEM)
    hbm = pl.BlockSpec(memory_space=pltpu.HBM)
    return pl.pallas_call(
        forward_kernel,
        in_specs=[hbm] * 4,
        out_specs=[vmem] + [hbm] * 3,
        out_shape=[
            jax.ShapeDtypeStruct((slots, D + WIDTH), bf16),
            jax.ShapeDtypeStruct((WIDTH, tokens), bf16),
            jax.ShapeDtypeStruct((tokens, D), bf16),
            jax.ShapeDtypeStruct((slots, tokens), bf16),
        ],
        scratch_shapes=[
            pltpu.VMEM((WIDTH, tokens), bf16),
            pltpu.VMEM((tokens, D), bf16),
            pltpu.VMEM((slots, tokens), bf16),
            pltpu.VMEM(w_uvqk.shape, bf16),
            pltpu.VMEM((2 * BIN, 3 * WIDTH), bf16),
            pltpu.VMEM((2 * BIN, WIDTH), f32),
            pltpu.VMEM((2 * BIN, WIDTH), f32),
            pltpu.VMEM((slots, D), f32),
            pltpu.VMEM((slots, WIDTH), f32),
            pltpu.SMEM(lengths.shape, jnp.int32),
            pltpu.SMEM(counts.shape, jnp.int32),
            pltpu.SMEM((slots,), jnp.int32),
            pltpu.SMEM((tokens // BIN,), jnp.int32),
            pltpu.SMEM((units,), jnp.int32),
            pltpu.SMEM((units,), jnp.int32),
            pltpu.SMEM((units,), jnp.int32),
            pltpu.SMEM((units,), jnp.int32),
            pltpu.SemaphoreType.DMA((3,)),
            pltpu.SemaphoreType.DMA((units,)),
            pltpu.SemaphoreType.DMA((3, tokens // (2 * BIN))),
        ],
        compiler_params=pltpu.CompilerParams(vmem_limit_bytes=58 * 1024 * 1024),
        name="forward",
    )(lengths, counts, histories.reshape(units, TILE, D), w_uvqk)


def exchange_kernel(
    nz, nr, *args,
):
    loaded = 8
    sources = args[:loaded]
    logit_ref, out_ref, gate_ref = args[loaded : loaded + 3]
    users = args[loaded + 3]
    user_ref, label_ref, items, w_out, slope, packed, holds = args[loaded + 4 : 2 * loaded + 3]
    exchange_steps(
        nz, nr, sources, user_ref, label_ref, items, w_out, slope, packed, holds,
        logit_ref, out_ref, gate_ref, users, *args[2 * loaded + 3 :],
    )


def exchange_steps(
    nz, nr, sources, user_ref, label_ref, items, w_out, slope, packed, holds,
    logit_ref, out_ref, gate_ref,
    users, pool_send, pool_core, pool_mine, pool_z, pool_got, *rest,
):
    per_sum = 8
    sums = [rest[n * per_sum : (n + 1) * per_sum] for n in range(3)]
    (
        load_sem, user_send, user_recv, relay_sem, pcore_send, pcore_recv, pz_send, pz_recv, sum_send, sum_recv,
    ) = rest[3 * per_sum :]
    own = lax.axis_index("own")
    rep = lax.axis_index("rep")
    z, c = own // CORES, own % CORES
    other = 1 - c
    slots = users.shape[1]
    side = nz * slots
    half_w = D // CORES
    deep = WIDTH // 2

    targets = (user_ref, label_ref, users.at[c * nz + z], items, w_out, slope, packed, holds)
    loads = [
        pltpu.make_async_copy(source, target, load_sem.at[k])
        for k, (source, target) in enumerate(zip(sources, targets))
    ]
    for k in (2, 3, 4, 0, 1, 7, 5, 6):
        loads[k].start()

    def z_id(k):
        return ((z + k) % nz * CORES + c, rep)

    def plane_id(k):
        return (own, (rep + k) % nr)

    sibling = (z * CORES + other, rep)

    def copy(source, target, send, recv, device):
        return pltpu.make_async_remote_copy(
            src_ref=source, dst_ref=target, send_sem=send, recv_sem=recv,
            device_id=device, device_id_type=MESH,
        )

    def signal(device):
        pl.semaphore_signal(barrier, inc=1, device_id=device, device_id_type=MESH)

    barrier = pltpu.get_barrier_semaphore()
    for k in range(1, nz):
        signal(z_id(k))
    for k in range(1, nr):
        signal(plane_id(k))
    signal(sibling)
    pl.semaphore_wait(barrier, nz - 1 + nr - 1 + 1)

    loads[2].wait()
    reach = nz // 2
    width = (D + WIDTH) // PARTS
    ends = (z_id(1), z_id(nz - 1))

    def origin(way, step):
        return (z + nz - step if way == 0 else z + step) % nz

    def hop(way, step, part):
        spot = users.at[c * nz + origin(way, step), :, part * width : (part + 1) * width]
        return copy(spot, spot, user_send, user_recv.at[(way * reach + step) * PARTS + part], ends[way])

    def landed(way, step, part):
        spot = users.at[c * nz + origin(way, step + 1), :, part * width : (part + 1) * width]
        copy(spot, spot, user_send, user_recv.at[(way * reach + step) * PARTS + part], ends[way]).wait_recv()

    def goes(way, step, part):
        return step < reach - 1 or part % 2 == way

    def user_relay(zz):
        spot = users.at[c * nz + zz]
        return copy(spot, spot, relay_sem.at[0], relay_sem.at[1], sibling)

    for part in range(PARTS):
        for way in range(2):
            hop(way, 0, part).start()
    user_relay(z).start()
    loads[3].wait()
    loads[4].wait()
    item_w = dot_t(items[...], w_out[...]).astype(jnp.bfloat16)
    for step in range(reach):
        for part in range(PARTS):
            for way in range(2):
                if goes(way, step, part):
                    landed(way, step, part)
                if step + 1 < reach and goes(way, step + 1, part):
                    hop(way, step + 1, part).start()
        user_relay(origin(0, step + 1)).start()
        if step + 1 < reach:
            user_relay(origin(1, step + 1)).start()
    all_relays = copy(
        users.at[pl.ds(c * nz, nz)], users.at[pl.ds(other * nz, nz)], relay_sem.at[0], relay_sem.at[1], sibling
    )
    loads[0].wait()
    loads[1].wait()
    all_relays.wait_recv()

    index = user_ref[...]
    source = (index % slots) // 2
    place = (source % CORES) * side + (source // CORES) * slots + index // slots * 2 + index % 2
    table = dot_t(users[:, :, 0:D].reshape(2 * side, D), items[...]) + dot_t(
        users[:, :, D : D + WIDTH].reshape(2 * side, WIDTH), item_w
    )
    imps = index.shape[1]
    picked = lax.broadcasted_iota(jnp.int32, (2 * side, imps), 0) == place
    logits = jnp.sum(jnp.where(picked, table, 0.0), 0, keepdims=True)
    logit_ref[...] = logits
    error = sigmoid(logits) - label_ref[...].astype(jnp.float32)

    line = lax.broadcasted_iota(jnp.int32, (side, imps), 0)

    def pool_side(core):
        weight = jnp.where(line + core * side == place, error, 0.0).astype(jnp.bfloat16)
        return [dot(weight, item_w[:, f * deep : (f + 1) * deep]).reshape(nz, slots, deep) for f in range(2)]

    def pool_copy(f):
        return copy(pool_send.at[f], pool_core.at[f], pcore_send.at[f], pcore_recv.at[f], sibling)

    for f, part in enumerate(pool_side(other)):
        pool_send[f] = part.astype(jnp.bfloat16)
        pool_copy(f).start()
    for f, part in enumerate(pool_side(c)):
        pool_mine[f] = part

    turned = users[:, :, D : D + WIDTH].reshape(2 * side, WIDTH).astype(jnp.float32).T.astype(jnp.bfloat16)

    def pool_out(f, k):
        zz = (z + k) % nz
        return copy(pool_z.at[f, zz], pool_got.at[f, z], pz_send.at[f], pz_recv.at[f], z_id(k))

    for f in range(2):
        pool_copy(f).wait()
        pool_z[f] = (pool_mine[f] + pool_core[f].astype(jnp.float32)).astype(jnp.bfloat16)
        for k in range(1, nz):
            pool_out(f, k).start()
        pool_got[f, z] = pool_z[f, z]

    chosen = dot(turned, picked.astype(jnp.bfloat16))
    chosen = (chosen * error).astype(jnp.bfloat16)

    def columns(core):
        return pl.ds(pl.multiple_of(core * half_w, half_w), half_w)

    places = ((out_ref, 0, WIDTH), (gate_ref, 0, deep), (gate_ref, deep, deep))
    CORE, PLANE, PIECE, BACK, WIDE, LAST = range(6)

    def sems(n, stage):
        return sum_send.at[n, stage], sum_recv.at[n, stage]

    def core_copy(n):
        return copy(sums[n][1], sums[n][2], *sems(n, CORE), sibling)

    def core_start(n, part):
        sums[n][1][...] = part.astype(jnp.bfloat16)
        core_copy(n).start()

    def block_of(n):
        return places[n][2] // nr

    def plane_rows(n, k):
        size = block_of(n)
        return pl.ds(pl.multiple_of((rep + k) % nr * size, size), size)

    def core_end(n):
        mine, _, core_got, half, plane_got = sums[n][:5]
        core_copy(n).wait()
        half[...] = (mine[...] + core_got[...].astype(jnp.float32)).astype(jnp.bfloat16)
        for k in range(1, nr):
            copy(half.at[plane_rows(n, k)], plane_got.at[rep], *sems(n, PLANE), plane_id(k)).start()
        plane_got[rep] = half[plane_rows(n, 0), :]

    def plane_all(n):
        size = block_of(n) * (nr - 1)
        return copy(sums[n][3].at[pl.ds(0, size)], sums[n][4].at[pl.ds(0, nr - 1)], *sems(n, PLANE), sibling)

    def piece_spot(n, zz):
        tall = block_of(n) // 2
        return pl.ds(pl.multiple_of(zz // 4 * tall, tall), tall), pl.ds(pl.multiple_of(zz % 4 * LANES, LANES), LANES)

    def plane_end(n):
        plane_got, row_sum, piece_got = sums[n][4:7]
        plane_all(n).wait_recv()
        total = plane_got[0].astype(jnp.float32)
        for k in range(1, nr):
            total += plane_got[k].astype(jnp.float32)
        row_sum[...] = total
        for k in range(1, nz):
            copy(row_sum.at[piece_spot(n, (z + k) % nz)], piece_got.at[z], *sems(n, PIECE), z_id(k)).start()
        piece_got[z] = row_sum[piece_spot(n, z)]

    def piece_all(n):
        spot = sums[n][6].at[pl.ds(0, nz - 1)]
        return copy(spot, spot, *sems(n, PIECE), sibling)

    def piece_end(n):
        piece_got, final = sums[n][6:8]
        piece_all(n).wait_recv()
        total = piece_got[0]
        for k in range(1, nz):
            total += piece_got[k]
        spot = final.at[piece_spot(n, z)]
        spot[...] = total
        for k in range(1, nz):
            copy(spot, spot, *sems(n, BACK), z_id(k)).start()

    def back_all(n):
        spot = sums[n][6].at[pl.ds(0, nz - 1)]
        return copy(spot, spot, *sems(n, BACK), sibling)

    def wide_spot(n, core, k):
        ref, first, _ = places[n]
        size = block_of(n)
        return ref.at[pl.ds(pl.multiple_of(first + (rep + k) % nr * size, size), size), columns(core)]

    def back_end(n):
        back_all(n).wait_recv()
        spot = wide_spot(n, c, 0)
        spot[...] = sums[n][7][...].astype(jnp.bfloat16)
        for k in range(1, nr):
            copy(spot, spot, *sems(n, WIDE), plane_id(k)).start()

    def wide_all(n):
        ref, first, _ = places[n]
        spot = ref.at[pl.ds(first, block_of(n) * (nr - 1)), columns(c)]
        return copy(spot, spot, *sems(n, WIDE), sibling)

    def last_copy(n, core):
        ref, first, size = places[n]
        spot = ref.at[pl.ds(first, size), columns(core)]
        return copy(spot, spot, *sems(n, LAST), sibling)

    def wide_end(n):
        wide_all(n).wait_recv()
        last_copy(n, c).start()

    core_start(0, dot(chosen, items[:, columns(other)]))
    sums[0][0][...] = dot(chosen, items[:, columns(c)])
    core_end(0)

    def pool_all(f):
        spot = pool_got.at[f, pl.ds(0, nz - 1)]
        return copy(spot, spot, pz_send.at[f], pz_recv.at[f], sibling)

    for k in (5, 6, 7):
        loads[k].wait()
    for f in range(2):
        pool_all(f).wait_recv()
        total = pool_got[f, 0].astype(jnp.float32)
        for k in range(1, nz):
            total += pool_got[f, k].astype(jnp.float32)
        pool_t = total.astype(jnp.bfloat16).astype(jnp.float32).T.astype(jnp.bfloat16)
        rows = slice(f * deep, (f + 1) * deep)
        pre = (dot(pool_t, holds[...]) * slope[rows, :].astype(jnp.float32)).astype(jnp.bfloat16)
        core_start(1 + f, dot(pre, packed[:, columns(other)]))
        sums[1 + f][0][...] = dot(pre, packed[:, columns(c)])
        if f == 0:
            plane_end(0)
        else:
            piece_end(0)
        core_end(1 + f)

    plane_end(1)
    back_end(0)
    plane_end(2)
    piece_end(1)
    piece_end(2)
    back_end(1)
    wide_end(0)
    back_end(2)
    wide_end(1)
    wide_end(2)

    spot = users.at[pl.ds(0, nz - 1)]
    copy(spot, spot, user_send, user_recv.at[0], sibling).wait_send()
    all_relays.wait_send()
    for f in range(2):
        pool_all(f).wait_send()
    for n in range(3):
        plane_all(n).wait_send()
        piece_all(n).wait_send()
        back_all(n).wait_send()
        wide_all(n).wait_send()
    for n in range(3):
        last_copy(n, other).wait()


def exchange(imp_user, labels, users, items, w_out, slope, packed, holds):
    nz = lax.axis_size("own") // CORES
    nr = lax.axis_size("rep")
    slots = users.shape[0]
    imps = imp_user.shape[0]
    half_w = D // CORES
    deep = WIDTH // 2
    bf16, f32 = jnp.bfloat16, jnp.float32
    vmem = pl.BlockSpec(memory_space=pltpu.VMEM)
    dma = pltpu.SemaphoreType.DMA
    sums = []
    for size in (WIDTH, deep, deep):
        block = size // nr
        sums += [
            pltpu.VMEM((size, half_w), f32),
            pltpu.VMEM((size, half_w), bf16),
            pltpu.VMEM((size, half_w), bf16),
            pltpu.VMEM((size, half_w), bf16),
            pltpu.VMEM((nr, block, half_w), bf16),
            pltpu.VMEM((block, half_w), f32),
            pltpu.VMEM((nz, block // 2, LANES), f32),
            pltpu.VMEM((block, half_w), f32),
        ]
    return pl.pallas_call(
        functools.partial(exchange_kernel, nz, nr),
        in_specs=[pl.BlockSpec(memory_space=pltpu.HBM)] * 8,
        out_specs=[vmem] * 3,
        out_shape=[
            jax.ShapeDtypeStruct((1, imps), f32),
            jax.ShapeDtypeStruct((WIDTH, D), bf16),
            jax.ShapeDtypeStruct((WIDTH, D), bf16),
        ],
        scratch_shapes=[
            pltpu.VMEM((CORES * nz, slots, D + WIDTH), bf16),
            pltpu.VMEM((1, imps), jnp.int32),
            pltpu.VMEM((1, imps), jnp.int32),
            *[pltpu.VMEM(entry.shape, bf16) for entry in (items, w_out, slope, packed, holds)],
            pltpu.VMEM((2, nz, slots, deep), bf16),
            pltpu.VMEM((2, nz, slots, deep), bf16),
            pltpu.VMEM((2, nz, slots, deep), f32),
            pltpu.VMEM((2, nz, slots, deep), bf16),
            pltpu.VMEM((2, nz, slots, deep), bf16),
            *sums,
            dma((8,)), dma(()), dma((nz * PARTS,)), dma((2,)),
            dma((2,)), dma((2,)), dma((2,)), dma((2,)),
            dma((3, 6)), dma((3, 6)),
        ],
        compiler_params=pltpu.CompilerParams(
            collective_id=0, has_side_effects=True, vmem_limit_bytes=58 * 1024 * 1024
        ),
        name="exchange",
    )(imp_user[None], labels[None], users, items, w_out, slope, packed, holds)


def body(histories, lengths, counts, imp_user, items, labels, w_uvqk, w_out):
    users, slope, packed, holds = forward(histories, lengths, counts, w_uvqk)
    logits, grad_out, grad_gate = exchange(
        imp_user, labels, users, items, w_out, slope, packed, holds
    )
    return (logits[0], grad_out, grad_gate.T)


def solution(mesh):
    return jax.shard_map(
        body,
        mesh=mesh,
        in_specs=(
            P(("own", "rep"), None, None),
            P(("own", "rep")),
            P(("own", "rep")),
            P(("own", "rep")),
            P(("own", "rep"), None),
            P(("own", "rep")),
            P(),
            P(),
        ),
        out_specs=(P(("own", "rep")), P(), P()),
        check_vma=False,
    )
```

```python
import functools

import jax
import jax.numpy as jnp
from jax import lax
from jax.experimental import pallas as pl
from jax.experimental.pallas import tpu as pltpu
from jax.sharding import PartitionSpec as P

D = 1024
HEADS = 4
HEAD = 128
HIST = 64
WIDTH = HEADS * HEAD
BIN = 128
STEP = 512
CORES = 2
LANES = 128
PARTS = 4
MESH = pl.DeviceIdType.MESH

EPS_NORM = 1e-06
EPS_LAYER = 1e-05


def sigmoid(v):
    return 0.5 * jnp.tanh(0.5 * v) + 0.5


def dot(a, b):
    return jnp.dot(a, b, preferred_element_type=jnp.float32)


def dot_t(a, b):
    return lax.dot_general(a, b, (((1,), (1,)), ((), ())), preferred_element_type=jnp.float32)


def forward_kernel(
    lengths_hbm, counts_hbm, h_hbm, w_hbm, both_hbm,
    x, w, user_ref, slope_ref, even, odd, sum_y, lengths, counts, load_sem, h_sem, w_sem, out_sem,
):
    slots = user_ref.shape[0]
    blocks = slots * HIST // STEP
    step_bins = STEP // BIN
    step_slots = STEP // HIST
    linear = (even, odd)

    def block_rows(i):
        return slice(i * STEP, (i + 1) * STEP)

    def part(n):
        return slice(n * WIDTH, (n + 1) * WIDTH)

    h_loads = [
        pltpu.make_async_copy(h_hbm.at[block_rows(i)], x.at[block_rows(i)], h_sem.at[i]) for i in range(blocks)
    ]
    w_loads = [pltpu.make_async_copy(w_hbm.at[:, part(n)], w.at[:, part(n)], w_sem.at[n]) for n in range(4)]
    small = [
        pltpu.make_async_copy(lengths_hbm, lengths, load_sem.at[0]),
        pltpu.make_async_copy(counts_hbm, counts, load_sem.at[1]),
    ]
    h_loads[0].start()
    for load in w_loads:
        load.start()
    for load in small + h_loads[1:]:
        load.start()

    def project(i, n):
        linear[i % 2][:, part(n)] = dot(x[block_rows(i), :], w[:, part(n)])

    def span_of(s):
        return jnp.where(s % 2 < counts[s // 2], lengths[s], 0)

    def one_bin(i, k):
        b = i * step_bins + k
        source = linear[i % 2]
        rows = slice(k * BIN, (k + 1) * BIN)
        first, second = span_of(2 * b), span_of(2 * b + 1)
        feats = x[b * BIN : (b + 1) * BIN, :].astype(jnp.float32)
        half_scale = 0.5 * lax.rsqrt(jnp.mean(feats * feats, -1, keepdims=True) + EPS_NORM)
        row = lax.broadcasted_iota(jnp.int32, (BIN, BIN), 0)
        col = lax.broadcasted_iota(jnp.int32, (BIN, BIN), 1)
        allowed = (
            (col <= row) & ((row < HIST) | (col >= HIST)) & (col < jnp.where(col < HIST, first, HIST + second))
        )
        span = jnp.where(row < HIST, first, second)
        share = jnp.where(row % HIST < span, 1.0 / jnp.maximum(span, 1).astype(jnp.float32), 0.0)
        back = share * half_scale

        def half_of(m, h):
            at = m * WIDTH + h * HEAD
            return source[rows, at : at + HEAD] * half_scale

        attended = []
        for h in range(HEADS):
            value, query, key = [
                (half * jnp.tanh(half) + half).astype(jnp.bfloat16) for half in (half_of(m, h) for m in (1, 2, 3))
            ]
            half = dot_t(query, key) * (0.5 * HEAD ** (-0.5))
            attn = jnp.where(allowed, half * jnp.tanh(half) + half, 0.0).astype(jnp.bfloat16)
            attended.append(dot(attn, value))
        center = jnp.sum(sum(attended), -1, keepdims=True) / WIDTH
        moved = [a - center for a in attended]
        spread = jnp.sum(sum(a * a for a in moved), -1, keepdims=True) / WIDTH
        norm = lax.rsqrt(spread + EPS_LAYER)
        for h in range(HEADS):
            cols = slice(h * HEAD, (h + 1) * HEAD)
            half = half_of(0, h)
            t = jnp.tanh(half)
            normal = moved[h] * norm
            mixed = share * normal * (half * t + half)
            for j in range(2):
                s = 2 * b + j
                sum_y[s : s + 1, cols] = jnp.sum(mixed[j * HIST : (j + 1) * HIST], 0, keepdims=True)
            slope = back * normal * ((1.0 + t) * (1.0 + half * (1.0 - t)))
            slope_ref[cols, b * BIN : (b + 1) * BIN] = slope.T.astype(jnp.bfloat16)

    def pool_x(i):
        slot = lax.broadcasted_iota(jnp.int32, (step_slots, STEP), 0)
        event = lax.broadcasted_iota(jnp.int32, (step_slots, STEP), 1) - slot * HIST
        which = lax.broadcasted_iota(jnp.int32, (step_slots, 1), 0)
        span = jnp.zeros((step_slots, 1), jnp.int32)
        for j in range(step_slots):
            span = jnp.where(which == j, span_of(i * step_slots + j), span)
        live = ((event >= 0) & (event < span)).astype(jnp.bfloat16)
        inverse = 1.0 / jnp.maximum(span, 1).astype(jnp.float32)
        return dot(live, x[block_rows(i), :]) * inverse

    def slope_out(i):
        cols = block_rows(i)
        return pltpu.make_async_copy(slope_ref.at[:, cols], both_hbm.at[0:WIDTH, cols], out_sem.at[i])

    h_loads[0].wait()
    for n in range(4):
        w_loads[n].wait()
        project(0, n)
    for load in small:
        load.wait()
    pooled = []
    for i in range(blocks):
        if i + 1 < blocks:
            h_loads[i + 1].wait()
        for k in range(step_bins):
            if i + 1 < blocks:
                project(i + 1, k)
            one_bin(i, k)
        pooled.append(pool_x(i))
        slope_out(i).start()
    user_ref[:, 0:D] = jnp.concatenate(pooled, 0).astype(jnp.bfloat16)
    user_ref[:, D : D + WIDTH] = sum_y[...].astype(jnp.bfloat16)
    user_out = pltpu.make_async_copy(
        user_ref, both_hbm.at[WIDTH : WIDTH + slots, 0 : D + WIDTH], out_sem.at[blocks]
    )
    user_out.start()
    for i in range(blocks):
        slope_out(i).wait()
    user_out.wait()


def forward(histories, lengths, counts, w_uvqk):
    slots = histories.shape[0]
    tokens = slots * HIST
    blocks = tokens // STEP
    bf16, f32 = jnp.bfloat16, jnp.float32
    hbm = pl.BlockSpec(memory_space=pltpu.HBM)
    dma = pltpu.SemaphoreType.DMA
    return pl.pallas_call(
        forward_kernel,
        in_specs=[hbm] * 4,
        out_specs=hbm,
        out_shape=jax.ShapeDtypeStruct((WIDTH + slots, tokens), bf16),
        scratch_shapes=[
            pltpu.VMEM((tokens, D), bf16),
            pltpu.VMEM(w_uvqk.shape, bf16),
            pltpu.VMEM((slots, D + WIDTH), bf16),
            pltpu.VMEM((WIDTH, tokens), bf16),
            pltpu.VMEM((STEP, 4 * WIDTH), f32),
            pltpu.VMEM((STEP, 4 * WIDTH), f32),
            pltpu.VMEM((slots, WIDTH), f32),
            pltpu.SMEM(lengths.shape, jnp.int32),
            pltpu.SMEM(counts.shape, jnp.int32),
            dma((2,)), dma((blocks,)), dma((4,)), dma((blocks + 1,)),
        ],
        compiler_params=pltpu.CompilerParams(vmem_limit_bytes=58 * 1024 * 1024),
        name="forward",
    )(lengths, counts, histories.reshape(tokens, D), w_uvqk)


def exchange_kernel(
    nz, nr, *args,
):
    loaded = 6
    user_src, label_src, both, items_src, w_src, hist_src = args[:loaded]
    deep, wide = WIDTH, D + WIDTH
    slots = both.shape[0] - deep
    sources = (user_src, label_src, both.at[deep : deep + slots, 0:wide], items_src, w_src, both.at[0:deep], hist_src)
    logit_ref, out_ref, gate_ref = args[loaded : loaded + 3]
    users = args[loaded + 3]
    user_ref, label_ref, items, w_out, slope, hist = args[loaded + 4 : loaded + 10]
    exchange_steps(
        nz, nr, sources, user_ref, label_ref, items, w_out, slope, hist,
        logit_ref, out_ref, gate_ref, users, *args[loaded + 10 :],
    )


def exchange_steps(
    nz, nr, sources, user_ref, label_ref, items, w_out, slope, hist,
    logit_ref, out_ref, gate_ref,
    users, pool_send, pool_core, pool_mine, pool_z, pool_got, pre, *rest,
):
    per_sum = 8
    sums = [rest[n * per_sum : (n + 1) * per_sum] for n in range(3)]
    (
        load_sem, user_send, user_recv, relay_sem, pool_sem, sum_send, sum_recv,
    ) = rest[3 * per_sum :]
    own = lax.axis_index("own")
    rep = lax.axis_index("rep")
    z, c = own // CORES, own % CORES
    other = 1 - c
    slots = users.shape[1]
    side = nz * slots
    half_w = D // CORES
    part_w = half_w // 2

    targets = (user_ref, label_ref, users.at[c * nz + z], items, w_out, slope, hist)
    loads = [
        pltpu.make_async_copy(source, target, load_sem.at[k])
        for k, (source, target) in enumerate(zip(sources, targets))
    ]
    for k in (2, 3, 4, 0, 1, 5, 6):
        loads[k].start()

    def z_id(k):
        return ((z + k) % nz * CORES + c, rep)

    def plane_id(k):
        return (own, (rep + k) % nr)

    sibling = (z * CORES + other, rep)

    def copy(source, target, send, recv, device):
        return pltpu.make_async_remote_copy(
            src_ref=source, dst_ref=target, send_sem=send, recv_sem=recv,
            device_id=device, device_id_type=MESH,
        )

    def signal(device):
        pl.semaphore_signal(barrier, inc=1, device_id=device, device_id_type=MESH)

    barrier = pltpu.get_barrier_semaphore()
    for k in range(1, nz):
        signal(z_id(k))
    for k in range(1, nr):
        signal(plane_id(k))
    signal(sibling)
    pl.semaphore_wait(barrier, nz - 1 + nr - 1 + 1)

    loads[2].wait()
    reach = nz // 2
    width = (D + WIDTH) // PARTS
    ends = (z_id(1), z_id(nz - 1))

    def origin(way, step):
        return (z + nz - step if way == 0 else z + step) % nz

    def hop(way, step, part):
        spot = users.at[c * nz + origin(way, step), :, part * width : (part + 1) * width]
        return copy(spot, spot, user_send, user_recv.at[(way * reach + step) * PARTS + part], ends[way])

    def landed(way, step, part):
        spot = users.at[c * nz + origin(way, step + 1), :, part * width : (part + 1) * width]
        copy(spot, spot, user_send, user_recv.at[(way * reach + step) * PARTS + part], ends[way]).wait_recv()

    def goes(way, step, part):
        return step < reach - 1 or part % 2 == way

    def user_relay(zz):
        spot = users.at[c * nz + zz]
        return copy(spot, spot, relay_sem.at[0], relay_sem.at[1], sibling)

    for part in range(PARTS):
        for way in range(2):
            hop(way, 0, part).start()
    user_relay(z).start()
    loads[3].wait()
    loads[4].wait()
    item_w = dot_t(items[...], w_out[...]).astype(jnp.bfloat16)
    for step in range(reach):
        for part in range(PARTS):
            for way in range(2):
                if goes(way, step, part):
                    landed(way, step, part)
                if step + 1 < reach and goes(way, step + 1, part):
                    hop(way, step + 1, part).start()
        user_relay(origin(0, step + 1)).start()
        if step + 1 < reach:
            user_relay(origin(1, step + 1)).start()
    all_relays = copy(
        users.at[pl.ds(c * nz, nz)], users.at[pl.ds(other * nz, nz)], relay_sem.at[0], relay_sem.at[1], sibling
    )
    loads[0].wait()
    loads[1].wait()
    all_relays.wait_recv()

    index = user_ref[...]
    source = (index % slots) // 2
    place = (source % CORES) * side + (source // CORES) * slots + index // slots * 2 + index % 2
    table = dot_t(users[:, :, 0:D].reshape(2 * side, D), items[...]) + dot_t(
        users[:, :, D : D + WIDTH].reshape(2 * side, WIDTH), item_w
    )
    imps = index.shape[1]
    picked = lax.broadcasted_iota(jnp.int32, (2 * side, imps), 0) == place
    logits = jnp.sum(jnp.where(picked, table, 0.0), 0, keepdims=True)
    logit_ref[...] = logits
    error = sigmoid(logits) - label_ref[...].astype(jnp.float32)

    line = lax.broadcasted_iota(jnp.int32, (side, imps), 0)

    def pool_side(core):
        weight = jnp.where(line + core * side == place, error, 0.0).astype(jnp.bfloat16)
        return dot(weight, item_w).reshape(nz, slots, WIDTH)

    pool_send[...] = pool_side(other).astype(jnp.bfloat16)
    pool_copy = copy(pool_send, pool_core, pool_sem.at[0], pool_sem.at[1], sibling)
    pool_copy.start()
    pool_mine[...] = pool_side(c)
    turned = users[:, :, D : D + WIDTH].reshape(2 * side, WIDTH).astype(jnp.float32).T.astype(jnp.bfloat16)
    pool_copy.wait()
    pool_z[...] = (pool_mine[...] + pool_core[...].astype(jnp.float32)).astype(jnp.bfloat16)
    for k in range(1, nz):
        copy(pool_z.at[(z + k) % nz], pool_got.at[z], pool_sem.at[2], pool_sem.at[3], z_id(k)).start()
    pool_got[z] = pool_z[z]

    chosen = dot(turned, picked.astype(jnp.bfloat16))
    chosen = (chosen * error).astype(jnp.bfloat16)

    def columns(core, first=0, size=half_w):
        step = min(size, part_w)
        return pl.ds(pl.multiple_of(core * half_w + first, step), size)

    places = ((out_ref, 0, half_w), (gate_ref, 0, part_w), (gate_ref, part_w, part_w))
    block = WIDTH // nr
    CORE, PLANE, PIECE, BACK, WIDE, LAST = range(6)

    def sems(n, stage):
        return sum_send.at[n, stage], sum_recv.at[n, stage]

    def core_copy(n):
        return copy(sums[n][1], sums[n][2], *sems(n, CORE), sibling)

    def core_start(n, part):
        sums[n][1][...] = part.astype(jnp.bfloat16)
        core_copy(n).start()

    def plane_rows(k):
        return pl.ds(pl.multiple_of((rep + k) % nr * block, block), block)

    def core_end(n):
        mine, _, core_got, half, plane_got = sums[n][:5]
        core_copy(n).wait()
        half[...] = (mine[...] + core_got[...].astype(jnp.float32)).astype(jnp.bfloat16)
        for k in range(1, nr):
            copy(half.at[plane_rows(k)], plane_got.at[rep], *sems(n, PLANE), plane_id(k)).start()
        plane_got[rep] = half[plane_rows(0), :]

    def plane_all(n):
        return copy(sums[n][3].at[pl.ds(0, block * (nr - 1))], sums[n][4].at[pl.ds(0, nr - 1)], *sems(n, PLANE), sibling)

    def piece_spot(n, zz):
        across = places[n][2] // LANES
        tall = block * across // nz
        return (
            pl.ds(pl.multiple_of(zz // across * tall, tall), tall),
            pl.ds(pl.multiple_of(zz % across * LANES, LANES), LANES),
        )

    def plane_end(n):
        plane_got, row_sum, piece_got = sums[n][4:7]
        plane_all(n).wait_recv()
        total = plane_got[0].astype(jnp.float32)
        for k in range(1, nr):
            total += plane_got[k].astype(jnp.float32)
        row_sum[...] = total
        for k in range(1, nz):
            copy(row_sum.at[piece_spot(n, (z + k) % nz)], piece_got.at[z], *sems(n, PIECE), z_id(k)).start()
        piece_got[z] = row_sum[piece_spot(n, z)]

    def piece_all(n):
        spot = sums[n][6].at[pl.ds(0, nz - 1)]
        return copy(spot, spot, *sems(n, PIECE), sibling)

    def piece_end(n):
        piece_got, final = sums[n][6:8]
        piece_all(n).wait_recv()
        total = piece_got[0]
        for k in range(1, nz):
            total += piece_got[k]
        spot = final.at[piece_spot(n, z)]
        spot[...] = total
        for k in range(1, nz):
            copy(spot, spot, *sems(n, BACK), z_id(k)).start()

    def back_all(n):
        spot = sums[n][6].at[pl.ds(0, nz - 1)]
        return copy(spot, spot, *sems(n, BACK), sibling)

    def wide_spot(n, core, k):
        ref, first, size = places[n]
        return ref.at[plane_rows(k), columns(core, first, size)]

    def back_end(n):
        back_all(n).wait_recv()
        spot = wide_spot(n, c, 0)
        spot[...] = sums[n][7][...].astype(jnp.bfloat16)
        for k in range(1, nr):
            copy(spot, spot, *sems(n, WIDE), plane_id(k)).start()

    def wide_all(n):
        ref, first, size = places[n]
        spot = ref.at[pl.ds(0, block * (nr - 1)), columns(c, first, size)]
        return copy(spot, spot, *sems(n, WIDE), sibling)

    def last_copy(n, core):
        ref, first, size = places[n]
        spot = ref.at[:, columns(core, first, size)]
        return copy(spot, spot, *sems(n, LAST), sibling)

    def wide_end(n):
        wide_all(n).wait_recv()
        last_copy(n, c).start()

    core_start(0, dot(chosen, items[:, columns(other)]))
    sums[0][0][...] = dot(chosen, items[:, columns(c)])
    core_end(0)

    pool_spot = pool_got.at[pl.ds(0, nz - 1)]
    pool_all = copy(pool_spot, pool_spot, pool_sem.at[2], pool_sem.at[3], sibling)
    loads[5].wait()
    loads[6].wait()
    pool_all.wait_recv()
    total = pool_got[0].astype(jnp.float32)
    for k in range(1, nz):
        total += pool_got[k].astype(jnp.float32)
    pool_t = total.astype(jnp.bfloat16).astype(jnp.float32).T.astype(jnp.bfloat16)
    tokens = slots * HIST
    slot = lax.broadcasted_iota(jnp.int32, (slots, tokens), 0)
    event = lax.broadcasted_iota(jnp.int32, (slots, tokens), 1)
    holds = (event // HIST == slot).astype(jnp.bfloat16)
    pre[...] = (dot(pool_t, holds) * slope[...].astype(jnp.float32)).astype(jnp.bfloat16)
    gate_part = dot(pre[...], hist[:, columns(other)])
    core_start(1, gate_part[:, 0:part_w])
    core_start(2, gate_part[:, part_w:half_w])
    plane_end(0)
    gate_part = dot(pre[...], hist[:, columns(c)])
    sums[1][0][...] = gate_part[:, 0:part_w]
    core_end(1)
    sums[2][0][...] = gate_part[:, part_w:half_w]
    core_end(2)
    piece_end(0)
    plane_end(1)
    back_end(0)
    plane_end(2)
    piece_end(1)
    piece_end(2)
    back_end(1)
    wide_end(0)
    back_end(2)
    wide_end(1)
    wide_end(2)

    spot = users.at[pl.ds(0, nz - 1)]
    copy(spot, spot, user_send, user_recv.at[0], sibling).wait_send()
    all_relays.wait_send()
    pool_all.wait_send()
    for n in range(3):
        plane_all(n).wait_send()
        piece_all(n).wait_send()
        back_all(n).wait_send()
        wide_all(n).wait_send()
    for n in range(3):
        last_copy(n, other).wait()


def exchange(imp_user, labels, both, items, w_out, hist):
    nz = lax.axis_size("own") // CORES
    nr = lax.axis_size("rep")
    slots = both.shape[0] - WIDTH
    tokens = both.shape[1]
    imps = imp_user.shape[0]
    half_w = D // CORES
    bf16, f32 = jnp.bfloat16, jnp.float32
    vmem = pl.BlockSpec(memory_space=pltpu.VMEM)
    dma = pltpu.SemaphoreType.DMA
    sums = []
    for size in (half_w, half_w // 2, half_w // 2):
        block = WIDTH // nr
        sums += [
            pltpu.VMEM((WIDTH, size), f32),
            pltpu.VMEM((WIDTH, size), bf16),
            pltpu.VMEM((WIDTH, size), bf16),
            pltpu.VMEM((WIDTH, size), bf16),
            pltpu.VMEM((nr, block, size), bf16),
            pltpu.VMEM((block, size), f32),
            pltpu.VMEM((nz, block * size // nz // LANES, LANES), f32),
            pltpu.VMEM((block, size), f32),
        ]
    return pl.pallas_call(
        functools.partial(exchange_kernel, nz, nr),
        in_specs=[pl.BlockSpec(memory_space=pltpu.HBM)] * 6,
        out_specs=[vmem] * 3,
        out_shape=[
            jax.ShapeDtypeStruct((1, imps), f32),
            jax.ShapeDtypeStruct((WIDTH, D), bf16),
            jax.ShapeDtypeStruct((WIDTH, D), bf16),
        ],
        scratch_shapes=[
            pltpu.VMEM((CORES * nz, slots, D + WIDTH), bf16),
            pltpu.VMEM((1, imps), jnp.int32),
            pltpu.VMEM((1, imps), jnp.int32),
            *[pltpu.VMEM(shape, bf16) for shape in (items.shape, w_out.shape, (WIDTH, tokens), hist.shape)],
            pltpu.VMEM((nz, slots, WIDTH), bf16),
            pltpu.VMEM((nz, slots, WIDTH), bf16),
            pltpu.VMEM((nz, slots, WIDTH), f32),
            pltpu.VMEM((nz, slots, WIDTH), bf16),
            pltpu.VMEM((nz, slots, WIDTH), bf16),
            pltpu.VMEM((WIDTH, tokens), bf16),
            *sums,
            dma((7,)), dma(()), dma((nz * PARTS,)), dma((2,)),
            dma((4,)),
            dma((3, 6)), dma((3, 6)),
        ],
        compiler_params=pltpu.CompilerParams(
            collective_id=0, has_side_effects=True, vmem_limit_bytes=50 * 1024 * 1024
        ),
        name="exchange",
    )(imp_user[None], labels[None], both, items, w_out, hist)


def body(histories, lengths, counts, imp_user, items, labels, w_uvqk, w_out):
    both = forward(histories, lengths, counts, w_uvqk)
    logits, grad_out, grad_gate = exchange(
        imp_user, labels, both, items, w_out, histories.reshape(-1, D)
    )
    return (logits[0], grad_out, grad_gate.T)


def solution(mesh):
    return jax.shard_map(
        body,
        mesh=mesh,
        in_specs=(
            P(("own", "rep"), None, None),
            P(("own", "rep")),
            P(("own", "rep")),
            P(("own", "rep")),
            P(("own", "rep"), None),
            P(("own", "rep")),
            P(),
            P(),
        ),
        out_specs=(P(("own", "rep")), P(), P()),
        check_vma=False,
    )
```

```python
import functools

import jax
import jax.numpy as jnp
from jax import lax
from jax.experimental import pallas as pl
from jax.experimental.pallas import tpu as pltpu
from jax.sharding import PartitionSpec as P

D = 1024
HEADS = 4
HEAD = 128
HIST = 64
WIDTH = HEADS * HEAD
BIN = 128
STEP = 512
CORES = 2
LANES = 128
PARTS = 4
MESH = pl.DeviceIdType.MESH

EPS_NORM = 1e-06
EPS_LAYER = 1e-05


def sigmoid(v):
    return 0.5 * jnp.tanh(0.5 * v) + 0.5


def dot(a, b):
    return jnp.dot(a, b, preferred_element_type=jnp.float32)


def dot_t(a, b):
    return lax.dot_general(a, b, (((1,), (1,)), ((), ())), preferred_element_type=jnp.float32)


def step_kernel(
    nz, nr, imp_hbm, label_hbm, lengths_hbm, counts_hbm, items_hbm, w_out_hbm, w_hbm, h_hbm,
    logit_hbm, out_hbm, gate_hbm,
    user_ref, label_ref, items, w_out, w, x, slope, even, odd, sum_y, logit_ref, out_ref, gate_ref,
    users, pool_send, pool_core, pool_mine, pool_z, pool_got, pre, *rest,
):
    per_sum = 8
    sums = [rest[n * per_sum : (n + 1) * per_sum] for n in range(3)]
    (
        lengths, counts, load_sem, h_sem, w_sem, out_sem,
        user_send, user_recv, relay_sem, pool_sem, sum_send, sum_recv,
    ) = rest[3 * per_sum :]
    own = lax.axis_index("own")
    rep = lax.axis_index("rep")
    z, c = own // CORES, own % CORES
    other = 1 - c
    slots = users.shape[1]
    side = nz * slots
    half_w = D // CORES
    part_w = half_w // 2
    blocks = slots * HIST // STEP
    step_bins = STEP // BIN
    step_slots = STEP // HIST
    linear = (even, odd)

    def block_rows(i):
        return slice(i * STEP, (i + 1) * STEP)

    def part(n):
        return slice(n * WIDTH, (n + 1) * WIDTH)

    h_loads = [
        pltpu.make_async_copy(h_hbm.at[block_rows(i)], x.at[block_rows(i)], h_sem.at[i]) for i in range(blocks)
    ]
    w_loads = [pltpu.make_async_copy(w_hbm.at[:, part(n)], w.at[:, part(n)], w_sem.at[n]) for n in range(4)]
    loads = [
        pltpu.make_async_copy(source, target, load_sem.at[k])
        for k, (source, target) in enumerate(
            (
                (lengths_hbm, lengths), (counts_hbm, counts), (w_out_hbm, w_out), (items_hbm, items),
                (imp_hbm, user_ref), (label_hbm, label_ref),
            )
        )
    ]
    h_loads[0].start()
    for load in w_loads:
        load.start()
    for load in loads[:2] + h_loads[1:] + loads[2:]:
        load.start()

    def z_id(k):
        return ((z + k) % nz * CORES + c, rep)

    def plane_id(k):
        return (own, (rep + k) % nr)

    sibling = (z * CORES + other, rep)

    def copy(source, target, send, recv, device):
        return pltpu.make_async_remote_copy(
            src_ref=source, dst_ref=target, send_sem=send, recv_sem=recv,
            device_id=device, device_id_type=MESH,
        )

    def signal(device):
        pl.semaphore_signal(barrier, inc=1, device_id=device, device_id_type=MESH)

    barrier = pltpu.get_barrier_semaphore()
    for k in range(1, nz):
        signal(z_id(k))
    for k in range(1, nr):
        signal(plane_id(k))
    signal(sibling)

    at = c * nz + z
    reach = nz // 2
    some = slots // 2
    ends = (z_id(1), z_id(nz - 1))

    def origin(way, step):
        return (z + nz - step if way == 0 else z + step) % nz

    def piece_of(block, piece):
        rows = pl.ds(piece % 2 * some, some)
        return users.at[block, rows, 0:D] if piece < 2 else users.at[block, rows, D : D + WIDTH]

    def hop(way, step, piece):
        spot = piece_of(c * nz + origin(way, step), piece)
        return copy(spot, spot, user_send, user_recv.at[(way * reach + step) * PARTS + piece], ends[way])

    def landed(way, step, piece):
        spot = piece_of(c * nz + origin(way, step + 1), piece)
        copy(spot, spot, user_send, user_recv.at[(way * reach + step) * PARTS + piece], ends[way]).wait_recv()

    def goes(way, step, piece):
        return step < reach - 1 or piece % 2 == way

    def forward_hop(step, piece):
        for way in range(2):
            if goes(way, step, piece):
                landed(way, step, piece)
            if step + 1 < reach and goes(way, step + 1, piece):
                hop(way, step + 1, piece).start()

    def user_relay(zz):
        spot = users.at[c * nz + zz, :, 0:D]
        return copy(spot, spot, relay_sem.at[0], relay_sem.at[1], sibling)

    def project(i, n):
        linear[i % 2][:, part(n)] = dot(x[block_rows(i), :], w[:, part(n)])

    def span_of(s):
        return jnp.where(s % 2 < counts[s // 2], lengths[s], 0)

    def one_bin(i, k):
        b = i * step_bins + k
        source = linear[i % 2]
        rows = slice(k * BIN, (k + 1) * BIN)
        first, second = span_of(2 * b), span_of(2 * b + 1)
        feats = x[b * BIN : (b + 1) * BIN, :].astype(jnp.float32)
        half_scale = 0.5 * lax.rsqrt(jnp.mean(feats * feats, -1, keepdims=True) + EPS_NORM)
        row = lax.broadcasted_iota(jnp.int32, (BIN, BIN), 0)
        col = lax.broadcasted_iota(jnp.int32, (BIN, BIN), 1)
        allowed = (
            (col <= row) & ((row < HIST) | (col >= HIST)) & (col < jnp.where(col < HIST, first, HIST + second))
        )
        span = jnp.where(row < HIST, first, second)
        share = jnp.where(row % HIST < span, 1.0 / jnp.maximum(span, 1).astype(jnp.float32), 0.0)
        back = share * half_scale

        def half_of(m, h):
            at = m * WIDTH + h * HEAD
            return source[rows, at : at + HEAD] * half_scale

        attended = []
        for h in range(HEADS):
            value, query, key = [
                (half * jnp.tanh(half) + half).astype(jnp.bfloat16) for half in (half_of(m, h) for m in (1, 2, 3))
            ]
            half = dot_t(query, key) * (0.5 * HEAD ** (-0.5))
            attn = jnp.where(allowed, half * jnp.tanh(half) + half, 0.0).astype(jnp.bfloat16)
            attended.append(dot(attn, value))
        center = jnp.sum(sum(attended), -1, keepdims=True) / WIDTH
        moved = [a - center for a in attended]
        spread = jnp.sum(sum(a * a for a in moved), -1, keepdims=True) / WIDTH
        norm = lax.rsqrt(spread + EPS_LAYER)
        for h in range(HEADS):
            cols = slice(h * HEAD, (h + 1) * HEAD)
            half = half_of(0, h)
            t = jnp.tanh(half)
            normal = moved[h] * norm
            mixed = share * normal * (half * t + half)
            for j in range(2):
                s = 2 * b + j
                sum_y[s : s + 1, cols] = jnp.sum(mixed[j * HIST : (j + 1) * HIST], 0, keepdims=True)
            falls = back * normal * ((1.0 + t) * (1.0 + half * (1.0 - t)))
            slope[cols, b * BIN : (b + 1) * BIN] = falls.T.astype(jnp.bfloat16)

    def pool_x(i):
        slot = lax.broadcasted_iota(jnp.int32, (step_slots, STEP), 0)
        event = lax.broadcasted_iota(jnp.int32, (step_slots, STEP), 1) - slot * HIST
        which = lax.broadcasted_iota(jnp.int32, (step_slots, 1), 0)
        span = jnp.zeros((step_slots, 1), jnp.int32)
        for j in range(step_slots):
            span = jnp.where(which == j, span_of(i * step_slots + j), span)
        live = ((event >= 0) & (event < span)).astype(jnp.bfloat16)
        inverse = 1.0 / jnp.maximum(span, 1).astype(jnp.float32)
        return dot(live, x[block_rows(i), :]) * inverse

    def embed(g):
        rows = slice(g * some, (g + 1) * some)
        py = sum_y[rows, :].astype(jnp.bfloat16)
        users[at, rows, D : D + WIDTH] = py
        px = jnp.concatenate(pooled[g * blocks // 2 : (g + 1) * blocks // 2], 0)
        users[at, rows, 0:D] = (px + dot(py, w_out[...])).astype(jnp.bfloat16)
        for piece in (g, g + 2):
            for way in range(2):
                hop(way, 0, piece).start()

    h_loads[0].wait()
    for n in range(4):
        w_loads[n].wait()
        project(0, n)
    for load in loads[:3]:
        load.wait()
    pooled = []
    for i in range(blocks):
        if i + 1 < blocks:
            h_loads[i + 1].wait()
        for k in range(step_bins):
            if i + 1 < blocks:
                project(i + 1, k)
            one_bin(i, k)
            if i == blocks - 1 and k == step_bins // 2 - 1:
                for piece in (0, 2):
                    forward_hop(1, piece)
        pooled.append(pool_x(i))
        if i == blocks // 2 - 1:
            pl.semaphore_wait(barrier, nz - 1 + nr - 1 + 1)
            embed(0)
        elif i == blocks - 2:
            for piece in (0, 2):
                forward_hop(0, piece)
    embed(1)
    user_relay(z).start()
    for piece in (0, 2):
        forward_hop(2, piece)
    for load in loads[3:]:
        load.wait()
    item_w = dot_t(items[...], w_out[...]).astype(jnp.bfloat16)
    for step in range(reach):
        forward_hop(step, 1)
        if step == reach - 1:
            forward_hop(step, 0)
        user_relay(origin(0, step + 1)).start()
        if step + 1 < reach:
            user_relay(origin(1, step + 1)).start()
    forward_hop(reach - 1, 2)
    forward_hop(0, 3)

    def line_of(core, first, size):
        return users.at[pl.ds(core * nz, nz), :, first : first + size]

    all_relays = copy(line_of(c, 0, D), line_of(other, 0, D), relay_sem.at[0], relay_sem.at[1], sibling)
    all_relays.wait_recv()
    forward_hop(1, 3)

    index = user_ref[...]
    source = (index % slots) // 2
    place = (source % CORES) * side + (source // CORES) * slots + index // slots * 2 + index % 2
    table = dot_t(users[:, :, 0:D].reshape(2 * side, D), items[...])
    imps = index.shape[1]
    picked = lax.broadcasted_iota(jnp.int32, (2 * side, imps), 0) == place
    logits = jnp.sum(jnp.where(picked, table, 0.0), 0, keepdims=True)
    logit_ref[...] = logits
    logit_out = pltpu.make_async_copy(logit_ref, logit_hbm, out_sem.at[0])
    logit_out.start()
    forward_hop(2, 3)
    error = sigmoid(logits) - label_ref[...].astype(jnp.float32)

    line = lax.broadcasted_iota(jnp.int32, (side, imps), 0)

    def pool_side(core):
        weight = jnp.where(line + core * side == place, error, 0.0).astype(jnp.bfloat16)
        return dot(weight, item_w).reshape(nz, slots, WIDTH)

    pool_send[...] = pool_side(other).astype(jnp.bfloat16)
    pool_copy = copy(pool_send, pool_core, pool_sem.at[0], pool_sem.at[1], sibling)
    pool_copy.start()
    pool_mine[...] = pool_side(c)
    forward_hop(reach - 1, 3)
    py_relay = copy(
        line_of(c, D, WIDTH), line_of(c, D, WIDTH), relay_sem.at[2], relay_sem.at[3], sibling
    )
    py_relay.start()
    pool_copy.wait()
    pool_z[...] = (pool_mine[...] + pool_core[...].astype(jnp.float32)).astype(jnp.bfloat16)
    for k in range(1, nz):
        copy(pool_z.at[(z + k) % nz], pool_got.at[z], pool_sem.at[2], pool_sem.at[3], z_id(k)).start()
    pool_got[z] = pool_z[z]

    copy(line_of(c, D, WIDTH), line_of(other, D, WIDTH), relay_sem.at[2], relay_sem.at[3], sibling).wait_recv()
    turned = users[:, :, D : D + WIDTH].reshape(2 * side, WIDTH).astype(jnp.float32).T.astype(jnp.bfloat16)
    chosen = dot(turned, picked.astype(jnp.bfloat16))
    chosen = (chosen * error).astype(jnp.bfloat16)

    def columns(core, first=0, size=half_w):
        step = min(size, part_w)
        return pl.ds(pl.multiple_of(core * half_w + first, step), size)

    places = ((out_ref, 0, half_w), (gate_ref, 0, part_w), (gate_ref, part_w, part_w))
    block = WIDTH // nr
    CORE, PLANE, PIECE, BACK, WIDE, LAST = range(6)

    def sems(n, stage):
        return sum_send.at[n, stage], sum_recv.at[n, stage]

    def core_copy(n):
        return copy(sums[n][1], sums[n][2], *sems(n, CORE), sibling)

    def core_start(n, part):
        sums[n][1][...] = part.astype(jnp.bfloat16)
        core_copy(n).start()

    def plane_rows(k):
        return pl.ds(pl.multiple_of((rep + k) % nr * block, block), block)

    def core_end(n):
        mine, _, core_got, half, plane_got = sums[n][:5]
        core_copy(n).wait()
        half[...] = (mine[...] + core_got[...].astype(jnp.float32)).astype(jnp.bfloat16)
        for k in range(1, nr):
            copy(half.at[plane_rows(k)], plane_got.at[rep], *sems(n, PLANE), plane_id(k)).start()
        plane_got[rep] = half[plane_rows(0), :]

    def plane_all(n):
        return copy(sums[n][3].at[pl.ds(0, block * (nr - 1))], sums[n][4].at[pl.ds(0, nr - 1)], *sems(n, PLANE), sibling)

    def piece_spot(n, zz):
        across = places[n][2] // LANES
        tall = block * across // nz
        return (
            pl.ds(pl.multiple_of(zz // across * tall, tall), tall),
            pl.ds(pl.multiple_of(zz % across * LANES, LANES), LANES),
        )

    def plane_end(n):
        plane_got, row_sum, piece_got = sums[n][4:7]
        plane_all(n).wait_recv()
        total = plane_got[0].astype(jnp.float32)
        for k in range(1, nr):
            total += plane_got[k].astype(jnp.float32)
        row_sum[...] = total
        for k in range(1, nz):
            copy(row_sum.at[piece_spot(n, (z + k) % nz)], piece_got.at[z], *sems(n, PIECE), z_id(k)).start()
        piece_got[z] = row_sum[piece_spot(n, z)]

    def piece_all(n):
        spot = sums[n][6].at[pl.ds(0, nz - 1)]
        return copy(spot, spot, *sems(n, PIECE), sibling)

    def piece_end(n):
        piece_got, final = sums[n][6:8]
        piece_all(n).wait_recv()
        total = piece_got[0]
        for k in range(1, nz):
            total += piece_got[k]
        spot = final.at[piece_spot(n, z)]
        spot[...] = total
        for k in range(1, nz):
            copy(spot, spot, *sems(n, BACK), z_id(k)).start()

    def back_all(n):
        spot = sums[n][6].at[pl.ds(0, nz - 1)]
        return copy(spot, spot, *sems(n, BACK), sibling)

    def wide_spot(n, core, k):
        ref, first, size = places[n]
        return ref.at[plane_rows(k), columns(core, first, size)]

    def back_end(n):
        back_all(n).wait_recv()
        spot = wide_spot(n, c, 0)
        spot[...] = sums[n][7][...].astype(jnp.bfloat16)
        for k in range(1, nr):
            copy(spot, spot, *sems(n, WIDE), plane_id(k)).start()

    def wide_all(n):
        ref, first, size = places[n]
        spot = ref.at[pl.ds(0, block * (nr - 1)), columns(c, first, size)]
        return copy(spot, spot, *sems(n, WIDE), sibling)

    def last_copy(n, core):
        ref, first, size = places[n]
        spot = ref.at[:, columns(core, first, size)]
        return copy(spot, spot, *sems(n, LAST), sibling)

    def wide_end(n):
        wide_all(n).wait_recv()
        last_copy(n, c).start()

    core_start(0, dot(chosen, items[:, columns(other)]))
    sums[0][0][...] = dot(chosen, items[:, columns(c)])
    core_end(0)

    pool_spot = pool_got.at[pl.ds(0, nz - 1)]
    pool_all = copy(pool_spot, pool_spot, pool_sem.at[2], pool_sem.at[3], sibling)
    pool_all.wait_recv()
    total = pool_got[0].astype(jnp.float32)
    for k in range(1, nz):
        total += pool_got[k].astype(jnp.float32)
    pool_t = total.astype(jnp.bfloat16).astype(jnp.float32).T.astype(jnp.bfloat16)
    tokens = slots * HIST
    slot = lax.broadcasted_iota(jnp.int32, (slots, tokens), 0)
    event = lax.broadcasted_iota(jnp.int32, (slots, tokens), 1)
    holds = (event // HIST == slot).astype(jnp.bfloat16)
    pre[...] = (dot(pool_t, holds) * slope[...].astype(jnp.float32)).astype(jnp.bfloat16)
    gate_part = dot(pre[...], x[:, columns(other)])
    core_start(1, gate_part[:, 0:part_w])
    core_start(2, gate_part[:, part_w:half_w])
    plane_end(0)
    gate_part = dot(pre[...], x[:, columns(c)])
    sums[1][0][...] = gate_part[:, 0:part_w]
    core_end(1)
    sums[2][0][...] = gate_part[:, part_w:half_w]
    core_end(2)
    piece_end(0)
    plane_end(1)
    back_end(0)
    plane_end(2)
    piece_end(1)
    piece_end(2)
    back_end(1)
    wide_end(0)
    back_end(2)
    wide_end(1)
    wide_end(2)

    def strips(n):
        ref, first, size = places[n]
        target = gate_hbm if n else out_hbm
        return [
            pltpu.make_async_copy(
                ref.at[:, core * half_w + first : core * half_w + first + size],
                target.at[:, core * half_w + first : core * half_w + first + size],
                out_sem.at[1 + n * CORES + core],
            )
            for core in range(CORES)
        ]

    for n in range(3):
        last_copy(n, other).wait()
        for strip in strips(n):
            strip.start()
    spot = users.at[pl.ds(0, nz - 1)]
    copy(spot, spot, user_send, user_recv.at[0], sibling).wait_send()
    all_relays.wait_send()
    py_relay.wait_send()
    pool_all.wait_send()
    for n in range(3):
        plane_all(n).wait_send()
        piece_all(n).wait_send()
        back_all(n).wait_send()
        wide_all(n).wait_send()
    logit_out.wait()
    for n in range(3):
        for strip in strips(n):
            strip.wait()


def train_step(histories, lengths, counts, imp_user, items, labels, w_uvqk, w_out):
    nz = lax.axis_size("own") // CORES
    nr = lax.axis_size("rep")
    slots = histories.shape[0]
    tokens = slots * HIST
    blocks = tokens // STEP
    imps = imp_user.shape[0]
    half_w = D // CORES
    bf16, f32 = jnp.bfloat16, jnp.float32
    hbm = pl.BlockSpec(memory_space=pltpu.HBM)
    dma = pltpu.SemaphoreType.DMA
    sums = []
    for size in (half_w, half_w // 2, half_w // 2):
        block = WIDTH // nr
        sums += [
            pltpu.VMEM((WIDTH, size), f32),
            pltpu.VMEM((WIDTH, size), bf16),
            pltpu.VMEM((WIDTH, size), bf16),
            pltpu.VMEM((WIDTH, size), bf16),
            pltpu.VMEM((nr, block, size), bf16),
            pltpu.VMEM((block, size), f32),
            pltpu.VMEM((nz, block * size // nz // LANES, LANES), f32),
            pltpu.VMEM((block, size), f32),
        ]
    return pl.pallas_call(
        functools.partial(step_kernel, nz, nr),
        in_specs=[hbm] * 8,
        out_specs=[hbm] * 3,
        out_shape=[
            jax.ShapeDtypeStruct((1, imps), f32),
            jax.ShapeDtypeStruct((WIDTH, D), bf16),
            jax.ShapeDtypeStruct((WIDTH, D), bf16),
        ],
        scratch_shapes=[
            pltpu.VMEM((1, imps), jnp.int32),
            pltpu.VMEM((1, imps), jnp.int32),
            pltpu.VMEM(items.shape, bf16),
            pltpu.VMEM(w_out.shape, bf16),
            pltpu.VMEM(w_uvqk.shape, bf16),
            pltpu.VMEM((tokens, D), bf16),
            pltpu.VMEM((WIDTH, tokens), bf16),
            pltpu.VMEM((STEP, 4 * WIDTH), f32),
            pltpu.VMEM((STEP, 4 * WIDTH), f32),
            pltpu.VMEM((slots, WIDTH), f32),
            pltpu.VMEM((1, imps), f32),
            pltpu.VMEM((WIDTH, D), bf16),
            pltpu.VMEM((WIDTH, D), bf16),
            pltpu.VMEM((CORES * nz, slots, D + WIDTH), bf16),
            pltpu.VMEM((nz, slots, WIDTH), bf16),
            pltpu.VMEM((nz, slots, WIDTH), bf16),
            pltpu.VMEM((nz, slots, WIDTH), f32),
            pltpu.VMEM((nz, slots, WIDTH), bf16),
            pltpu.VMEM((nz, slots, WIDTH), bf16),
            pltpu.VMEM((WIDTH, tokens), bf16),
            *sums,
            pltpu.SMEM(lengths.shape, jnp.int32),
            pltpu.SMEM(counts.shape, jnp.int32),
            dma((6,)), dma((blocks,)), dma((4,)), dma((1 + 3 * CORES,)),
            dma(()), dma((nz * PARTS,)), dma((4,)), dma((4,)),
            dma((3, 6)), dma((3, 6)),
        ],
        compiler_params=pltpu.CompilerParams(
            collective_id=0, has_side_effects=True, vmem_limit_bytes=58 * 1024 * 1024
        ),
        name="train_step",
    )(
        imp_user[None], labels[None], lengths, counts, items, w_out, w_uvqk, histories.reshape(tokens, D)
    )


def finish_kernel(logit_in, out_in, gate_in, logit_out, out_out, gate_out, turned, rows, flat, logit, sem):
    pieces = gate_in.shape[0] // LANES

    def moves(source, between, target, k):
        return (
            pltpu.make_async_copy(source, between, sem.at[0, k]),
            pltpu.make_async_copy(between, target, sem.at[1, k]),
        )

    def part(k):
        return pl.ds(k * LANES, LANES)

    gate_in_moves = [
        pltpu.make_async_copy(gate_in.at[part(k)], rows.at[part(k)], sem.at[0, k]) for k in range(pieces)
    ]
    out_moves = [
        moves(out_in.at[part(k)], flat.at[part(k)], out_out.at[part(k)], pieces + k) for k in range(pieces)
    ]
    logit_moves = moves(logit_in, logit, logit_out, 2 * pieces)
    for load in gate_in_moves:
        load.start()
    for load, _ in out_moves:
        load.start()
    logit_moves[0].start()
    for k in range(pieces):
        gate_in_moves[k].wait()
        turned[:, k * LANES : (k + 1) * LANES] = rows[part(k), :].astype(jnp.float32).T.astype(jnp.bfloat16)
        out_moves[k][0].wait()
        out_moves[k][1].start()
    last = pltpu.make_async_copy(turned, gate_out, sem.at[1, 0])
    last.start()
    logit_moves[0].wait()
    logit_moves[1].start()
    for _, store in out_moves:
        store.wait()
    logit_moves[1].wait()
    last.wait()


def finish(logits, grad_out, gate_t):
    hbm = pl.BlockSpec(memory_space=pltpu.HBM)
    across, deep = gate_t.shape
    return pl.pallas_call(
        finish_kernel,
        in_specs=[hbm] * 3,
        out_specs=[hbm] * 3,
        out_shape=[
            jax.ShapeDtypeStruct(logits.shape, logits.dtype),
            jax.ShapeDtypeStruct(grad_out.shape, grad_out.dtype),
            jax.ShapeDtypeStruct((deep, across), gate_t.dtype),
        ],
        scratch_shapes=[
            pltpu.VMEM((deep, across), gate_t.dtype),
            pltpu.VMEM((across, deep), gate_t.dtype),
            pltpu.VMEM(grad_out.shape, grad_out.dtype),
            pltpu.VMEM(logits.shape, logits.dtype),
            pltpu.SemaphoreType.DMA((2, 1 + 2 * across // LANES)),
        ],
        compiler_params=pltpu.CompilerParams(vmem_limit_bytes=58 * 1024 * 1024),
        name="finish",
    )(logits, grad_out, gate_t)


def body(histories, lengths, counts, imp_user, items, labels, w_uvqk, w_out):
    logits, grad_out, grad_gate = finish(
        *train_step(histories, lengths, counts, imp_user, items, labels, w_uvqk, w_out)
    )
    return (logits[0], grad_out, grad_gate)


def solution(mesh):
    return jax.shard_map(
        body,
        mesh=mesh,
        in_specs=(
            P(("own", "rep"), None, None),
            P(("own", "rep")),
            P(("own", "rep")),
            P(("own", "rep")),
            P(("own", "rep"), None),
            P(("own", "rep")),
            P(),
            P(),
        ),
        out_specs=(P(("own", "rep")), P(), P()),
        check_vma=False,
    )
```

```python
import functools

import jax
import jax.numpy as jnp
from jax import lax
from jax.experimental import pallas as pl
from jax.experimental.pallas import tpu as pltpu
from jax.sharding import PartitionSpec as P

D = 1024
HEADS = 4
HEAD = 128
HIST = 64
WIDTH = HEADS * HEAD
BIN = 128
STEP = 512
CORES = 2
LANES = 128
PARTS = 4
MESH = pl.DeviceIdType.MESH

EPS_NORM = 1e-06
EPS_LAYER = 1e-05


def sigmoid(v):
    return 0.5 * jnp.tanh(0.5 * v) + 0.5


def dot(a, b):
    return jnp.dot(a, b, preferred_element_type=jnp.float32)


def dot_t(a, b):
    return lax.dot_general(a, b, (((1,), (1,)), ((), ())), preferred_element_type=jnp.float32)


def forward_kernel(
    lengths_hbm, counts_hbm, h_hbm, w_hbm, both_hbm,
    x, w, user_ref, slope_ref, upper, lower, sum_x, sum_y, tile_y, lengths, counts, load_sem, h_sem, w_sem, out_sem,
):
    slots = user_ref.shape[0]
    blocks = slots * HIST // STEP
    half_rows = STEP // 2
    half_bins = half_rows // BIN
    step_bins = STEP // BIN
    step_slots = STEP // HIST
    linear = (upper, lower)

    def block_rows(i):
        return pl.ds(pl.multiple_of(i * STEP, STEP), STEP)

    def part(n):
        return slice(n * WIDTH, (n + 1) * WIDTH)

    def h_load(i):
        return pltpu.make_async_copy(h_hbm.at[block_rows(i)], x.at[block_rows(i)], h_sem.at[i])

    w_loads = [pltpu.make_async_copy(w_hbm.at[:, part(n)], w.at[:, part(n)], w_sem.at[n]) for n in range(4)]
    small = [
        pltpu.make_async_copy(lengths_hbm, lengths, load_sem.at[0]),
        pltpu.make_async_copy(counts_hbm, counts, load_sem.at[1]),
    ]
    h_load(0).start()
    for load in w_loads + small:
        load.start()
    for i in range(1, blocks):
        h_load(i).start()

    def project(i, half, n):
        rows = pl.ds(pl.multiple_of(i * STEP + half * half_rows, half_rows), half_rows)
        linear[half][:, part(n)] = dot(x[rows, :], w[:, part(n)])

    def span_of(s):
        return jnp.where(s % 2 < counts[s // 2], lengths[s], 0)

    def one_bin(i, k):
        b = i * step_bins + k
        source = linear[k // half_bins]
        rows = slice(k % half_bins * BIN, (k % half_bins + 1) * BIN)
        place = pl.ds(pl.multiple_of(b * BIN, BIN), BIN)
        first, second = span_of(2 * b), span_of(2 * b + 1)
        feats = x[place, :].astype(jnp.float32)
        half_scale = 0.5 * lax.rsqrt(jnp.mean(feats * feats, -1, keepdims=True) + EPS_NORM)
        row = lax.broadcasted_iota(jnp.int32, (BIN, BIN), 0)
        col = lax.broadcasted_iota(jnp.int32, (BIN, BIN), 1)
        allowed = (
            (col <= row) & ((row < HIST) | (col >= HIST)) & (col < jnp.where(col < HIST, first, HIST + second))
        )
        span = jnp.where(row < HIST, first, second)
        share = jnp.where(row % HIST < span, 1.0 / jnp.maximum(span, 1).astype(jnp.float32), 0.0)
        back = share * half_scale

        def half_of(m, h):
            at = m * WIDTH + h * HEAD
            return source[rows, at : at + HEAD] * half_scale

        attended = []
        for h in range(HEADS):
            value, query, key = [
                (half * jnp.tanh(half) + half).astype(jnp.bfloat16) for half in (half_of(m, h) for m in (1, 2, 3))
            ]
            half = dot_t(query, key) * (0.5 * HEAD ** (-0.5))
            attn = jnp.where(allowed, half * jnp.tanh(half) + half, 0.0).astype(jnp.bfloat16)
            attended.append(dot(attn, value))
        center = jnp.sum(sum(attended), -1, keepdims=True) / WIDTH
        moved = [a - center for a in attended]
        spread = jnp.sum(sum(a * a for a in moved), -1, keepdims=True) / WIDTH
        norm = lax.rsqrt(spread + EPS_LAYER)
        for h in range(HEADS):
            cols = slice(h * HEAD, (h + 1) * HEAD)
            half = half_of(0, h)
            t = jnp.tanh(half)
            normal = moved[h] * norm
            mixed = share * normal * (half * t + half)
            for j in range(2):
                s = 2 * k + j
                tile_y[s : s + 1, cols] = jnp.sum(mixed[j * HIST : (j + 1) * HIST], 0, keepdims=True)
            slope = back * normal * ((1.0 + t) * (1.0 + half * (1.0 - t)))
            slope_ref[cols, place] = slope.T.astype(jnp.bfloat16)

    def pool_x(i):
        slot = lax.broadcasted_iota(jnp.int32, (step_slots, STEP), 0)
        event = lax.broadcasted_iota(jnp.int32, (step_slots, STEP), 1) - slot * HIST
        which = lax.broadcasted_iota(jnp.int32, (step_slots, 1), 0)
        span = jnp.zeros((step_slots, 1), jnp.int32)
        for j in range(step_slots):
            span = jnp.where(which == j, span_of(i * step_slots + j), span)
        live = ((event >= 0) & (event < span)).astype(jnp.bfloat16)
        inverse = 1.0 / jnp.maximum(span, 1).astype(jnp.float32)
        return dot(live, x[block_rows(i), :]) * inverse

    def slope_out(i):
        cols = block_rows(i)
        return pltpu.make_async_copy(slope_ref.at[:, cols], both_hbm.at[0:WIDTH, cols], out_sem.at[i])

    h_load(0).wait()
    for n in range(4):
        w_loads[n].wait()
        project(0, 0, n)
    for load in small:
        load.wait()

    def block(i, carry):
        for n in range(4):
            project(i, 1, n)
            if n % 2 == 1:
                one_bin(i, n // 2)
        later = jnp.minimum(i + 1, blocks - 1)

        @pl.when(i + 1 < blocks)
        def _():
            h_load(later).wait()

        for n in range(4):
            project(later, 0, n)
            if n % 2 == 1:
                one_bin(i, half_bins + n // 2)
        group = pl.ds(pl.multiple_of(i * step_slots, step_slots), step_slots)
        sum_x[group, :] = pool_x(i)
        sum_y[group, :] = tile_y[...]
        slope_out(i).start()
        return carry

    lax.fori_loop(0, blocks, block, 0)
    user_ref[:, 0:D] = sum_x[...].astype(jnp.bfloat16)
    user_ref[:, D : D + WIDTH] = sum_y[...].astype(jnp.bfloat16)
    user_out = pltpu.make_async_copy(
        user_ref, both_hbm.at[WIDTH : WIDTH + slots, 0 : D + WIDTH], out_sem.at[blocks]
    )
    user_out.start()
    for i in range(blocks):
        slope_out(i).wait()
    user_out.wait()


def forward(histories, lengths, counts, w_uvqk):
    slots = histories.shape[0]
    tokens = slots * HIST
    blocks = tokens // STEP
    bf16, f32 = jnp.bfloat16, jnp.float32
    hbm = pl.BlockSpec(memory_space=pltpu.HBM)
    dma = pltpu.SemaphoreType.DMA
    return pl.pallas_call(
        forward_kernel,
        in_specs=[hbm] * 4,
        out_specs=hbm,
        out_shape=jax.ShapeDtypeStruct((WIDTH + slots, tokens), bf16),
        scratch_shapes=[
            pltpu.VMEM((tokens, D), bf16),
            pltpu.VMEM(w_uvqk.shape, bf16),
            pltpu.VMEM((slots, D + WIDTH), bf16),
            pltpu.VMEM((WIDTH, tokens), bf16),
            pltpu.VMEM((STEP // 2, 4 * WIDTH), f32),
            pltpu.VMEM((STEP // 2, 4 * WIDTH), f32),
            pltpu.VMEM((slots, D), f32),
            pltpu.VMEM((slots, WIDTH), f32),
            pltpu.VMEM((STEP // HIST, WIDTH), f32),
            pltpu.SMEM(lengths.shape, jnp.int32),
            pltpu.SMEM(counts.shape, jnp.int32),
            dma((2,)), dma((blocks,)), dma((4,)), dma((blocks + 1,)),
        ],
        compiler_params=pltpu.CompilerParams(vmem_limit_bytes=58 * 1024 * 1024),
        name="forward",
    )(lengths, counts, histories.reshape(tokens, D), w_uvqk)


def exchange_kernel(
    nz, nr, *args,
):
    loaded = 6
    user_src, label_src, both, items_src, w_src, hist_src = args[:loaded]
    deep, wide = WIDTH, D + WIDTH
    slots = both.shape[0] - deep
    sources = (user_src, label_src, both.at[deep : deep + slots, 0:wide], items_src, w_src, both.at[0:deep], hist_src)
    logit_ref, out_ref, gate_ref = args[loaded : loaded + 3]
    users = args[loaded + 3]
    user_ref, label_ref, items, w_out, slope, hist = args[loaded + 4 : loaded + 10]
    exchange_steps(
        nz, nr, sources, user_ref, label_ref, items, w_out, slope, hist,
        logit_ref, out_ref, gate_ref, users, *args[loaded + 10 :],
    )


def exchange_steps(
    nz, nr, sources, user_ref, label_ref, items, w_out, slope, hist,
    logit_ref, out_ref, gate_ref,
    users, pool_send, pool_core, pool_mine, pool_z, pool_got, pre, *rest,
):
    per_sum = 8
    sums = [rest[n * per_sum : (n + 1) * per_sum] for n in range(3)]
    (
        load_sem, user_send, user_recv, relay_sem, pool_sem, sum_send, sum_recv,
    ) = rest[3 * per_sum :]
    own = lax.axis_index("own")
    rep = lax.axis_index("rep")
    z, c = own // CORES, own % CORES
    other = 1 - c
    slots = users.shape[1]
    side = nz * slots
    half_w = D // CORES
    part_w = half_w // 2

    targets = (user_ref, label_ref, users.at[c * nz + z], items, w_out, slope, hist)
    loads = [
        pltpu.make_async_copy(source, target, load_sem.at[k])
        for k, (source, target) in enumerate(zip(sources, targets))
    ]
    for k in (2, 3, 4, 0, 1, 5, 6):
        loads[k].start()

    def z_id(k):
        return ((z + k) % nz * CORES + c, rep)

    def plane_id(k):
        return (own, (rep + k) % nr)

    sibling = (z * CORES + other, rep)

    def copy(source, target, send, recv, device):
        return pltpu.make_async_remote_copy(
            src_ref=source, dst_ref=target, send_sem=send, recv_sem=recv,
            device_id=device, device_id_type=MESH,
        )

    def each(count, step):
        def run(k, carry):
            step(k)
            return carry
        lax.fori_loop(1, count, run, 0)

    def signal(device):
        pl.semaphore_signal(barrier, inc=1, device_id=device, device_id_type=MESH)

    barrier = pltpu.get_barrier_semaphore()
    each(nz, lambda k: signal(z_id(k)))
    each(nr, lambda k: signal(plane_id(k)))
    signal(sibling)
    pl.semaphore_wait(barrier, nz - 1 + nr - 1 + 1)

    loads[2].wait()
    reach = nz // 2
    width = (D + WIDTH) // PARTS
    ends = (z_id(1), z_id(nz - 1))

    def origin(way, step):
        return (z + nz - step if way == 0 else z + step) % nz

    def hop(way, step, part):
        spot = users.at[c * nz + origin(way, step), :, part * width : (part + 1) * width]
        return copy(spot, spot, user_send, user_recv.at[(way * reach + step) * PARTS + part], ends[way])

    def landed(way, step, part):
        spot = users.at[c * nz + origin(way, step + 1), :, part * width : (part + 1) * width]
        copy(spot, spot, user_send, user_recv.at[(way * reach + step) * PARTS + part], ends[way]).wait_recv()

    def goes(way, step, part):
        return step < reach - 1 or part % 2 == way

    def user_relay(zz):
        spot = users.at[c * nz + zz]
        return copy(spot, spot, relay_sem.at[0], relay_sem.at[1], sibling)

    for part in range(PARTS):
        for way in range(2):
            hop(way, 0, part).start()
    user_relay(z).start()
    loads[3].wait()
    loads[4].wait()
    item_w = dot_t(items[...], w_out[...]).astype(jnp.bfloat16)
    for step in range(reach):
        for part in range(PARTS):
            for way in range(2):
                if goes(way, step, part):
                    landed(way, step, part)
                if step + 1 < reach and goes(way, step + 1, part):
                    hop(way, step + 1, part).start()
        user_relay(origin(0, step + 1)).start()
        if step + 1 < reach:
            user_relay(origin(1, step + 1)).start()
    all_relays = copy(
        users.at[pl.ds(c * nz, nz)], users.at[pl.ds(other * nz, nz)], relay_sem.at[0], relay_sem.at[1], sibling
    )
    loads[0].wait()
    loads[1].wait()
    all_relays.wait_recv()

    index = user_ref[...]
    source = (index % slots) // 2
    place = (source % CORES) * side + (source // CORES) * slots + index // slots * 2 + index % 2
    table = dot_t(users[:, :, 0:D].reshape(2 * side, D), items[...]) + dot_t(
        users[:, :, D : D + WIDTH].reshape(2 * side, WIDTH), item_w
    )
    imps = index.shape[1]
    picked = lax.broadcasted_iota(jnp.int32, (2 * side, imps), 0) == place
    logits = jnp.sum(jnp.where(picked, table, 0.0), 0, keepdims=True)
    logit_ref[...] = logits
    error = sigmoid(logits) - label_ref[...].astype(jnp.float32)

    line = lax.broadcasted_iota(jnp.int32, (side, imps), 0)

    def pool_side(core):
        weight = jnp.where(line + core * side == place, error, 0.0).astype(jnp.bfloat16)
        return dot(weight, item_w).reshape(nz, slots, WIDTH)

    pool_send[...] = pool_side(other).astype(jnp.bfloat16)
    pool_copy = copy(pool_send, pool_core, pool_sem.at[0], pool_sem.at[1], sibling)
    pool_copy.start()
    pool_mine[...] = pool_side(c)
    turned = users[:, :, D : D + WIDTH].reshape(2 * side, WIDTH).astype(jnp.float32).T.astype(jnp.bfloat16)
    pool_copy.wait()
    pool_z[...] = (pool_mine[...] + pool_core[...].astype(jnp.float32)).astype(jnp.bfloat16)
    each(nz, lambda k: copy(pool_z.at[(z + k) % nz], pool_got.at[z], pool_sem.at[2], pool_sem.at[3], z_id(k)).start())
    pool_got[z] = pool_z[z]

    chosen = dot(turned, picked.astype(jnp.bfloat16))
    chosen = (chosen * error).astype(jnp.bfloat16)

    def columns(core, first=0, size=half_w):
        step = min(size, part_w)
        return pl.ds(pl.multiple_of(core * half_w + first, step), size)

    places = ((out_ref, 0, half_w), (gate_ref, 0, part_w), (gate_ref, part_w, part_w))
    block = WIDTH // nr
    CORE, PLANE, PIECE, BACK, WIDE, LAST = range(6)

    def sems(n, stage):
        return sum_send.at[n, stage], sum_recv.at[n, stage]

    def core_copy(n):
        return copy(sums[n][1], sums[n][2], *sems(n, CORE), sibling)

    def core_start(n, part):
        sums[n][1][...] = part.astype(jnp.bfloat16)
        core_copy(n).start()

    def plane_rows(k):
        return pl.ds(pl.multiple_of((rep + k) % nr * block, block), block)

    def core_end(n):
        mine, _, core_got, half, plane_got = sums[n][:5]
        core_copy(n).wait()
        half[...] = (mine[...] + core_got[...].astype(jnp.float32)).astype(jnp.bfloat16)
        each(nr, lambda k: copy(half.at[plane_rows(k)], plane_got.at[rep], *sems(n, PLANE), plane_id(k)).start())
        plane_got[rep] = half[plane_rows(0), :]

    def plane_all(n):
        return copy(sums[n][3].at[pl.ds(0, block * (nr - 1))], sums[n][4].at[pl.ds(0, nr - 1)], *sems(n, PLANE), sibling)

    def piece_spot(n, zz):
        across = places[n][2] // LANES
        tall = block * across // nz
        return (
            pl.ds(pl.multiple_of(zz // across * tall, tall), tall),
            pl.ds(pl.multiple_of(zz % across * LANES, LANES), LANES),
        )

    def plane_end(n):
        plane_got, row_sum, piece_got = sums[n][4:7]
        plane_all(n).wait_recv()
        total = plane_got[0].astype(jnp.float32)
        for k in range(1, nr):
            total += plane_got[k].astype(jnp.float32)
        row_sum[...] = total
        each(nz, lambda k: copy(row_sum.at[piece_spot(n, (z + k) % nz)], piece_got.at[z], *sems(n, PIECE), z_id(k)).start())
        piece_got[z] = row_sum[piece_spot(n, z)]

    def piece_all(n):
        spot = sums[n][6].at[pl.ds(0, nz - 1)]
        return copy(spot, spot, *sems(n, PIECE), sibling)

    def piece_end(n):
        piece_got, final = sums[n][6:8]
        piece_all(n).wait_recv()
        total = piece_got[0]
        for k in range(1, nz):
            total += piece_got[k]
        spot = final.at[piece_spot(n, z)]
        spot[...] = total
        each(nz, lambda k: copy(spot, spot, *sems(n, BACK), z_id(k)).start())

    def back_all(n):
        spot = sums[n][6].at[pl.ds(0, nz - 1)]
        return copy(spot, spot, *sems(n, BACK), sibling)

    def wide_spot(n, core, k):
        ref, first, size = places[n]
        return ref.at[plane_rows(k), columns(core, first, size)]

    def back_end(n):
        back_all(n).wait_recv()
        spot = wide_spot(n, c, 0)
        spot[...] = sums[n][7][...].astype(jnp.bfloat16)
        each(nr, lambda k: copy(spot, spot, *sems(n, WIDE), plane_id(k)).start())

    def wide_all(n):
        ref, first, size = places[n]
        spot = ref.at[pl.ds(0, block * (nr - 1)), columns(c, first, size)]
        return copy(spot, spot, *sems(n, WIDE), sibling)

    def last_copy(n, core):
        ref, first, size = places[n]
        spot = ref.at[:, columns(core, first, size)]
        return copy(spot, spot, *sems(n, LAST), sibling)

    def wide_end(n):
        wide_all(n).wait_recv()
        last_copy(n, c).start()

    core_start(0, dot(chosen, items[:, columns(other)]))
    sums[0][0][...] = dot(chosen, items[:, columns(c)])
    core_end(0)

    pool_spot = pool_got.at[pl.ds(0, nz - 1)]
    pool_all = copy(pool_spot, pool_spot, pool_sem.at[2], pool_sem.at[3], sibling)
    loads[5].wait()
    loads[6].wait()
    pool_all.wait_recv()
    total = pool_got[0].astype(jnp.float32)
    for k in range(1, nz):
        total += pool_got[k].astype(jnp.float32)
    pool_t = total.astype(jnp.bfloat16).astype(jnp.float32).T.astype(jnp.bfloat16)
    tokens = slots * HIST
    slot = lax.broadcasted_iota(jnp.int32, (slots, tokens), 0)
    event = lax.broadcasted_iota(jnp.int32, (slots, tokens), 1)
    holds = (event // HIST == slot).astype(jnp.bfloat16)
    pre[...] = (dot(pool_t, holds) * slope[...].astype(jnp.float32)).astype(jnp.bfloat16)
    gate_part = dot(pre[...], hist[:, columns(other)])
    core_start(1, gate_part[:, 0:part_w])
    core_start(2, gate_part[:, part_w:half_w])
    plane_end(0)
    sums[1][0][...] = dot(pre[...], hist[:, columns(c, 0, part_w)])
    core_end(1)
    sums[2][0][...] = dot(pre[...], hist[:, columns(c, part_w, part_w)])
    core_end(2)
    piece_end(0)
    plane_end(1)
    back_end(0)
    plane_end(2)
    piece_end(1)
    piece_end(2)
    back_end(1)
    wide_end(0)
    back_end(2)
    wide_end(1)
    wide_end(2)

    spot = users.at[pl.ds(0, nz - 1)]
    copy(spot, spot, user_send, user_recv.at[0], sibling).wait_send()
    all_relays.wait_send()
    pool_all.wait_send()
    for n in range(3):
        plane_all(n).wait_send()
        piece_all(n).wait_send()
        back_all(n).wait_send()
        wide_all(n).wait_send()
    for n in range(3):
        last_copy(n, other).wait()


def exchange(imp_user, labels, both, items, w_out, hist):
    nz = lax.axis_size("own") // CORES
    nr = lax.axis_size("rep")
    slots = both.shape[0] - WIDTH
    tokens = both.shape[1]
    imps = imp_user.shape[0]
    half_w = D // CORES
    bf16, f32 = jnp.bfloat16, jnp.float32
    vmem = pl.BlockSpec(memory_space=pltpu.VMEM)
    dma = pltpu.SemaphoreType.DMA
    sums = []
    for size in (half_w, half_w // 2, half_w // 2):
        block = WIDTH // nr
        sums += [
            pltpu.VMEM((WIDTH, size), f32),
            pltpu.VMEM((WIDTH, size), bf16),
            pltpu.VMEM((WIDTH, size), bf16),
            pltpu.VMEM((WIDTH, size), bf16),
            pltpu.VMEM((nr, block, size), bf16),
            pltpu.VMEM((block, size), f32),
            pltpu.VMEM((nz, block * size // nz // LANES, LANES), f32),
            pltpu.VMEM((block, size), f32),
        ]
    return pl.pallas_call(
        functools.partial(exchange_kernel, nz, nr),
        in_specs=[pl.BlockSpec(memory_space=pltpu.HBM)] * 6,
        out_specs=[vmem] * 3,
        out_shape=[
            jax.ShapeDtypeStruct((1, imps), f32),
            jax.ShapeDtypeStruct((WIDTH, D), bf16),
            jax.ShapeDtypeStruct((WIDTH, D), bf16),
        ],
        scratch_shapes=[
            pltpu.VMEM((CORES * nz, slots, D + WIDTH), bf16),
            pltpu.VMEM((1, imps), jnp.int32),
            pltpu.VMEM((1, imps), jnp.int32),
            *[pltpu.VMEM(shape, bf16) for shape in (items.shape, w_out.shape, (WIDTH, tokens), hist.shape)],
            pltpu.VMEM((nz, slots, WIDTH), bf16),
            pltpu.VMEM((nz, slots, WIDTH), bf16),
            pltpu.VMEM((nz, slots, WIDTH), f32),
            pltpu.VMEM((nz, slots, WIDTH), bf16),
            pltpu.VMEM((nz, slots, WIDTH), bf16),
            pltpu.VMEM((WIDTH, tokens), bf16),
            *sums,
            dma((7,)), dma(()), dma((nz * PARTS,)), dma((2,)),
            dma((4,)),
            dma((3, 6)), dma((3, 6)),
        ],
        compiler_params=pltpu.CompilerParams(
            collective_id=0, has_side_effects=True, vmem_limit_bytes=50 * 1024 * 1024
        ),
        name="exchange",
    )(imp_user[None], labels[None], both, items, w_out, hist)


def body(histories, lengths, counts, imp_user, items, labels, w_uvqk, w_out):
    both = forward(histories, lengths, counts, w_uvqk)
    logits, grad_out, grad_gate = exchange(
        imp_user, labels, both, items, w_out, histories.reshape(-1, D)
    )
    return (logits[0], grad_out, grad_gate.T)


def solution(mesh):
    return jax.shard_map(
        body,
        mesh=mesh,
        in_specs=(
            P(("own", "rep"), None, None),
            P(("own", "rep")),
            P(("own", "rep")),
            P(("own", "rep")),
            P(("own", "rep"), None),
            P(("own", "rep")),
            P(),
            P(),
        ),
        out_specs=(P(("own", "rep")), P(), P()),
        check_vma=False,
    )
```

```python
import functools

import jax
import jax.numpy as jnp
from jax import lax
from jax.experimental import pallas as pl
from jax.experimental.pallas import tpu as pltpu
from jax.sharding import PartitionSpec as P

D = 1024
HEADS = 4
HEAD = 128
HIST = 64
WIDTH = HEADS * HEAD
BIN = 128
STEP = 512
CORES = 2
LANES = 128
PARTS = 4
MESH = pl.DeviceIdType.MESH

EPS_NORM = 1e-06
EPS_LAYER = 1e-05


def sigmoid(v):
    return 0.5 * jnp.tanh(0.5 * v) + 0.5


def dot(a, b):
    return jnp.dot(a, b, preferred_element_type=jnp.float32)


def dot_t(a, b):
    return lax.dot_general(a, b, (((1,), (1,)), ((), ())), preferred_element_type=jnp.float32)


def forward_kernel(
    lengths_hbm, counts_hbm, h_hbm, w_hbm, w_out_hbm, both_hbm,
    x, w, w_out, user_ref, slope_ref, even, odd, sum_y, lengths, counts, load_sem, h_sem, w_sem, out_sem,
):
    slots = user_ref.shape[0]
    blocks = slots * HIST // STEP
    step_bins = STEP // BIN
    step_slots = STEP // HIST
    linear = (even, odd)

    def block_rows(i):
        return slice(i * STEP, (i + 1) * STEP)

    def part(n):
        return slice(n * WIDTH, (n + 1) * WIDTH)

    h_loads = [
        pltpu.make_async_copy(h_hbm.at[block_rows(i)], x.at[block_rows(i)], h_sem.at[i]) for i in range(blocks)
    ]
    w_loads = [pltpu.make_async_copy(w_hbm.at[:, part(n)], w.at[:, part(n)], w_sem.at[n]) for n in range(4)]
    small = [
        pltpu.make_async_copy(lengths_hbm, lengths, load_sem.at[0]),
        pltpu.make_async_copy(counts_hbm, counts, load_sem.at[1]),
        pltpu.make_async_copy(w_out_hbm, w_out, load_sem.at[2]),
    ]
    h_loads[0].start()
    for load in w_loads:
        load.start()
    for load in small[:2] + h_loads[1:] + small[2:]:
        load.start()

    def project(i, n):
        cols = slice(2 * n * WIDTH, 2 * (n + 1) * WIDTH)
        linear[i % 2][:, cols] = dot(x[block_rows(i), :], w[:, cols])

    def span_of(s):
        return jnp.where(s % 2 < counts[s // 2], lengths[s], 0)

    def one_bin(i, k):
        b = i * step_bins + k
        source = linear[i % 2]
        rows = slice(k * BIN, (k + 1) * BIN)
        first, second = span_of(2 * b), span_of(2 * b + 1)
        feats = x[b * BIN : (b + 1) * BIN, :].astype(jnp.float32)
        half_scale = 0.5 * lax.rsqrt(jnp.mean(feats * feats, -1, keepdims=True) + EPS_NORM)
        row = lax.broadcasted_iota(jnp.int32, (BIN, BIN), 0)
        col = lax.broadcasted_iota(jnp.int32, (BIN, BIN), 1)
        allowed = (
            (col <= row) & ((row < HIST) | (col >= HIST)) & (col < jnp.where(col < HIST, first, HIST + second))
        )
        span = jnp.where(row < HIST, first, second)
        share = jnp.where(row % HIST < span, 1.0 / jnp.maximum(span, 1).astype(jnp.float32), 0.0)
        back = share * half_scale

        def half_of(m, h):
            at = m * WIDTH + h * HEAD
            return source[rows, at : at + HEAD] * half_scale

        attended = []
        for h in range(HEADS):
            value, query, key = [
                (half * jnp.tanh(half) + half).astype(jnp.bfloat16) for half in (half_of(m, h) for m in (1, 2, 3))
            ]
            half = dot_t(query, key) * (0.5 * HEAD ** (-0.5))
            attn = jnp.where(allowed, half * jnp.tanh(half) + half, 0.0).astype(jnp.bfloat16)
            attended.append(dot(attn, value))
        center = jnp.sum(sum(attended), -1, keepdims=True) / WIDTH
        moved = [a - center for a in attended]
        spread = jnp.sum(sum(a * a for a in moved), -1, keepdims=True) / WIDTH
        norm = lax.rsqrt(spread + EPS_LAYER)
        for h in range(HEADS):
            cols = slice(h * HEAD, (h + 1) * HEAD)
            half = half_of(0, h)
            t = jnp.tanh(half)
            normal = moved[h] * norm
            mixed = share * normal * (half * t + half)
            for j in range(2):
                s = 2 * b + j
                sum_y[s : s + 1, cols] = jnp.sum(mixed[j * HIST : (j + 1) * HIST], 0, keepdims=True)
            slope = back * normal * ((1.0 + t) * (1.0 + half * (1.0 - t)))
            slope_ref[cols, b * BIN : (b + 1) * BIN] = slope.T.astype(jnp.bfloat16)

    def pool_x(i):
        slot = lax.broadcasted_iota(jnp.int32, (step_slots, STEP), 0)
        event = lax.broadcasted_iota(jnp.int32, (step_slots, STEP), 1) - slot * HIST
        which = lax.broadcasted_iota(jnp.int32, (step_slots, 1), 0)
        span = jnp.zeros((step_slots, 1), jnp.int32)
        for j in range(step_slots):
            span = jnp.where(which == j, span_of(i * step_slots + j), span)
        live = ((event >= 0) & (event < span)).astype(jnp.bfloat16)
        inverse = 1.0 / jnp.maximum(span, 1).astype(jnp.float32)
        return dot(live, x[block_rows(i), :]) * inverse

    def slope_out(i):
        cols = block_rows(i)
        return pltpu.make_async_copy(slope_ref.at[:, cols], both_hbm.at[0:WIDTH, cols], out_sem.at[i])

    h_loads[0].wait()
    for n in range(2):
        w_loads[2 * n].wait()
        w_loads[2 * n + 1].wait()
        project(0, n)
    for load in small[:2]:
        load.wait()
    pooled = []
    for i in range(blocks):
        if i + 1 < blocks:
            h_loads[i + 1].wait()
        for k in range(step_bins):
            if i + 1 < blocks and k % 2 == 0:
                project(i + 1, k // 2)
            one_bin(i, k)
        pooled.append(pool_x(i))
        slope_out(i).start()
    small[2].wait()
    py = sum_y[...].astype(jnp.bfloat16)
    user_ref[:, 0:D] = (jnp.concatenate(pooled, 0) + dot(py, w_out[...])).astype(jnp.bfloat16)
    user_ref[:, D : D + WIDTH] = py
    user_out = pltpu.make_async_copy(
        user_ref, both_hbm.at[WIDTH : WIDTH + slots, 0 : D + WIDTH], out_sem.at[blocks]
    )
    user_out.start()
    for i in range(blocks):
        slope_out(i).wait()
    user_out.wait()


def forward(histories, lengths, counts, w_uvqk, w_out):
    slots = histories.shape[0]
    tokens = slots * HIST
    blocks = tokens // STEP
    bf16, f32 = jnp.bfloat16, jnp.float32
    hbm = pl.BlockSpec(memory_space=pltpu.HBM)
    dma = pltpu.SemaphoreType.DMA
    return pl.pallas_call(
        forward_kernel,
        in_specs=[hbm] * 5,
        out_specs=hbm,
        out_shape=jax.ShapeDtypeStruct((WIDTH + slots, tokens), bf16),
        scratch_shapes=[
            pltpu.VMEM((tokens, D), bf16),
            pltpu.VMEM(w_uvqk.shape, bf16),
            pltpu.VMEM(w_out.shape, bf16),
            pltpu.VMEM((slots, D + WIDTH), bf16),
            pltpu.VMEM((WIDTH, tokens), bf16),
            pltpu.VMEM((STEP, 4 * WIDTH), f32),
            pltpu.VMEM((STEP, 4 * WIDTH), f32),
            pltpu.VMEM((slots, WIDTH), f32),
            pltpu.SMEM(lengths.shape, jnp.int32),
            pltpu.SMEM(counts.shape, jnp.int32),
            dma((3,)), dma((blocks,)), dma((4,)), dma((blocks + 1,)),
        ],
        compiler_params=pltpu.CompilerParams(vmem_limit_bytes=58 * 1024 * 1024),
        name="forward",
    )(lengths, counts, histories.reshape(tokens, D), w_uvqk, w_out)


def exchange_kernel(
    nz, nr, *args,
):
    loaded = 6
    user_src, label_src, both, items_src, w_src, hist_src = args[:loaded]
    deep, wide = WIDTH, D + WIDTH
    slots = both.shape[0] - deep
    sources = (user_src, label_src, both.at[deep : deep + slots, 0:wide], items_src, w_src, both.at[0:deep], hist_src)
    logit_ref, out_ref, gate_ref = args[loaded : loaded + 3]
    users = args[loaded + 3]
    user_ref, label_ref, items, w_out, slope, hist = args[loaded + 4 : loaded + 10]
    exchange_steps(
        nz, nr, sources, user_ref, label_ref, items, w_out, slope, hist,
        logit_ref, out_ref, gate_ref, users, *args[loaded + 10 :],
    )


def exchange_steps(
    nz, nr, sources, user_ref, label_ref, items, w_out, slope, hist,
    logit_ref, out_ref, gate_ref,
    users, pool_send, pool_core, pool_mine, pool_z, pool_got, pre, *rest,
):
    per_sum = 8
    sums = [rest[n * per_sum : (n + 1) * per_sum] for n in range(3)]
    (
        load_sem, user_send, user_recv, relay_sem, pool_sem, sum_send, sum_recv,
    ) = rest[3 * per_sum :]
    own = lax.axis_index("own")
    rep = lax.axis_index("rep")
    z, c = own // CORES, own % CORES
    other = 1 - c
    slots = users.shape[1]
    side = nz * slots
    half_w = D // CORES
    part_w = half_w // 2

    targets = (user_ref, label_ref, users.at[c * nz + z], items, w_out, slope, hist)
    loads = [
        pltpu.make_async_copy(source, target, load_sem.at[k])
        for k, (source, target) in enumerate(zip(sources, targets))
    ]
    for k in (2, 3, 4, 0, 1, 5, 6):
        loads[k].start()

    def z_id(k):
        return ((z + k) % nz * CORES + c, rep)

    def plane_id(k):
        return (own, (rep + k) % nr)

    sibling = (z * CORES + other, rep)

    def copy(source, target, send, recv, device):
        return pltpu.make_async_remote_copy(
            src_ref=source, dst_ref=target, send_sem=send, recv_sem=recv,
            device_id=device, device_id_type=MESH,
        )

    def each(count, step):
        def run(k, carry):
            step(k)
            return carry
        lax.fori_loop(1, count, run, 0)

    def signal(device):
        pl.semaphore_signal(barrier, inc=1, device_id=device, device_id_type=MESH)

    barrier = pltpu.get_barrier_semaphore()
    each(nz, lambda k: signal(z_id(k)))
    each(nr, lambda k: signal(plane_id(k)))
    signal(sibling)
    pl.semaphore_wait(barrier, nz - 1 + nr - 1 + 1)

    loads[2].wait()
    at = c * nz + z
    reach = nz // 2
    some = slots // 2
    ends = (z_id(1), z_id(nz - 1))

    def origin(way, step):
        return (z + nz - step if way == 0 else z + step) % nz

    def piece_of(block, piece):
        rows = pl.ds(piece % 2 * some, some)
        return users.at[block, rows, 0:D] if piece < 2 else users.at[block, rows, D : D + WIDTH]

    def hop(way, step, piece):
        spot = piece_of(c * nz + origin(way, step), piece)
        return copy(spot, spot, user_send, user_recv.at[(way * reach + step) * PARTS + piece], ends[way])

    def landed(way, step, piece):
        spot = piece_of(c * nz + origin(way, step + 1), piece)
        copy(spot, spot, user_send, user_recv.at[(way * reach + step) * PARTS + piece], ends[way]).wait_recv()

    def goes(way, step, piece):
        return step < reach - 1 or piece % 2 == way

    def pass_on(step, pieces):
        for piece in pieces:
            for way in range(2):
                if goes(way, step, piece):
                    landed(way, step, piece)
                if step + 1 < reach and goes(way, step + 1, piece):
                    hop(way, step + 1, piece).start()

    def user_relay(zz):
        spot = users.at[c * nz + zz, :, 0:D]
        return copy(spot, spot, relay_sem.at[0], relay_sem.at[1], sibling)

    for piece in range(PARTS):
        for way in range(2):
            hop(way, 0, piece).start()
    user_relay(z).start()
    loads[3].wait()
    loads[4].wait()
    item_w = dot_t(items[...], w_out[...]).astype(jnp.bfloat16)
    for step in range(reach):
        pass_on(step, (0, 1))
        user_relay(origin(0, step + 1)).start()
        if step + 1 < reach:
            user_relay(origin(1, step + 1)).start()
    pass_on(0, (2, 3))

    def line_of(core, first, size):
        return users.at[pl.ds(core * nz, nz), :, first : first + size]

    def line_relay(first, size, k):
        return copy(
            line_of(c, first, size), line_of(other, first, size), relay_sem.at[k], relay_sem.at[k + 1], sibling
        )

    loads[0].wait()
    loads[1].wait()
    line_relay(0, D, 0).wait_recv()
    pass_on(1, (2, 3))

    index = user_ref[...]
    source = (index % slots) // 2
    place = (source % CORES) * side + (source // CORES) * slots + index // slots * 2 + index % 2
    table = dot_t(users[:, :, 0:D].reshape(2 * side, D), items[...])
    imps = index.shape[1]
    picked = lax.broadcasted_iota(jnp.int32, (2 * side, imps), 0) == place
    logits = jnp.sum(jnp.where(picked, table, 0.0), 0, keepdims=True)
    logit_ref[...] = logits
    pass_on(2, (2, 3))
    error = sigmoid(logits) - label_ref[...].astype(jnp.float32)

    line = lax.broadcasted_iota(jnp.int32, (side, imps), 0)

    def pool_side(core):
        weight = jnp.where(line + core * side == place, error, 0.0).astype(jnp.bfloat16)
        return dot(weight, item_w).reshape(nz, slots, WIDTH)

    pool_send[...] = pool_side(other).astype(jnp.bfloat16)
    pool_copy = copy(pool_send, pool_core, pool_sem.at[0], pool_sem.at[1], sibling)
    pool_copy.start()
    pool_mine[...] = pool_side(c)
    pool_copy.wait()
    pool_z[...] = (pool_mine[...] + pool_core[...].astype(jnp.float32)).astype(jnp.bfloat16)
    each(nz, lambda k: copy(pool_z.at[(z + k) % nz], pool_got.at[z], pool_sem.at[2], pool_sem.at[3], z_id(k)).start())
    pool_got[z] = pool_z[z]

    pass_on(reach - 1, (2, 3))
    spot = line_of(c, D, WIDTH)
    py_relay = copy(spot, spot, relay_sem.at[2], relay_sem.at[3], sibling)
    py_relay.start()
    line_relay(D, WIDTH, 2).wait_recv()
    turned = users[:, :, D : D + WIDTH].reshape(2 * side, WIDTH).astype(jnp.float32).T.astype(jnp.bfloat16)
    chosen = dot(turned, picked.astype(jnp.bfloat16))
    chosen = (chosen * error).astype(jnp.bfloat16)

    def columns(core, first=0, size=half_w):
        step = min(size, part_w)
        return pl.ds(pl.multiple_of(core * half_w + first, step), size)

    places = ((out_ref, 0, half_w), (gate_ref, 0, part_w), (gate_ref, part_w, part_w))
    block = WIDTH // nr
    CORE, PLANE, PIECE, BACK, WIDE, LAST = range(6)

    def sems(n, stage):
        return sum_send.at[n, stage], sum_recv.at[n, stage]

    def core_copy(n):
        return copy(sums[n][1], sums[n][2], *sems(n, CORE), sibling)

    def core_start(n, part):
        sums[n][1][...] = part.astype(jnp.bfloat16)
        core_copy(n).start()

    def plane_rows(k):
        return pl.ds(pl.multiple_of((rep + k) % nr * block, block), block)

    def core_end(n):
        mine, _, core_got, half, plane_got = sums[n][:5]
        core_copy(n).wait()
        half[...] = (mine[...] + core_got[...].astype(jnp.float32)).astype(jnp.bfloat16)
        each(nr, lambda k: copy(half.at[plane_rows(k)], plane_got.at[rep], *sems(n, PLANE), plane_id(k)).start())
        plane_got[rep] = half[plane_rows(0), :]

    def plane_all(n):
        return copy(sums[n][3].at[pl.ds(0, block * (nr - 1))], sums[n][4].at[pl.ds(0, nr - 1)], *sems(n, PLANE), sibling)

    def piece_spot(n, zz):
        across = places[n][2] // LANES
        tall = block * across // nz
        return (
            pl.ds(pl.multiple_of(zz // across * tall, tall), tall),
            pl.ds(pl.multiple_of(zz % across * LANES, LANES), LANES),
        )

    def plane_end(n):
        plane_got, row_sum, piece_got = sums[n][4:7]
        plane_all(n).wait_recv()
        total = plane_got[0].astype(jnp.float32)
        for k in range(1, nr):
            total += plane_got[k].astype(jnp.float32)
        row_sum[...] = total
        each(nz, lambda k: copy(row_sum.at[piece_spot(n, (z + k) % nz)], piece_got.at[z], *sems(n, PIECE), z_id(k)).start())
        piece_got[z] = row_sum[piece_spot(n, z)]

    def piece_all(n):
        spot = sums[n][6].at[pl.ds(0, nz - 1)]
        return copy(spot, spot, *sems(n, PIECE), sibling)

    def piece_end(n):
        piece_got, final = sums[n][6:8]
        piece_all(n).wait_recv()
        total = piece_got[0]
        for k in range(1, nz):
            total += piece_got[k]
        spot = final.at[piece_spot(n, z)]
        spot[...] = total
        each(nz, lambda k: copy(spot, spot, *sems(n, BACK), z_id(k)).start())

    def back_all(n):
        spot = sums[n][6].at[pl.ds(0, nz - 1)]
        return copy(spot, spot, *sems(n, BACK), sibling)

    def wide_spot(n, core, k):
        ref, first, size = places[n]
        return ref.at[plane_rows(k), columns(core, first, size)]

    def back_end(n):
        back_all(n).wait_recv()
        spot = wide_spot(n, c, 0)
        spot[...] = sums[n][7][...].astype(jnp.bfloat16)
        each(nr, lambda k: copy(spot, spot, *sems(n, WIDE), plane_id(k)).start())

    def wide_all(n):
        ref, first, size = places[n]
        spot = ref.at[pl.ds(0, block * (nr - 1)), columns(c, first, size)]
        return copy(spot, spot, *sems(n, WIDE), sibling)

    def last_copy(n, core):
        ref, first, size = places[n]
        spot = ref.at[:, columns(core, first, size)]
        return copy(spot, spot, *sems(n, LAST), sibling)

    def wide_end(n):
        wide_all(n).wait_recv()
        last_copy(n, c).start()

    core_start(0, dot(chosen, items[:, columns(other)]))
    sums[0][0][...] = dot(chosen, items[:, columns(c)])
    core_end(0)

    pool_spot = pool_got.at[pl.ds(0, nz - 1)]
    pool_all = copy(pool_spot, pool_spot, pool_sem.at[2], pool_sem.at[3], sibling)
    loads[5].wait()
    loads[6].wait()
    pool_all.wait_recv()
    total = pool_got[0].astype(jnp.float32)
    for k in range(1, nz):
        total += pool_got[k].astype(jnp.float32)
    pool_t = total.astype(jnp.bfloat16).astype(jnp.float32).T.astype(jnp.bfloat16)
    tokens = slots * HIST
    slot = lax.broadcasted_iota(jnp.int32, (slots, tokens), 0)
    event = lax.broadcasted_iota(jnp.int32, (slots, tokens), 1)
    holds = (event // HIST == slot).astype(jnp.bfloat16)
    pre[...] = (dot(pool_t, holds) * slope[...].astype(jnp.float32)).astype(jnp.bfloat16)
    gate_part = dot(pre[...], hist[:, columns(other)])
    core_start(1, gate_part[:, 0:part_w])
    core_start(2, gate_part[:, part_w:half_w])
    plane_end(0)
    gate_part = dot(pre[...], hist[:, columns(c)])
    sums[1][0][...] = gate_part[:, 0:part_w]
    core_end(1)
    sums[2][0][...] = gate_part[:, part_w:half_w]
    core_end(2)
    piece_end(0)
    plane_end(1)
    back_end(0)
    plane_end(2)
    piece_end(1)
    piece_end(2)
    back_end(1)
    wide_end(0)
    back_end(2)
    wide_end(1)
    wide_end(2)

    spot = users.at[pl.ds(0, nz - 1)]
    copy(spot, spot, user_send, user_recv.at[0], sibling).wait_send()
    line_relay(0, D, 0).wait_send()
    py_relay.wait_send()
    pool_all.wait_send()
    for n in range(3):
        plane_all(n).wait_send()
        piece_all(n).wait_send()
        back_all(n).wait_send()
        wide_all(n).wait_send()
    for n in range(3):
        last_copy(n, other).wait()


def exchange(imp_user, labels, both, items, w_out, hist):
    nz = lax.axis_size("own") // CORES
    nr = lax.axis_size("rep")
    slots = both.shape[0] - WIDTH
    tokens = both.shape[1]
    imps = imp_user.shape[0]
    half_w = D // CORES
    bf16, f32 = jnp.bfloat16, jnp.float32
    vmem = pl.BlockSpec(memory_space=pltpu.VMEM)
    dma = pltpu.SemaphoreType.DMA
    sums = []
    for size in (half_w, half_w // 2, half_w // 2):
        block = WIDTH // nr
        sums += [
            pltpu.VMEM((WIDTH, size), f32),
            pltpu.VMEM((WIDTH, size), bf16),
            pltpu.VMEM((WIDTH, size), bf16),
            pltpu.VMEM((WIDTH, size), bf16),
            pltpu.VMEM((nr, block, size), bf16),
            pltpu.VMEM((block, size), f32),
            pltpu.VMEM((nz, block * size // nz // LANES, LANES), f32),
            pltpu.VMEM((block, size), f32),
        ]
    return pl.pallas_call(
        functools.partial(exchange_kernel, nz, nr),
        in_specs=[pl.BlockSpec(memory_space=pltpu.HBM)] * 6,
        out_specs=[vmem] * 3,
        out_shape=[
            jax.ShapeDtypeStruct((1, imps), f32),
            jax.ShapeDtypeStruct((WIDTH, D), bf16),
            jax.ShapeDtypeStruct((WIDTH, D), bf16),
        ],
        scratch_shapes=[
            pltpu.VMEM((CORES * nz, slots, D + WIDTH), bf16),
            pltpu.VMEM((1, imps), jnp.int32),
            pltpu.VMEM((1, imps), jnp.int32),
            *[pltpu.VMEM(shape, bf16) for shape in (items.shape, w_out.shape, (WIDTH, tokens), hist.shape)],
            pltpu.VMEM((nz, slots, WIDTH), bf16),
            pltpu.VMEM((nz, slots, WIDTH), bf16),
            pltpu.VMEM((nz, slots, WIDTH), f32),
            pltpu.VMEM((nz, slots, WIDTH), bf16),
            pltpu.VMEM((nz, slots, WIDTH), bf16),
            pltpu.VMEM((WIDTH, tokens), bf16),
            *sums,
            dma((7,)), dma(()), dma((nz * PARTS,)), dma((4,)),
            dma((4,)),
            dma((3, 6)), dma((3, 6)),
        ],
        compiler_params=pltpu.CompilerParams(
            collective_id=0, has_side_effects=True, vmem_limit_bytes=50 * 1024 * 1024
        ),
        name="exchange",
    )(imp_user[None], labels[None], both, items, w_out, hist)


def body(histories, lengths, counts, imp_user, items, labels, w_uvqk, w_out):
    both = forward(histories, lengths, counts, w_uvqk, w_out)
    logits, grad_out, grad_gate = exchange(
        imp_user, labels, both, items, w_out, histories.reshape(-1, D)
    )
    return (logits[0], grad_out, grad_gate.T)


def solution(mesh):
    return jax.shard_map(
        body,
        mesh=mesh,
        in_specs=(
            P(("own", "rep"), None, None),
            P(("own", "rep")),
            P(("own", "rep")),
            P(("own", "rep")),
            P(("own", "rep"), None),
            P(("own", "rep")),
            P(),
            P(),
        ),
        out_specs=(P(("own", "rep")), P(), P()),
        check_vma=False,
    )
```

```python
import functools

import jax
import jax.numpy as jnp
from jax import lax
from jax.experimental import pallas as pl
from jax.experimental.pallas import tpu as pltpu
from jax.sharding import PartitionSpec as P

D = 1024
HEADS = 4
HEAD = 128
HIST = 64
WIDTH = HEADS * HEAD
BIN = 128
STEP = 512
CORES = 2
LANES = 128
PARTS = 4
MESH = pl.DeviceIdType.MESH

EPS_NORM = 1e-06
EPS_LAYER = 1e-05


def sigmoid(v):
    return 0.5 * jnp.tanh(0.5 * v) + 0.5


def dot(a, b):
    return jnp.dot(a, b, preferred_element_type=jnp.float32)


def dot_t(a, b):
    return lax.dot_general(a, b, (((1,), (1,)), ((), ())), preferred_element_type=jnp.float32)


def step_kernel(
    nz, nr, imp_hbm, label_hbm, lengths_hbm, counts_hbm, items_hbm, w_out_hbm, w_hbm, h_hbm,
    logit_hbm, out_hbm, gate_hbm,
    user_ref, label_ref, items, w_out, w, x, slope, even, odd, sum_y, logit_ref, out_ref, gate_ref,
    users, pool_send, pool_core, pool_mine, pool_z, pool_got, pre, *rest,
):
    per_sum = 8
    sums = [rest[n * per_sum : (n + 1) * per_sum] for n in range(3)]
    (
        lengths, counts, load_sem, h_sem, w_sem, out_sem,
        user_send, user_recv, relay_sem, pool_sem, sum_send, sum_recv,
    ) = rest[3 * per_sum :]
    own = lax.axis_index("own")
    rep = lax.axis_index("rep")
    z, c = own // CORES, own % CORES
    other = 1 - c
    slots = users.shape[1]
    side = nz * slots
    half_w = D // CORES
    part_w = half_w // 2
    blocks = slots * HIST // STEP
    step_bins = STEP // BIN
    step_slots = STEP // HIST
    linear = (even, odd)

    def block_rows(i):
        return slice(i * STEP, (i + 1) * STEP)

    def part(n):
        return slice(n * WIDTH, (n + 1) * WIDTH)

    h_loads = [
        pltpu.make_async_copy(h_hbm.at[block_rows(i)], x.at[block_rows(i)], h_sem.at[i]) for i in range(blocks)
    ]
    w_loads = [pltpu.make_async_copy(w_hbm.at[:, part(n)], w.at[:, part(n)], w_sem.at[n]) for n in range(4)]
    loads = [
        pltpu.make_async_copy(source, target, load_sem.at[k])
        for k, (source, target) in enumerate(
            (
                (lengths_hbm, lengths), (counts_hbm, counts), (w_out_hbm, w_out), (items_hbm, items),
                (imp_hbm, user_ref), (label_hbm, label_ref),
            )
        )
    ]
    h_loads[0].start()
    for load in w_loads:
        load.start()
    for load in loads[:2] + h_loads[1:] + loads[2:]:
        load.start()

    def z_id(k):
        return ((z + k) % nz * CORES + c, rep)

    def plane_id(k):
        return (own, (rep + k) % nr)

    sibling = (z * CORES + other, rep)

    def copy(source, target, send, recv, device):
        return pltpu.make_async_remote_copy(
            src_ref=source, dst_ref=target, send_sem=send, recv_sem=recv,
            device_id=device, device_id_type=MESH,
        )

    def signal(device):
        pl.semaphore_signal(barrier, inc=1, device_id=device, device_id_type=MESH)

    barrier = pltpu.get_barrier_semaphore()
    for k in range(1, nz):
        signal(z_id(k))
    for k in range(1, nr):
        signal(plane_id(k))
    signal(sibling)

    at = c * nz + z
    reach = nz // 2
    width = (D + WIDTH) // PARTS
    ends = (z_id(1), z_id(nz - 1))

    def origin(way, step):
        return (z + nz - step if way == 0 else z + step) % nz

    def hop(way, step, part):
        spot = users.at[c * nz + origin(way, step), :, part * width : (part + 1) * width]
        return copy(spot, spot, user_send, user_recv.at[(way * reach + step) * PARTS + part], ends[way])

    def landed(way, step, part):
        spot = users.at[c * nz + origin(way, step + 1), :, part * width : (part + 1) * width]
        copy(spot, spot, user_send, user_recv.at[(way * reach + step) * PARTS + part], ends[way]).wait_recv()

    def goes(way, step, part):
        return step < reach - 1 or part % 2 == way

    def user_relay(zz):
        spot = users.at[c * nz + zz]
        return copy(spot, spot, relay_sem.at[0], relay_sem.at[1], sibling)

    def project(i, n):
        linear[i % 2][:, part(n)] = dot(x[block_rows(i), :], w[:, part(n)])

    def span_of(s):
        return jnp.where(s % 2 < counts[s // 2], lengths[s], 0)

    def one_bin(i, k):
        b = i * step_bins + k
        source = linear[i % 2]
        rows = slice(k * BIN, (k + 1) * BIN)
        first, second = span_of(2 * b), span_of(2 * b + 1)
        feats = x[b * BIN : (b + 1) * BIN, :].astype(jnp.float32)
        half_scale = 0.5 * lax.rsqrt(jnp.mean(feats * feats, -1, keepdims=True) + EPS_NORM)
        row = lax.broadcasted_iota(jnp.int32, (BIN, BIN), 0)
        col = lax.broadcasted_iota(jnp.int32, (BIN, BIN), 1)
        allowed = (
            (col <= row) & ((row < HIST) | (col >= HIST)) & (col < jnp.where(col < HIST, first, HIST + second))
        )
        span = jnp.where(row < HIST, first, second)
        share = jnp.where(row % HIST < span, 1.0 / jnp.maximum(span, 1).astype(jnp.float32), 0.0)
        back = share * half_scale

        def half_of(m, h):
            at = m * WIDTH + h * HEAD
            return source[rows, at : at + HEAD] * half_scale

        attended = []
        for h in range(HEADS):
            value, query, key = [
                (half * jnp.tanh(half) + half).astype(jnp.bfloat16) for half in (half_of(m, h) for m in (1, 2, 3))
            ]
            half = dot_t(query, key) * (0.5 * HEAD ** (-0.5))
            attn = jnp.where(allowed, half * jnp.tanh(half) + half, 0.0).astype(jnp.bfloat16)
            attended.append(dot(attn, value))
        center = jnp.sum(sum(attended), -1, keepdims=True) / WIDTH
        moved = [a - center for a in attended]
        spread = jnp.sum(sum(a * a for a in moved), -1, keepdims=True) / WIDTH
        norm = lax.rsqrt(spread + EPS_LAYER)
        for h in range(HEADS):
            cols = slice(h * HEAD, (h + 1) * HEAD)
            half = half_of(0, h)
            t = jnp.tanh(half)
            normal = moved[h] * norm
            mixed = share * normal * (half * t + half)
            for j in range(2):
                s = 2 * b + j
                sum_y[s : s + 1, cols] = jnp.sum(mixed[j * HIST : (j + 1) * HIST], 0, keepdims=True)
            falls = back * normal * ((1.0 + t) * (1.0 + half * (1.0 - t)))
            slope[cols, b * BIN : (b + 1) * BIN] = falls.T.astype(jnp.bfloat16)

    def pool_x(i):
        slot = lax.broadcasted_iota(jnp.int32, (step_slots, STEP), 0)
        event = lax.broadcasted_iota(jnp.int32, (step_slots, STEP), 1) - slot * HIST
        which = lax.broadcasted_iota(jnp.int32, (step_slots, 1), 0)
        span = jnp.zeros((step_slots, 1), jnp.int32)
        for j in range(step_slots):
            span = jnp.where(which == j, span_of(i * step_slots + j), span)
        live = ((event >= 0) & (event < span)).astype(jnp.bfloat16)
        inverse = 1.0 / jnp.maximum(span, 1).astype(jnp.float32)
        return dot(live, x[block_rows(i), :]) * inverse

    h_loads[0].wait()
    for n in range(4):
        w_loads[n].wait()
        project(0, n)
    for load in loads[:3]:
        load.wait()
    pooled = []
    for i in range(blocks):
        if i + 1 < blocks:
            h_loads[i + 1].wait()
        for k in range(step_bins):
            if i + 1 < blocks:
                project(i + 1, k)
            one_bin(i, k)
        pooled.append(pool_x(i))
    users[at, :, 0:D] = jnp.concatenate(pooled, 0).astype(jnp.bfloat16)
    users[at, :, D : D + WIDTH] = sum_y[...].astype(jnp.bfloat16)
    pl.semaphore_wait(barrier, nz - 1 + nr - 1 + 1)
    for piece in range(PARTS):
        for way in range(2):
            hop(way, 0, piece).start()
    user_relay(z).start()
    for load in loads[3:]:
        load.wait()
    item_w = dot_t(items[...], w_out[...]).astype(jnp.bfloat16)
    for step in range(reach):
        for piece in range(PARTS):
            for way in range(2):
                if goes(way, step, piece):
                    landed(way, step, piece)
                if step + 1 < reach and goes(way, step + 1, piece):
                    hop(way, step + 1, piece).start()
        user_relay(origin(0, step + 1)).start()
        if step + 1 < reach:
            user_relay(origin(1, step + 1)).start()
    all_relays = copy(
        users.at[pl.ds(c * nz, nz)], users.at[pl.ds(other * nz, nz)], relay_sem.at[0], relay_sem.at[1], sibling
    )
    all_relays.wait_recv()

    index = user_ref[...]
    source = (index % slots) // 2
    place = (source % CORES) * side + (source // CORES) * slots + index // slots * 2 + index % 2
    table = dot_t(users[:, :, 0:D].reshape(2 * side, D), items[...]) + dot_t(
        users[:, :, D : D + WIDTH].reshape(2 * side, WIDTH), item_w
    )
    imps = index.shape[1]
    picked = lax.broadcasted_iota(jnp.int32, (2 * side, imps), 0) == place
    logits = jnp.sum(jnp.where(picked, table, 0.0), 0, keepdims=True)
    logit_ref[...] = logits
    logit_out = pltpu.make_async_copy(logit_ref, logit_hbm, out_sem.at[0])
    logit_out.start()
    error = sigmoid(logits) - label_ref[...].astype(jnp.float32)

    line = lax.broadcasted_iota(jnp.int32, (side, imps), 0)

    def pool_side(core):
        weight = jnp.where(line + core * side == place, error, 0.0).astype(jnp.bfloat16)
        return dot(weight, item_w).reshape(nz, slots, WIDTH)

    pool_send[...] = pool_side(other).astype(jnp.bfloat16)
    pool_copy = copy(pool_send, pool_core, pool_sem.at[0], pool_sem.at[1], sibling)
    pool_copy.start()
    pool_mine[...] = pool_side(c)
    turned = users[:, :, D : D + WIDTH].reshape(2 * side, WIDTH).astype(jnp.float32).T.astype(jnp.bfloat16)
    pool_copy.wait()
    pool_z[...] = (pool_mine[...] + pool_core[...].astype(jnp.float32)).astype(jnp.bfloat16)
    for k in range(1, nz):
        copy(pool_z.at[(z + k) % nz], pool_got.at[z], pool_sem.at[2], pool_sem.at[3], z_id(k)).start()
    pool_got[z] = pool_z[z]

    chosen = dot(turned, picked.astype(jnp.bfloat16))
    chosen = (chosen * error).astype(jnp.bfloat16)

    def columns(core, first=0, size=half_w):
        step = min(size, part_w)
        return pl.ds(pl.multiple_of(core * half_w + first, step), size)

    places = ((out_ref, 0, half_w), (gate_ref, 0, part_w), (gate_ref, part_w, part_w))
    block = WIDTH // nr
    CORE, PLANE, PIECE, BACK, WIDE, LAST = range(6)

    def sems(n, stage):
        return sum_send.at[n, stage], sum_recv.at[n, stage]

    def core_copy(n):
        return copy(sums[n][1], sums[n][2], *sems(n, CORE), sibling)

    def core_start(n, part):
        sums[n][1][...] = part.astype(jnp.bfloat16)
        core_copy(n).start()

    def plane_rows(k):
        return pl.ds(pl.multiple_of((rep + k) % nr * block, block), block)

    def core_end(n):
        mine, _, core_got, half, plane_got = sums[n][:5]
        core_copy(n).wait()
        half[...] = (mine[...] + core_got[...].astype(jnp.float32)).astype(jnp.bfloat16)
        for k in range(1, nr):
            copy(half.at[plane_rows(k)], plane_got.at[rep], *sems(n, PLANE), plane_id(k)).start()
        plane_got[rep] = half[plane_rows(0), :]

    def plane_all(n):
        return copy(sums[n][3].at[pl.ds(0, block * (nr - 1))], sums[n][4].at[pl.ds(0, nr - 1)], *sems(n, PLANE), sibling)

    def piece_spot(n, zz):
        across = places[n][2] // LANES
        tall = block * across // nz
        return (
            pl.ds(pl.multiple_of(zz // across * tall, tall), tall),
            pl.ds(pl.multiple_of(zz % across * LANES, LANES), LANES),
        )

    def plane_end(n):
        plane_got, row_sum, piece_got = sums[n][4:7]
        plane_all(n).wait_recv()
        total = plane_got[0].astype(jnp.float32)
        for k in range(1, nr):
            total += plane_got[k].astype(jnp.float32)
        row_sum[...] = total
        for k in range(1, nz):
            copy(row_sum.at[piece_spot(n, (z + k) % nz)], piece_got.at[z], *sems(n, PIECE), z_id(k)).start()
        piece_got[z] = row_sum[piece_spot(n, z)]

    def piece_all(n):
        spot = sums[n][6].at[pl.ds(0, nz - 1)]
        return copy(spot, spot, *sems(n, PIECE), sibling)

    def piece_end(n):
        piece_got, final = sums[n][6:8]
        piece_all(n).wait_recv()
        total = piece_got[0]
        for k in range(1, nz):
            total += piece_got[k]
        spot = final.at[piece_spot(n, z)]
        spot[...] = total
        for k in range(1, nz):
            copy(spot, spot, *sems(n, BACK), z_id(k)).start()

    def back_all(n):
        spot = sums[n][6].at[pl.ds(0, nz - 1)]
        return copy(spot, spot, *sems(n, BACK), sibling)

    def wide_spot(n, core, k):
        ref, first, size = places[n]
        return ref.at[plane_rows(k), columns(core, first, size)]

    def back_end(n):
        back_all(n).wait_recv()
        spot = wide_spot(n, c, 0)
        spot[...] = sums[n][7][...].astype(jnp.bfloat16)
        for k in range(1, nr):
            copy(spot, spot, *sems(n, WIDE), plane_id(k)).start()

    def wide_all(n):
        ref, first, size = places[n]
        spot = ref.at[pl.ds(0, block * (nr - 1)), columns(c, first, size)]
        return copy(spot, spot, *sems(n, WIDE), sibling)

    def last_copy(n, core):
        ref, first, size = places[n]
        spot = ref.at[:, columns(core, first, size)]
        return copy(spot, spot, *sems(n, LAST), sibling)

    def wide_end(n):
        wide_all(n).wait_recv()
        last_copy(n, c).start()

    core_start(0, dot(chosen, items[:, columns(other)]))
    sums[0][0][...] = dot(chosen, items[:, columns(c)])
    core_end(0)

    pool_spot = pool_got.at[pl.ds(0, nz - 1)]
    pool_all = copy(pool_spot, pool_spot, pool_sem.at[2], pool_sem.at[3], sibling)
    pool_all.wait_recv()
    total = pool_got[0].astype(jnp.float32)
    for k in range(1, nz):
        total += pool_got[k].astype(jnp.float32)
    pool_t = total.astype(jnp.bfloat16).astype(jnp.float32).T.astype(jnp.bfloat16)
    tokens = slots * HIST
    slot = lax.broadcasted_iota(jnp.int32, (slots, tokens), 0)
    event = lax.broadcasted_iota(jnp.int32, (slots, tokens), 1)
    holds = (event // HIST == slot).astype(jnp.bfloat16)
    pre[...] = (dot(pool_t, holds) * slope[...].astype(jnp.float32)).astype(jnp.bfloat16)
    gate_part = dot(pre[...], x[:, columns(other)])
    core_start(1, gate_part[:, 0:part_w])
    core_start(2, gate_part[:, part_w:half_w])
    plane_end(0)
    gate_part = dot(pre[...], x[:, columns(c)])
    sums[1][0][...] = gate_part[:, 0:part_w]
    core_end(1)
    sums[2][0][...] = gate_part[:, part_w:half_w]
    core_end(2)
    piece_end(0)
    plane_end(1)
    back_end(0)
    plane_end(2)
    piece_end(1)
    piece_end(2)
    back_end(1)
    wide_end(0)
    back_end(2)
    wide_end(1)
    wide_end(2)

    def strips(n):
        ref, first, size = places[n]
        target = gate_hbm if n else out_hbm
        return [
            pltpu.make_async_copy(
                ref.at[:, core * half_w + first : core * half_w + first + size],
                target.at[:, core * half_w + first : core * half_w + first + size],
                out_sem.at[1 + n * CORES + core],
            )
            for core in range(CORES)
        ]

    for n in range(3):
        last_copy(n, other).wait()
        for strip in strips(n):
            strip.start()
    spot = users.at[pl.ds(0, nz - 1)]
    copy(spot, spot, user_send, user_recv.at[0], sibling).wait_send()
    all_relays.wait_send()
    pool_all.wait_send()
    for n in range(3):
        plane_all(n).wait_send()
        piece_all(n).wait_send()
        back_all(n).wait_send()
        wide_all(n).wait_send()
    logit_out.wait()
    for n in range(3):
        for strip in strips(n):
            strip.wait()


def train_step(histories, lengths, counts, imp_user, items, labels, w_uvqk, w_out):
    nz = lax.axis_size("own") // CORES
    nr = lax.axis_size("rep")
    slots = histories.shape[0]
    tokens = slots * HIST
    blocks = tokens // STEP
    imps = imp_user.shape[0]
    half_w = D // CORES
    bf16, f32 = jnp.bfloat16, jnp.float32
    hbm = pl.BlockSpec(memory_space=pltpu.HBM)
    dma = pltpu.SemaphoreType.DMA
    sums = []
    for size in (half_w, half_w // 2, half_w // 2):
        block = WIDTH // nr
        sums += [
            pltpu.VMEM((WIDTH, size), f32),
            pltpu.VMEM((WIDTH, size), bf16),
            pltpu.VMEM((WIDTH, size), bf16),
            pltpu.VMEM((WIDTH, size), bf16),
            pltpu.VMEM((nr, block, size), bf16),
            pltpu.VMEM((block, size), f32),
            pltpu.VMEM((nz, block * size // nz // LANES, LANES), f32),
            pltpu.VMEM((block, size), f32),
        ]
    return pl.pallas_call(
        functools.partial(step_kernel, nz, nr),
        in_specs=[hbm] * 8,
        out_specs=[hbm] * 3,
        out_shape=[
            jax.ShapeDtypeStruct((1, imps), f32),
            jax.ShapeDtypeStruct((WIDTH, D), bf16),
            jax.ShapeDtypeStruct((WIDTH, D), bf16),
        ],
        scratch_shapes=[
            pltpu.VMEM((1, imps), jnp.int32),
            pltpu.VMEM((1, imps), jnp.int32),
            pltpu.VMEM(items.shape, bf16),
            pltpu.VMEM(w_out.shape, bf16),
            pltpu.VMEM(w_uvqk.shape, bf16),
            pltpu.VMEM((tokens, D), bf16),
            pltpu.VMEM((WIDTH, tokens), bf16),
            pltpu.VMEM((STEP, 4 * WIDTH), f32),
            pltpu.VMEM((STEP, 4 * WIDTH), f32),
            pltpu.VMEM((slots, WIDTH), f32),
            pltpu.VMEM((1, imps), f32),
            pltpu.VMEM((WIDTH, D), bf16),
            pltpu.VMEM((WIDTH, D), bf16),
            pltpu.VMEM((CORES * nz, slots, D + WIDTH), bf16),
            pltpu.VMEM((nz, slots, WIDTH), bf16),
            pltpu.VMEM((nz, slots, WIDTH), bf16),
            pltpu.VMEM((nz, slots, WIDTH), f32),
            pltpu.VMEM((nz, slots, WIDTH), bf16),
            pltpu.VMEM((nz, slots, WIDTH), bf16),
            pltpu.VMEM((WIDTH, tokens), bf16),
            *sums,
            pltpu.SMEM(lengths.shape, jnp.int32),
            pltpu.SMEM(counts.shape, jnp.int32),
            dma((6,)), dma((blocks,)), dma((4,)), dma((1 + 3 * CORES,)),
            dma(()), dma((nz * PARTS,)), dma((4,)), dma((4,)),
            dma((3, 6)), dma((3, 6)),
        ],
        compiler_params=pltpu.CompilerParams(
            collective_id=0, has_side_effects=True, vmem_limit_bytes=58 * 1024 * 1024
        ),
        name="train_step",
    )(
        imp_user[None], labels[None], lengths, counts, items, w_out, w_uvqk, histories.reshape(tokens, D)
    )


def finish_kernel(logit_in, out_in, gate_in, logit_out, out_out, gate_out, turned, rows, flat, logit, sem):
    pieces = gate_in.shape[0] // LANES

    def moves(source, between, target, k):
        return (
            pltpu.make_async_copy(source, between, sem.at[0, k]),
            pltpu.make_async_copy(between, target, sem.at[1, k]),
        )

    def part(k):
        return pl.ds(k * LANES, LANES)

    gate_in_moves = [
        pltpu.make_async_copy(gate_in.at[part(k)], rows.at[part(k)], sem.at[0, k]) for k in range(pieces)
    ]
    out_moves = [
        moves(out_in.at[part(k)], flat.at[part(k)], out_out.at[part(k)], pieces + k) for k in range(pieces)
    ]
    logit_moves = moves(logit_in, logit, logit_out, 2 * pieces)
    for load in gate_in_moves:
        load.start()
    for load, _ in out_moves:
        load.start()
    logit_moves[0].start()
    for k in range(pieces):
        gate_in_moves[k].wait()
        turned[:, k * LANES : (k + 1) * LANES] = rows[part(k), :].astype(jnp.float32).T.astype(jnp.bfloat16)
        out_moves[k][0].wait()
        out_moves[k][1].start()
    last = pltpu.make_async_copy(turned, gate_out, sem.at[1, 0])
    last.start()
    logit_moves[0].wait()
    logit_moves[1].start()
    for _, store in out_moves:
        store.wait()
    logit_moves[1].wait()
    last.wait()


def finish(logits, grad_out, gate_t):
    hbm = pl.BlockSpec(memory_space=pltpu.HBM)
    across, deep = gate_t.shape
    return pl.pallas_call(
        finish_kernel,
        in_specs=[hbm] * 3,
        out_specs=[hbm] * 3,
        out_shape=[
            jax.ShapeDtypeStruct(logits.shape, logits.dtype),
            jax.ShapeDtypeStruct(grad_out.shape, grad_out.dtype),
            jax.ShapeDtypeStruct((deep, across), gate_t.dtype),
        ],
        scratch_shapes=[
            pltpu.VMEM((deep, across), gate_t.dtype),
            pltpu.VMEM((across, deep), gate_t.dtype),
            pltpu.VMEM(grad_out.shape, grad_out.dtype),
            pltpu.VMEM(logits.shape, logits.dtype),
            pltpu.SemaphoreType.DMA((2, 1 + 2 * across // LANES)),
        ],
        compiler_params=pltpu.CompilerParams(vmem_limit_bytes=58 * 1024 * 1024),
        name="finish",
    )(logits, grad_out, gate_t)


def body(histories, lengths, counts, imp_user, items, labels, w_uvqk, w_out):
    logits, grad_out, grad_gate = finish(
        *train_step(histories, lengths, counts, imp_user, items, labels, w_uvqk, w_out)
    )
    return (logits[0], grad_out, grad_gate)


def solution(mesh):
    return jax.shard_map(
        body,
        mesh=mesh,
        in_specs=(
            P(("own", "rep"), None, None),
            P(("own", "rep")),
            P(("own", "rep")),
            P(("own", "rep")),
            P(("own", "rep"), None),
            P(("own", "rep")),
            P(),
            P(),
        ),
        out_specs=(P(("own", "rep")), P(), P()),
        check_vma=False,
    )
```

```python
import functools

import jax
import jax.numpy as jnp
from jax import lax
from jax.experimental import pallas as pl
from jax.experimental.pallas import tpu as pltpu
from jax.sharding import PartitionSpec as P

D = 1024
HEADS = 4
HEAD = 128
HIST = 64
WIDTH = HEADS * HEAD
BIN = 128
STEP = 512
CORES = 2
LANES = 128
PARTS = 2
MESH = pl.DeviceIdType.MESH

EPS_NORM = 1e-06
EPS_LAYER = 1e-05


def sigmoid(v):
    return 0.5 * jnp.tanh(0.5 * v) + 0.5


def dot(a, b):
    return jnp.dot(a, b, preferred_element_type=jnp.float32)


def dot_t(a, b):
    return lax.dot_general(a, b, (((1,), (1,)), ((), ())), preferred_element_type=jnp.float32)


def step_kernel(
    nz, nr, imp_hbm, label_hbm, lengths_hbm, counts_hbm, items_hbm, w_out_hbm, w_hbm, h_hbm,
    logit_hbm, out_hbm, gate_hbm,
    user_ref, label_ref, items, w_out, w, x, slope, even, odd, sum_y, logit_ref, out_ref, gate_ref,
    users, pool_send, pool_core, pool_mine, pool_z, pool_got, pre, *rest,
):
    per_sum = 8
    sums = [rest[n * per_sum : (n + 1) * per_sum] for n in range(3)]
    (
        lengths, counts, load_sem, h_sem, w_sem, out_sem,
        user_send, user_recv, py_send, py_recv, relay_sem, pool_sem, sum_send, sum_recv,
    ) = rest[3 * per_sum :]
    own = lax.axis_index("own")
    rep = lax.axis_index("rep")
    z, c = own // CORES, own % CORES
    other = 1 - c
    slots = users.shape[1]
    side = nz * slots
    half_w = D // CORES
    part_w = half_w // 2
    blocks = slots * HIST // STEP
    step_bins = STEP // BIN
    step_slots = STEP // HIST
    linear = (even, odd)

    def block_rows(i):
        return slice(i * STEP, (i + 1) * STEP)

    def part(n):
        return slice(n * WIDTH, (n + 1) * WIDTH)

    h_loads = [
        pltpu.make_async_copy(h_hbm.at[block_rows(i)], x.at[block_rows(i)], h_sem.at[i]) for i in range(blocks)
    ]
    w_loads = [pltpu.make_async_copy(w_hbm.at[:, part(n)], w.at[:, part(n)], w_sem.at[n]) for n in range(4)]
    loads = [
        pltpu.make_async_copy(source, target, load_sem.at[k])
        for k, (source, target) in enumerate(
            (
                (lengths_hbm, lengths), (counts_hbm, counts), (w_out_hbm, w_out), (items_hbm, items),
                (imp_hbm, user_ref), (label_hbm, label_ref),
            )
        )
    ]
    h_loads[0].start()
    for load in w_loads:
        load.start()
    for load in loads[:2] + h_loads[1:] + loads[2:]:
        load.start()

    def z_id(k):
        return ((z + k) % nz * CORES + c, rep)

    def plane_id(k):
        return (own, (rep + k) % nr)

    sibling = (z * CORES + other, rep)

    def copy(source, target, send, recv, device):
        return pltpu.make_async_remote_copy(
            src_ref=source, dst_ref=target, send_sem=send, recv_sem=recv,
            device_id=device, device_id_type=MESH,
        )

    def signal(device):
        pl.semaphore_signal(barrier, inc=1, device_id=device, device_id_type=MESH)

    barrier = pltpu.get_barrier_semaphore()
    for k in range(1, nz):
        signal(z_id(k))
    for k in range(1, nr):
        signal(plane_id(k))
    signal(sibling)

    at = c * nz + z
    reach = nz // 2
    width = D // PARTS
    ends = (z_id(1), z_id(nz - 1))

    def origin(way, step):
        return (z + nz - step if way == 0 else z + step) % nz

    def hop(way, step, part):
        spot = users.at[c * nz + origin(way, step), :, part * width : (part + 1) * width]
        return copy(spot, spot, user_send, user_recv.at[(way * reach + step) * PARTS + part], ends[way])

    def landed(way, step, part):
        spot = users.at[c * nz + origin(way, step + 1), :, part * width : (part + 1) * width]
        copy(spot, spot, user_send, user_recv.at[(way * reach + step) * PARTS + part], ends[way]).wait_recv()

    def goes(way, step, part):
        return step < reach - 1 or part % 2 == way

    def pass_on(step):
        for piece in range(PARTS):
            for way in range(2):
                if goes(way, step, piece):
                    landed(way, step, piece)
                if step + 1 < reach and goes(way, step + 1, piece):
                    hop(way, step + 1, piece).start()
        user_relay(origin(0, step + 1), 0).start()
        if step + 1 < reach:
            user_relay(origin(1, step + 1), 0).start()

    def user_relay(zz, k):
        spot = users.at[c * nz + zz, :, D * k : D + WIDTH * k]
        return copy(spot, spot, relay_sem.at[2 * k], relay_sem.at[2 * k + 1], sibling)

    def all_relays(k):
        cols = slice(D * k, D + WIDTH * k)
        return copy(
            users.at[pl.ds(c * nz, nz), :, cols], users.at[pl.ds(other * nz, nz), :, cols],
            relay_sem.at[2 * k], relay_sem.at[2 * k + 1], sibling,
        )

    def direct(k):
        spot = users.at[at, :, D : D + WIDTH]
        return copy(spot, spot, py_send, py_recv.at[z], z_id(k))

    def direct_landed(zz):
        spot = users.at[c * nz + zz, :, D : D + WIDTH]
        copy(spot, spot, py_send, py_recv.at[zz], sibling).wait_recv()

    def project(i, n):
        linear[i % 2][:, part(n)] = dot(x[block_rows(i), :], w[:, part(n)])

    def span_of(s):
        return jnp.where(s % 2 < counts[s // 2], lengths[s], 0)

    def one_bin(i, k):
        b = i * step_bins + k
        source = linear[i % 2]
        rows = slice(k * BIN, (k + 1) * BIN)
        first, second = span_of(2 * b), span_of(2 * b + 1)
        feats = x[b * BIN : (b + 1) * BIN, :].astype(jnp.float32)
        half_scale = 0.5 * lax.rsqrt(jnp.mean(feats * feats, -1, keepdims=True) + EPS_NORM)
        row = lax.broadcasted_iota(jnp.int32, (BIN, BIN), 0)
        col = lax.broadcasted_iota(jnp.int32, (BIN, BIN), 1)
        allowed = (
            (col <= row) & ((row < HIST) | (col >= HIST)) & (col < jnp.where(col < HIST, first, HIST + second))
        )
        span = jnp.where(row < HIST, first, second)
        share = jnp.where(row % HIST < span, 1.0 / jnp.maximum(span, 1).astype(jnp.float32), 0.0)
        back = share * half_scale

        def half_of(m, h):
            at = m * WIDTH + h * HEAD
            return source[rows, at : at + HEAD] * half_scale

        attended = []
        for h in range(HEADS):
            value, query, key = [
                (half * jnp.tanh(half) + half).astype(jnp.bfloat16) for half in (half_of(m, h) for m in (1, 2, 3))
            ]
            half = dot_t(query, key) * (0.5 * HEAD ** (-0.5))
            attn = jnp.where(allowed, half * jnp.tanh(half) + half, 0.0).astype(jnp.bfloat16)
            attended.append(dot(attn, value))
        center = jnp.sum(sum(attended), -1, keepdims=True) / WIDTH
        moved = [a - center for a in attended]
        spread = jnp.sum(sum(a * a for a in moved), -1, keepdims=True) / WIDTH
        norm = lax.rsqrt(spread + EPS_LAYER)
        for h in range(HEADS):
            cols = slice(h * HEAD, (h + 1) * HEAD)
            half = half_of(0, h)
            t = jnp.tanh(half)
            normal = moved[h] * norm
            mixed = share * normal * (half * t + half)
            for j in range(2):
                s = 2 * b + j
                sum_y[s : s + 1, cols] = jnp.sum(mixed[j * HIST : (j + 1) * HIST], 0, keepdims=True)
            falls = back * normal * ((1.0 + t) * (1.0 + half * (1.0 - t)))
            slope[cols, b * BIN : (b + 1) * BIN] = falls.T.astype(jnp.bfloat16)

    def pool_x(i):
        slot = lax.broadcasted_iota(jnp.int32, (step_slots, STEP), 0)
        event = lax.broadcasted_iota(jnp.int32, (step_slots, STEP), 1) - slot * HIST
        which = lax.broadcasted_iota(jnp.int32, (step_slots, 1), 0)
        span = jnp.zeros((step_slots, 1), jnp.int32)
        for j in range(step_slots):
            span = jnp.where(which == j, span_of(i * step_slots + j), span)
        live = ((event >= 0) & (event < span)).astype(jnp.bfloat16)
        inverse = 1.0 / jnp.maximum(span, 1).astype(jnp.float32)
        return dot(live, x[block_rows(i), :]) * inverse

    h_loads[0].wait()
    for n in range(4):
        w_loads[n].wait()
        project(0, n)
    for load in loads[:3]:
        load.wait()
    for i in range(blocks):
        if i == 0:
            for load in h_loads[1:]:
                load.wait()
        for k in range(step_bins):
            if i + 1 < blocks:
                project(i + 1, k)
            one_bin(i, k)
            if k == step_bins // 2 - 1 and i >= 2:
                pass_on(2 * i - 3)
        if i == 0:
            px = jnp.concatenate([pool_x(j) for j in range(blocks)], 0)
            users[at, :, 0:D] = px.astype(jnp.bfloat16)
            pl.semaphore_wait(barrier, nz - 1 + nr - 1 + 1)
            for piece in range(PARTS):
                for way in range(2):
                    hop(way, 0, piece).start()
            user_relay(z, 0).start()
        elif i < blocks - 1:
            pass_on(2 * i - 2)
    users[at, :, D : D + WIDTH] = sum_y[...].astype(jnp.bfloat16)
    order = [k for near in range(1, reach) for k in (near, nz - near)] + [reach]
    for k in order:
        direct(k).start()
    user_relay(z, 1).start()
    for load in loads[3:]:
        load.wait()
    item_w = dot_t(items[...], w_out[...]).astype(jnp.bfloat16)
    all_relays(0).wait_recv()
    table_x = dot_t(users[:, :, 0:D].reshape(2 * side, D), items[...])
    for k in order:
        zz = (z + k) % nz
        direct_landed(zz)
        user_relay(zz, 1).start()
    all_relays(1).wait_recv()

    index = user_ref[...]
    source = (index % slots) // 2
    place = (source % CORES) * side + (source // CORES) * slots + index // slots * 2 + index % 2
    table = table_x + dot_t(users[:, :, D : D + WIDTH].reshape(2 * side, WIDTH), item_w)
    imps = index.shape[1]
    picked = lax.broadcasted_iota(jnp.int32, (2 * side, imps), 0) == place
    logits = jnp.sum(jnp.where(picked, table, 0.0), 0, keepdims=True)
    logit_ref[...] = logits
    logit_out = pltpu.make_async_copy(logit_ref, logit_hbm, out_sem.at[0])
    logit_out.start()
    error = sigmoid(logits) - label_ref[...].astype(jnp.float32)

    line = lax.broadcasted_iota(jnp.int32, (side, imps), 0)

    def pool_side(core):
        weight = jnp.where(line + core * side == place, error, 0.0).astype(jnp.bfloat16)
        return dot(weight, item_w).reshape(nz, slots, WIDTH)

    pool_send[...] = pool_side(other).astype(jnp.bfloat16)
    pool_copy = copy(pool_send, pool_core, pool_sem.at[0], pool_sem.at[1], sibling)
    pool_copy.start()
    pool_mine[...] = pool_side(c)
    turned = users[:, :, D : D + WIDTH].reshape(2 * side, WIDTH).astype(jnp.float32).T.astype(jnp.bfloat16)
    pool_copy.wait()
    pool_z[...] = (pool_mine[...] + pool_core[...].astype(jnp.float32)).astype(jnp.bfloat16)
    for k in range(1, nz):
        copy(pool_z.at[(z + k) % nz], pool_got.at[z], pool_sem.at[2], pool_sem.at[3], z_id(k)).start()
    pool_got[z] = pool_z[z]

    chosen = dot(turned, picked.astype(jnp.bfloat16))
    chosen = (chosen * error).astype(jnp.bfloat16)

    def columns(core, first=0, size=half_w):
        step = min(size, part_w)
        return pl.ds(pl.multiple_of(core * half_w + first, step), size)

    places = ((out_ref, 0, half_w), (gate_ref, 0, part_w), (gate_ref, part_w, part_w))
    block = WIDTH // nr
    CORE, PLANE, PIECE, BACK, WIDE, LAST = range(6)

    def sems(n, stage):
        return sum_send.at[n, stage], sum_recv.at[n, stage]

    def core_copy(n):
        return copy(sums[n][1], sums[n][2], *sems(n, CORE), sibling)

    def core_start(n, part):
        sums[n][1][...] = part.astype(jnp.bfloat16)
        core_copy(n).start()

    def plane_rows(k):
        return pl.ds(pl.multiple_of((rep + k) % nr * block, block), block)

    def core_end(n):
        mine, _, core_got, half, plane_got = sums[n][:5]
        core_copy(n).wait()
        half[...] = (mine[...] + core_got[...].astype(jnp.float32)).astype(jnp.bfloat16)
        for k in range(1, nr):
            copy(half.at[plane_rows(k)], plane_got.at[rep], *sems(n, PLANE), plane_id(k)).start()
        plane_got[rep] = half[plane_rows(0), :]

    def plane_all(n):
        return copy(sums[n][3].at[pl.ds(0, block * (nr - 1))], sums[n][4].at[pl.ds(0, nr - 1)], *sems(n, PLANE), sibling)

    def piece_spot(n, zz):
        across = places[n][2] // LANES
        tall = block * across // nz
        return (
            pl.ds(pl.multiple_of(zz // across * tall, tall), tall),
            pl.ds(pl.multiple_of(zz % across * LANES, LANES), LANES),
        )

    def plane_end(n):
        plane_got, row_sum, piece_got = sums[n][4:7]
        plane_all(n).wait_recv()
        total = plane_got[0].astype(jnp.float32)
        for k in range(1, nr):
            total += plane_got[k].astype(jnp.float32)
        row_sum[...] = total
        for k in range(1, nz):
            copy(row_sum.at[piece_spot(n, (z + k) % nz)], piece_got.at[z], *sems(n, PIECE), z_id(k)).start()
        piece_got[z] = row_sum[piece_spot(n, z)]

    def piece_all(n):
        spot = sums[n][6].at[pl.ds(0, nz - 1)]
        return copy(spot, spot, *sems(n, PIECE), sibling)

    def piece_end(n):
        piece_got, final = sums[n][6:8]
        piece_all(n).wait_recv()
        total = piece_got[0]
        for k in range(1, nz):
            total += piece_got[k]
        spot = final.at[piece_spot(n, z)]
        spot[...] = total
        for k in range(1, nz):
            copy(spot, spot, *sems(n, BACK), z_id(k)).start()

    def back_all(n):
        spot = sums[n][6].at[pl.ds(0, nz - 1)]
        return copy(spot, spot, *sems(n, BACK), sibling)

    def wide_spot(n, core, k):
        ref, first, size = places[n]
        return ref.at[plane_rows(k), columns(core, first, size)]

    def back_end(n):
        back_all(n).wait_recv()
        spot = wide_spot(n, c, 0)
        spot[...] = sums[n][7][...].astype(jnp.bfloat16)
        for k in range(1, nr):
            copy(spot, spot, *sems(n, WIDE), plane_id(k)).start()

    def wide_all(n):
        ref, first, size = places[n]
        spot = ref.at[pl.ds(0, block * (nr - 1)), columns(c, first, size)]
        return copy(spot, spot, *sems(n, WIDE), sibling)

    def last_copy(n, core):
        ref, first, size = places[n]
        spot = ref.at[:, columns(core, first, size)]
        return copy(spot, spot, *sems(n, LAST), sibling)

    def wide_end(n):
        wide_all(n).wait_recv()
        last_copy(n, c).start()

    core_start(0, dot(chosen, items[:, columns(other)]))
    sums[0][0][...] = dot(chosen, items[:, columns(c)])
    core_end(0)

    pool_spot = pool_got.at[pl.ds(0, nz - 1)]
    pool_all = copy(pool_spot, pool_spot, pool_sem.at[2], pool_sem.at[3], sibling)
    pool_all.wait_recv()
    total = pool_got[0].astype(jnp.float32)
    for k in range(1, nz):
        total += pool_got[k].astype(jnp.float32)
    pool_t = total.astype(jnp.bfloat16).astype(jnp.float32).T.astype(jnp.bfloat16)
    tokens = slots * HIST
    slot = lax.broadcasted_iota(jnp.int32, (slots, tokens), 0)
    event = lax.broadcasted_iota(jnp.int32, (slots, tokens), 1)
    holds = (event // HIST == slot).astype(jnp.bfloat16)
    pre[...] = (dot(pool_t, holds) * slope[...].astype(jnp.float32)).astype(jnp.bfloat16)
    gate_part = dot(pre[...], x[:, columns(other)])
    core_start(1, gate_part[:, 0:part_w])
    core_start(2, gate_part[:, part_w:half_w])
    plane_end(0)
    gate_part = dot(pre[...], x[:, columns(c)])
    sums[1][0][...] = gate_part[:, 0:part_w]
    core_end(1)
    sums[2][0][...] = gate_part[:, part_w:half_w]
    core_end(2)
    piece_end(0)
    plane_end(1)
    back_end(0)
    plane_end(2)
    piece_end(1)
    piece_end(2)
    back_end(1)
    wide_end(0)
    back_end(2)
    wide_end(1)
    wide_end(2)

    def strips(n):
        ref, first, size = places[n]
        target = gate_hbm if n else out_hbm
        return [
            pltpu.make_async_copy(
                ref.at[:, core * half_w + first : core * half_w + first + size],
                target.at[:, core * half_w + first : core * half_w + first + size],
                out_sem.at[1 + n * CORES + core],
            )
            for core in range(CORES)
        ]

    for n in range(3):
        last_copy(n, other).wait()
        for strip in strips(n):
            strip.start()
    spot = users.at[pl.ds(0, nz - 1), :, 0:D]
    copy(spot, spot, user_send, user_recv.at[0], sibling).wait_send()
    spot = users.at[pl.ds(0, nz - 1), :, D : D + WIDTH]
    copy(spot, spot, py_send, py_recv.at[0], sibling).wait_send()
    for k in range(2):
        all_relays(k).wait_send()
    pool_all.wait_send()
    for n in range(3):
        plane_all(n).wait_send()
        piece_all(n).wait_send()
        back_all(n).wait_send()
        wide_all(n).wait_send()
    logit_out.wait()
    for n in range(3):
        for strip in strips(n):
            strip.wait()


def train_step(histories, lengths, counts, imp_user, items, labels, w_uvqk, w_out):
    nz = lax.axis_size("own") // CORES
    nr = lax.axis_size("rep")
    slots = histories.shape[0]
    tokens = slots * HIST
    blocks = tokens // STEP
    imps = imp_user.shape[0]
    half_w = D // CORES
    bf16, f32 = jnp.bfloat16, jnp.float32
    hbm = pl.BlockSpec(memory_space=pltpu.HBM)
    dma = pltpu.SemaphoreType.DMA
    sums = []
    for size in (half_w, half_w // 2, half_w // 2):
        block = WIDTH // nr
        sums += [
            pltpu.VMEM((WIDTH, size), f32),
            pltpu.VMEM((WIDTH, size), bf16),
            pltpu.VMEM((WIDTH, size), bf16),
            pltpu.VMEM((WIDTH, size), bf16),
            pltpu.VMEM((nr, block, size), bf16),
            pltpu.VMEM((block, size), f32),
            pltpu.VMEM((nz, block * size // nz // LANES, LANES), f32),
            pltpu.VMEM((block, size), f32),
        ]
    return pl.pallas_call(
        functools.partial(step_kernel, nz, nr),
        in_specs=[hbm] * 8,
        out_specs=[hbm] * 3,
        out_shape=[
            jax.ShapeDtypeStruct((1, imps), f32),
            jax.ShapeDtypeStruct((WIDTH, D), bf16),
            jax.ShapeDtypeStruct((WIDTH, D), bf16),
        ],
        scratch_shapes=[
            pltpu.VMEM((1, imps), jnp.int32),
            pltpu.VMEM((1, imps), jnp.int32),
            pltpu.VMEM(items.shape, bf16),
            pltpu.VMEM(w_out.shape, bf16),
            pltpu.VMEM(w_uvqk.shape, bf16),
            pltpu.VMEM((tokens, D), bf16),
            pltpu.VMEM((WIDTH, tokens), bf16),
            pltpu.VMEM((STEP, 4 * WIDTH), f32),
            pltpu.VMEM((STEP, 4 * WIDTH), f32),
            pltpu.VMEM((slots, WIDTH), f32),
            pltpu.VMEM((1, imps), f32),
            pltpu.VMEM((WIDTH, D), bf16),
            pltpu.VMEM((WIDTH, D), bf16),
            pltpu.VMEM((CORES * nz, slots, D + WIDTH), bf16),
            pltpu.VMEM((nz, slots, WIDTH), bf16),
            pltpu.VMEM((nz, slots, WIDTH), bf16),
            pltpu.VMEM((nz, slots, WIDTH), f32),
            pltpu.VMEM((nz, slots, WIDTH), bf16),
            pltpu.VMEM((nz, slots, WIDTH), bf16),
            pltpu.VMEM((WIDTH, tokens), bf16),
            *sums,
            pltpu.SMEM(lengths.shape, jnp.int32),
            pltpu.SMEM(counts.shape, jnp.int32),
            dma((6,)), dma((blocks,)), dma((4,)), dma((1 + 3 * CORES,)),
            dma(()), dma((nz * PARTS,)), dma(()), dma((nz,)), dma((4,)), dma((4,)),
            dma((3, 6)), dma((3, 6)),
        ],
        compiler_params=pltpu.CompilerParams(
            collective_id=0, has_side_effects=True, vmem_limit_bytes=58 * 1024 * 1024
        ),
        name="train_step",
    )(
        imp_user[None], labels[None], lengths, counts, items, w_out, w_uvqk, histories.reshape(tokens, D)
    )


def finish_kernel(logit_in, out_in, gate_in, logit_out, out_out, gate_out, turned, rows, flat, logit, sem):
    pieces = gate_in.shape[0] // LANES

    def moves(source, between, target, k):
        return (
            pltpu.make_async_copy(source, between, sem.at[0, k]),
            pltpu.make_async_copy(between, target, sem.at[1, k]),
        )

    def part(k):
        return pl.ds(k * LANES, LANES)

    gate_in_moves = [
        pltpu.make_async_copy(gate_in.at[part(k)], rows.at[part(k)], sem.at[0, k]) for k in range(pieces)
    ]
    out_moves = [
        moves(out_in.at[part(k)], flat.at[part(k)], out_out.at[part(k)], pieces + k) for k in range(pieces)
    ]
    logit_moves = moves(logit_in, logit, logit_out, 2 * pieces)
    for load in gate_in_moves:
        load.start()
    for load, _ in out_moves:
        load.start()
    logit_moves[0].start()
    for k in range(pieces):
        gate_in_moves[k].wait()
        turned[:, k * LANES : (k + 1) * LANES] = rows[part(k), :].astype(jnp.float32).T.astype(jnp.bfloat16)
        out_moves[k][0].wait()
        out_moves[k][1].start()
    last = pltpu.make_async_copy(turned, gate_out, sem.at[1, 0])
    last.start()
    logit_moves[0].wait()
    logit_moves[1].start()
    for _, store in out_moves:
        store.wait()
    logit_moves[1].wait()
    last.wait()


def finish(logits, grad_out, gate_t):
    hbm = pl.BlockSpec(memory_space=pltpu.HBM)
    across, deep = gate_t.shape
    return pl.pallas_call(
        finish_kernel,
        in_specs=[hbm] * 3,
        out_specs=[hbm] * 3,
        out_shape=[
            jax.ShapeDtypeStruct(logits.shape, logits.dtype),
            jax.ShapeDtypeStruct(grad_out.shape, grad_out.dtype),
            jax.ShapeDtypeStruct((deep, across), gate_t.dtype),
        ],
        scratch_shapes=[
            pltpu.VMEM((deep, across), gate_t.dtype),
            pltpu.VMEM((across, deep), gate_t.dtype),
            pltpu.VMEM(grad_out.shape, grad_out.dtype),
            pltpu.VMEM(logits.shape, logits.dtype),
            pltpu.SemaphoreType.DMA((2, 1 + 2 * across // LANES)),
        ],
        compiler_params=pltpu.CompilerParams(vmem_limit_bytes=58 * 1024 * 1024),
        name="finish",
    )(logits, grad_out, gate_t)


def body(histories, lengths, counts, imp_user, items, labels, w_uvqk, w_out):
    logits, grad_out, grad_gate = finish(
        *train_step(histories, lengths, counts, imp_user, items, labels, w_uvqk, w_out)
    )
    return (logits[0], grad_out, grad_gate)


def solution(mesh):
    return jax.shard_map(
        body,
        mesh=mesh,
        in_specs=(
            P(("own", "rep"), None, None),
            P(("own", "rep")),
            P(("own", "rep")),
            P(("own", "rep")),
            P(("own", "rep"), None),
            P(("own", "rep")),
            P(),
            P(),
        ),
        out_specs=(P(("own", "rep")), P(), P()),
        check_vma=False,
    )
```

```python
import functools

import jax
import jax.numpy as jnp
from jax import lax
from jax.experimental import pallas as pl
from jax.experimental.pallas import tpu as pltpu
from jax.sharding import PartitionSpec as P

D = 1024
HEADS = 4
HEAD = 128
HIST = 64
WIDTH = HEADS * HEAD
BIN = 128
STEP = 512
CORES = 2
LANES = 128
PARTS = 2
MESH = pl.DeviceIdType.MESH

EPS_NORM = 1e-06
EPS_LAYER = 1e-05


def sigmoid(v):
    return 0.5 * jnp.tanh(0.5 * v) + 0.5


def dot(a, b):
    return jnp.dot(a, b, preferred_element_type=jnp.float32)


def dot_t(a, b):
    return lax.dot_general(a, b, (((1,), (1,)), ((), ())), preferred_element_type=jnp.float32)


def step_kernel(
    nz, nr, imp_hbm, label_hbm, lengths_hbm, counts_hbm, items_hbm, w_out_hbm, w_hbm, h_hbm,
    logit_hbm, out_hbm, gate_hbm,
    user_ref, label_ref, items, w_out, w, x, slope, even, odd, sum_y, logit_ref, out_ref, gate_ref,
    users, pool_send, pool_core, pool_mine, pool_z, pool_got, pre, *rest,
):
    per_sum = 8
    sums = [rest[n * per_sum : (n + 1) * per_sum] for n in range(3)]
    (
        lengths, counts, load_sem, h_sem, w_sem, out_sem,
        user_send, user_recv, py_send, py_recv, relay_sem, pool_sem, sum_send, sum_recv,
    ) = rest[3 * per_sum :]
    own = lax.axis_index("own")
    rep = lax.axis_index("rep")
    z, c = own // CORES, own % CORES
    other = 1 - c
    slots = users.shape[1]
    side = nz * slots
    half_w = D // CORES
    part_w = half_w // 2
    blocks = slots * HIST // STEP
    step_bins = STEP // BIN
    step_slots = STEP // HIST
    linear = (even, odd)

    def block_rows(i):
        return slice(i * STEP, (i + 1) * STEP)

    def part(n):
        return slice(n * WIDTH, (n + 1) * WIDTH)

    h_loads = [
        pltpu.make_async_copy(h_hbm.at[block_rows(i)], x.at[block_rows(i)], h_sem.at[i]) for i in range(blocks)
    ]
    w_loads = [pltpu.make_async_copy(w_hbm.at[:, part(n)], w.at[:, part(n)], w_sem.at[n]) for n in range(4)]
    loads = [
        pltpu.make_async_copy(source, target, load_sem.at[k])
        for k, (source, target) in enumerate(
            (
                (lengths_hbm, lengths), (counts_hbm, counts), (w_out_hbm, w_out), (items_hbm, items),
                (imp_hbm, user_ref), (label_hbm, label_ref),
            )
        )
    ]
    h_loads[0].start()
    for load in w_loads:
        load.start()
    for load in loads[:2] + h_loads[1:] + loads[2:]:
        load.start()

    def z_id(k):
        return ((z + k) % nz * CORES + c, rep)

    def plane_id(k):
        return (own, (rep + k) % nr)

    sibling = (z * CORES + other, rep)

    def copy(source, target, send, recv, device):
        return pltpu.make_async_remote_copy(
            src_ref=source, dst_ref=target, send_sem=send, recv_sem=recv,
            device_id=device, device_id_type=MESH,
        )

    def signal(device):
        pl.semaphore_signal(barrier, inc=1, device_id=device, device_id_type=MESH)

    barrier = pltpu.get_barrier_semaphore()
    for k in range(1, nz):
        signal(z_id(k))
    for k in range(1, nr):
        signal(plane_id(k))
    signal(sibling)

    at = c * nz + z
    reach = nz // 2
    width = D // PARTS
    ends = (z_id(1), z_id(nz - 1))

    def origin(way, step):
        return (z + nz - step if way == 0 else z + step) % nz

    def hop(way, step, part):
        spot = users.at[c * nz + origin(way, step), :, part * width : (part + 1) * width]
        return copy(spot, spot, user_send, user_recv.at[(way * reach + step) * PARTS + part], ends[way])

    def landed(way, step, part):
        spot = users.at[c * nz + origin(way, step + 1), :, part * width : (part + 1) * width]
        copy(spot, spot, user_send, user_recv.at[(way * reach + step) * PARTS + part], ends[way]).wait_recv()

    def goes(way, step, part):
        return step < reach - 1 or part % 2 == way

    def pass_on(step):
        for piece in range(PARTS):
            for way in range(2):
                if goes(way, step, piece):
                    landed(way, step, piece)
                if step + 1 < reach and goes(way, step + 1, piece):
                    hop(way, step + 1, piece).start()
        user_relay(origin(0, step + 1), 0).start()
        if step + 1 < reach:
            user_relay(origin(1, step + 1), 0).start()

    def user_relay(zz, k):
        spot = users.at[c * nz + zz, :, D * k : D + WIDTH * k]
        return copy(spot, spot, relay_sem.at[2 * k], relay_sem.at[2 * k + 1], sibling)

    def all_relays(k):
        cols = slice(D * k, D + WIDTH * k)
        return copy(
            users.at[pl.ds(c * nz, nz), :, cols], users.at[pl.ds(other * nz, nz), :, cols],
            relay_sem.at[2 * k], relay_sem.at[2 * k + 1], sibling,
        )

    order = [k for near in range(1, reach) for k in (near, nz - near)] + [reach]
    some = slots // 2

    def direct(g):
        rows = slice(g * some, (g + 1) * some)
        users[at, rows, D : D + WIDTH] = sum_y[rows, :].astype(jnp.bfloat16)
        spot = users.at[at, rows, D : D + WIDTH]
        for k in order:
            copy(spot, spot, py_send, py_recv.at[g * nz + z], z_id(k)).start()

    def direct_landed(zz):
        for g in range(2):
            spot = users.at[c * nz + zz, g * some : (g + 1) * some, D : D + WIDTH]
            copy(spot, spot, py_send, py_recv.at[g * nz + zz], sibling).wait_recv()

    def project(i, n):
        linear[i % 2][:, part(n)] = dot(x[block_rows(i), :], w[:, part(n)])

    def span_of(s):
        return jnp.where(s % 2 < counts[s // 2], lengths[s], 0)

    def one_bin(i, k):
        b = i * step_bins + k
        source = linear[i % 2]
        rows = slice(k * BIN, (k + 1) * BIN)
        first, second = span_of(2 * b), span_of(2 * b + 1)
        feats = x[b * BIN : (b + 1) * BIN, :].astype(jnp.float32)
        half_scale = 0.5 * lax.rsqrt(jnp.mean(feats * feats, -1, keepdims=True) + EPS_NORM)
        row = lax.broadcasted_iota(jnp.int32, (BIN, BIN), 0)
        col = lax.broadcasted_iota(jnp.int32, (BIN, BIN), 1)
        allowed = (
            (col <= row) & ((row < HIST) | (col >= HIST)) & (col < jnp.where(col < HIST, first, HIST + second))
        )
        span = jnp.where(row < HIST, first, second)
        share = jnp.where(row % HIST < span, 1.0 / jnp.maximum(span, 1).astype(jnp.float32), 0.0)
        back = share * half_scale

        def half_of(m, h):
            at = m * WIDTH + h * HEAD
            return source[rows, at : at + HEAD] * half_scale

        attended = []
        for h in range(HEADS):
            value, query, key = [
                (half * jnp.tanh(half) + half).astype(jnp.bfloat16) for half in (half_of(m, h) for m in (1, 2, 3))
            ]
            half = dot_t(query, key) * (0.5 * HEAD ** (-0.5))
            attn = jnp.where(allowed, half * jnp.tanh(half) + half, 0.0).astype(jnp.bfloat16)
            attended.append(dot(attn, value))
        center = jnp.sum(sum(attended), -1, keepdims=True) / WIDTH
        moved = [a - center for a in attended]
        spread = jnp.sum(sum(a * a for a in moved), -1, keepdims=True) / WIDTH
        norm = lax.rsqrt(spread + EPS_LAYER)
        for h in range(HEADS):
            cols = slice(h * HEAD, (h + 1) * HEAD)
            half = half_of(0, h)
            t = jnp.tanh(half)
            normal = moved[h] * norm
            mixed = share * normal * (half * t + half)
            for j in range(2):
                s = 2 * b + j
                sum_y[s : s + 1, cols] = jnp.sum(mixed[j * HIST : (j + 1) * HIST], 0, keepdims=True)
            falls = back * normal * ((1.0 + t) * (1.0 + half * (1.0 - t)))
            slope[cols, b * BIN : (b + 1) * BIN] = falls.T.astype(jnp.bfloat16)

    def pool_x(i):
        slot = lax.broadcasted_iota(jnp.int32, (step_slots, STEP), 0)
        event = lax.broadcasted_iota(jnp.int32, (step_slots, STEP), 1) - slot * HIST
        which = lax.broadcasted_iota(jnp.int32, (step_slots, 1), 0)
        span = jnp.zeros((step_slots, 1), jnp.int32)
        for j in range(step_slots):
            span = jnp.where(which == j, span_of(i * step_slots + j), span)
        live = ((event >= 0) & (event < span)).astype(jnp.bfloat16)
        inverse = 1.0 / jnp.maximum(span, 1).astype(jnp.float32)
        return dot(live, x[block_rows(i), :]) * inverse

    h_loads[0].wait()
    for n in range(4):
        w_loads[n].wait()
        project(0, n)
    for load in loads[:3]:
        load.wait()
    for i in range(blocks):
        if i == 0:
            for load in h_loads[1:]:
                load.wait()
        for k in range(step_bins):
            if i + 1 < blocks:
                project(i + 1, k)
            one_bin(i, k)
            if k == step_bins // 2 - 1 and i >= 2:
                pass_on(2 * i - 3)
        if i == 0:
            px = jnp.concatenate([pool_x(j) for j in range(blocks)], 0)
            users[at, :, 0:D] = px.astype(jnp.bfloat16)
            pl.semaphore_wait(barrier, nz - 1 + nr - 1 + 1)
            for piece in range(PARTS):
                for way in range(2):
                    hop(way, 0, piece).start()
            user_relay(z, 0).start()
        elif i < blocks - 1:
            pass_on(2 * i - 2)
        if i == blocks // 2 - 1:
            direct(0)
    direct(1)
    user_relay(z, 1).start()
    for load in loads[3:]:
        load.wait()
    item_w = dot_t(items[...], w_out[...]).astype(jnp.bfloat16)
    all_relays(0).wait_recv()
    table_x = dot_t(users[:, :, 0:D].reshape(2 * side, D), items[...])
    for k in order:
        zz = (z + k) % nz
        direct_landed(zz)
        user_relay(zz, 1).start()
    all_relays(1).wait_recv()

    index = user_ref[...]
    source = (index % slots) // 2
    place = (source % CORES) * side + (source // CORES) * slots + index // slots * 2 + index % 2
    table = table_x + dot_t(users[:, :, D : D + WIDTH].reshape(2 * side, WIDTH), item_w)
    imps = index.shape[1]
    picked = lax.broadcasted_iota(jnp.int32, (2 * side, imps), 0) == place
    logits = jnp.sum(jnp.where(picked, table, 0.0), 0, keepdims=True)
    logit_ref[...] = logits
    logit_out = pltpu.make_async_copy(logit_ref, logit_hbm, out_sem.at[0])
    logit_out.start()
    error = sigmoid(logits) - label_ref[...].astype(jnp.float32)

    line = lax.broadcasted_iota(jnp.int32, (side, imps), 0)

    def pool_side(core):
        weight = jnp.where(line + core * side == place, error, 0.0).astype(jnp.bfloat16)
        return dot(weight, item_w).reshape(nz, slots, WIDTH)

    pool_send[...] = pool_side(other).astype(jnp.bfloat16)
    pool_copy = copy(pool_send, pool_core, pool_sem.at[0], pool_sem.at[1], sibling)
    pool_copy.start()
    pool_mine[...] = pool_side(c)
    turned = users[:, :, D : D + WIDTH].reshape(2 * side, WIDTH).astype(jnp.float32).T.astype(jnp.bfloat16)
    pool_copy.wait()
    pool_z[...] = (pool_mine[...] + pool_core[...].astype(jnp.float32)).astype(jnp.bfloat16)
    for k in range(1, nz):
        copy(pool_z.at[(z + k) % nz], pool_got.at[z], pool_sem.at[2], pool_sem.at[3], z_id(k)).start()
    pool_got[z] = pool_z[z]

    chosen = dot(turned, picked.astype(jnp.bfloat16))
    chosen = (chosen * error).astype(jnp.bfloat16)

    def columns(core, first=0, size=half_w):
        step = min(size, part_w)
        return pl.ds(pl.multiple_of(core * half_w + first, step), size)

    places = ((out_ref, 0, half_w), (gate_ref, 0, part_w), (gate_ref, part_w, part_w))
    block = WIDTH // nr
    CORE, PLANE, PIECE, BACK, WIDE, LAST = range(6)

    def sems(n, stage):
        return sum_send.at[n, stage], sum_recv.at[n, stage]

    def core_copy(n):
        return copy(sums[n][1], sums[n][2], *sems(n, CORE), sibling)

    def core_start(n, part):
        sums[n][1][...] = part.astype(jnp.bfloat16)
        core_copy(n).start()

    def plane_rows(k):
        return pl.ds(pl.multiple_of((rep + k) % nr * block, block), block)

    def core_end(n):
        mine, _, core_got, half, plane_got = sums[n][:5]
        core_copy(n).wait()
        half[...] = (mine[...] + core_got[...].astype(jnp.float32)).astype(jnp.bfloat16)
        for k in range(1, nr):
            copy(half.at[plane_rows(k)], plane_got.at[rep], *sems(n, PLANE), plane_id(k)).start()
        plane_got[rep] = half[plane_rows(0), :]

    def plane_all(n):
        return copy(sums[n][3].at[pl.ds(0, block * (nr - 1))], sums[n][4].at[pl.ds(0, nr - 1)], *sems(n, PLANE), sibling)

    def piece_spot(n, zz):
        across = places[n][2] // LANES
        tall = block * across // nz
        return (
            pl.ds(pl.multiple_of(zz // across * tall, tall), tall),
            pl.ds(pl.multiple_of(zz % across * LANES, LANES), LANES),
        )

    def plane_end(n):
        plane_got, row_sum, piece_got = sums[n][4:7]
        plane_all(n).wait_recv()
        total = plane_got[0].astype(jnp.float32)
        for k in range(1, nr):
            total += plane_got[k].astype(jnp.float32)
        row_sum[...] = total
        for k in range(1, nz):
            copy(row_sum.at[piece_spot(n, (z + k) % nz)], piece_got.at[z], *sems(n, PIECE), z_id(k)).start()
        piece_got[z] = row_sum[piece_spot(n, z)]

    def piece_all(n):
        spot = sums[n][6].at[pl.ds(0, nz - 1)]
        return copy(spot, spot, *sems(n, PIECE), sibling)

    def piece_end(n):
        piece_got, final = sums[n][6:8]
        piece_all(n).wait_recv()
        total = piece_got[0]
        for k in range(1, nz):
            total += piece_got[k]
        spot = final.at[piece_spot(n, z)]
        spot[...] = total
        for k in range(1, nz):
            copy(spot, spot, *sems(n, BACK), z_id(k)).start()

    def back_all(n):
        spot = sums[n][6].at[pl.ds(0, nz - 1)]
        return copy(spot, spot, *sems(n, BACK), sibling)

    def wide_spot(n, core, k):
        ref, first, size = places[n]
        return ref.at[plane_rows(k), columns(core, first, size)]

    def back_end(n):
        back_all(n).wait_recv()
        spot = wide_spot(n, c, 0)
        spot[...] = sums[n][7][...].astype(jnp.bfloat16)
        for k in range(1, nr):
            copy(spot, spot, *sems(n, WIDE), plane_id(k)).start()

    def wide_all(n):
        ref, first, size = places[n]
        spot = ref.at[pl.ds(0, block * (nr - 1)), columns(c, first, size)]
        return copy(spot, spot, *sems(n, WIDE), sibling)

    def last_copy(n, core):
        ref, first, size = places[n]
        spot = ref.at[:, columns(core, first, size)]
        return copy(spot, spot, *sems(n, LAST), sibling)

    def wide_end(n):
        wide_all(n).wait_recv()
        last_copy(n, c).start()

    core_start(0, dot(chosen, items[:, columns(other)]))
    sums[0][0][...] = dot(chosen, items[:, columns(c)])
    core_end(0)

    pool_spot = pool_got.at[pl.ds(0, nz - 1)]
    pool_all = copy(pool_spot, pool_spot, pool_sem.at[2], pool_sem.at[3], sibling)
    pool_all.wait_recv()
    total = pool_got[0].astype(jnp.float32)
    for k in range(1, nz):
        total += pool_got[k].astype(jnp.float32)
    pool_t = total.astype(jnp.bfloat16).astype(jnp.float32).T.astype(jnp.bfloat16)
    tokens = slots * HIST
    slot = lax.broadcasted_iota(jnp.int32, (slots, tokens), 0)
    event = lax.broadcasted_iota(jnp.int32, (slots, tokens), 1)
    holds = (event // HIST == slot).astype(jnp.bfloat16)
    pre[...] = (dot(pool_t, holds) * slope[...].astype(jnp.float32)).astype(jnp.bfloat16)
    gate_part = dot(pre[...], x[:, columns(other)])
    core_start(1, gate_part[:, 0:part_w])
    core_start(2, gate_part[:, part_w:half_w])
    plane_end(0)
    gate_part = dot(pre[...], x[:, columns(c)])
    sums[1][0][...] = gate_part[:, 0:part_w]
    core_end(1)
    sums[2][0][...] = gate_part[:, part_w:half_w]
    core_end(2)
    piece_end(0)
    plane_end(1)
    back_end(0)
    plane_end(2)
    piece_end(1)
    piece_end(2)
    back_end(1)
    wide_end(0)
    back_end(2)
    wide_end(1)
    wide_end(2)

    def strips(n):
        ref, first, size = places[n]
        target = gate_hbm if n else out_hbm
        return [
            pltpu.make_async_copy(
                ref.at[:, core * half_w + first : core * half_w + first + size],
                target.at[:, core * half_w + first : core * half_w + first + size],
                out_sem.at[1 + n * CORES + core],
            )
            for core in range(CORES)
        ]

    for n in range(3):
        last_copy(n, other).wait()
        for strip in strips(n):
            strip.start()
    spot = users.at[pl.ds(0, nz - 1), :, 0:D]
    copy(spot, spot, user_send, user_recv.at[0], sibling).wait_send()
    spot = users.at[pl.ds(0, nz - 1), :, D : D + WIDTH]
    copy(spot, spot, py_send, py_recv.at[0], sibling).wait_send()
    for k in range(2):
        all_relays(k).wait_send()
    pool_all.wait_send()
    for n in range(3):
        plane_all(n).wait_send()
        piece_all(n).wait_send()
        back_all(n).wait_send()
        wide_all(n).wait_send()
    logit_out.wait()
    for n in range(3):
        for strip in strips(n):
            strip.wait()


def train_step(histories, lengths, counts, imp_user, items, labels, w_uvqk, w_out):
    nz = lax.axis_size("own") // CORES
    nr = lax.axis_size("rep")
    slots = histories.shape[0]
    tokens = slots * HIST
    blocks = tokens // STEP
    imps = imp_user.shape[0]
    half_w = D // CORES
    bf16, f32 = jnp.bfloat16, jnp.float32
    hbm = pl.BlockSpec(memory_space=pltpu.HBM)
    dma = pltpu.SemaphoreType.DMA
    sums = []
    for size in (half_w, half_w // 2, half_w // 2):
        block = WIDTH // nr
        sums += [
            pltpu.VMEM((WIDTH, size), f32),
            pltpu.VMEM((WIDTH, size), bf16),
            pltpu.VMEM((WIDTH, size), bf16),
            pltpu.VMEM((WIDTH, size), bf16),
            pltpu.VMEM((nr, block, size), bf16),
            pltpu.VMEM((block, size), f32),
            pltpu.VMEM((nz, block * size // nz // LANES, LANES), f32),
            pltpu.VMEM((block, size), f32),
        ]
    return pl.pallas_call(
        functools.partial(step_kernel, nz, nr),
        in_specs=[hbm] * 8,
        out_specs=[hbm] * 3,
        out_shape=[
            jax.ShapeDtypeStruct((1, imps), f32),
            jax.ShapeDtypeStruct((WIDTH, D), bf16),
            jax.ShapeDtypeStruct((WIDTH, D), bf16),
        ],
        scratch_shapes=[
            pltpu.VMEM((1, imps), jnp.int32),
            pltpu.VMEM((1, imps), jnp.int32),
            pltpu.VMEM(items.shape, bf16),
            pltpu.VMEM(w_out.shape, bf16),
            pltpu.VMEM(w_uvqk.shape, bf16),
            pltpu.VMEM((tokens, D), bf16),
            pltpu.VMEM((WIDTH, tokens), bf16),
            pltpu.VMEM((STEP, 4 * WIDTH), f32),
            pltpu.VMEM((STEP, 4 * WIDTH), f32),
            pltpu.VMEM((slots, WIDTH), f32),
            pltpu.VMEM((1, imps), f32),
            pltpu.VMEM((WIDTH, D), bf16),
            pltpu.VMEM((WIDTH, D), bf16),
            pltpu.VMEM((CORES * nz, slots, D + WIDTH), bf16),
            pltpu.VMEM((nz, slots, WIDTH), bf16),
            pltpu.VMEM((nz, slots, WIDTH), bf16),
            pltpu.VMEM((nz, slots, WIDTH), f32),
            pltpu.VMEM((nz, slots, WIDTH), bf16),
            pltpu.VMEM((nz, slots, WIDTH), bf16),
            pltpu.VMEM((WIDTH, tokens), bf16),
            *sums,
            pltpu.SMEM(lengths.shape, jnp.int32),
            pltpu.SMEM(counts.shape, jnp.int32),
            dma((6,)), dma((blocks,)), dma((4,)), dma((1 + 3 * CORES,)),
            dma(()), dma((nz * PARTS,)), dma(()), dma((2 * nz,)), dma((4,)), dma((4,)),
            dma((3, 6)), dma((3, 6)),
        ],
        compiler_params=pltpu.CompilerParams(
            collective_id=0, has_side_effects=True, vmem_limit_bytes=58 * 1024 * 1024
        ),
        name="train_step",
    )(
        imp_user[None], labels[None], lengths, counts, items, w_out, w_uvqk, histories.reshape(tokens, D)
    )


def finish_kernel(logit_in, out_in, gate_in, logit_out, out_out, gate_out, turned, rows, flat, logit, sem):
    pieces = gate_in.shape[0] // LANES

    def moves(source, between, target, k):
        return (
            pltpu.make_async_copy(source, between, sem.at[0, k]),
            pltpu.make_async_copy(between, target, sem.at[1, k]),
        )

    def part(k):
        return pl.ds(k * LANES, LANES)

    gate_in_moves = [
        pltpu.make_async_copy(gate_in.at[part(k)], rows.at[part(k)], sem.at[0, k]) for k in range(pieces)
    ]
    out_moves = [
        moves(out_in.at[part(k)], flat.at[part(k)], out_out.at[part(k)], pieces + k) for k in range(pieces)
    ]
    logit_moves = moves(logit_in, logit, logit_out, 2 * pieces)
    for load in gate_in_moves:
        load.start()
    for load, _ in out_moves:
        load.start()
    logit_moves[0].start()
    for k in range(pieces):
        gate_in_moves[k].wait()
        turned[:, k * LANES : (k + 1) * LANES] = rows[part(k), :].astype(jnp.float32).T.astype(jnp.bfloat16)
        out_moves[k][0].wait()
        out_moves[k][1].start()
    last = pltpu.make_async_copy(turned, gate_out, sem.at[1, 0])
    last.start()
    logit_moves[0].wait()
    logit_moves[1].start()
    for _, store in out_moves:
        store.wait()
    logit_moves[1].wait()
    last.wait()


def finish(logits, grad_out, gate_t):
    hbm = pl.BlockSpec(memory_space=pltpu.HBM)
    across, deep = gate_t.shape
    return pl.pallas_call(
        finish_kernel,
        in_specs=[hbm] * 3,
        out_specs=[hbm] * 3,
        out_shape=[
            jax.ShapeDtypeStruct(logits.shape, logits.dtype),
            jax.ShapeDtypeStruct(grad_out.shape, grad_out.dtype),
            jax.ShapeDtypeStruct((deep, across), gate_t.dtype),
        ],
        scratch_shapes=[
            pltpu.VMEM((deep, across), gate_t.dtype),
            pltpu.VMEM((across, deep), gate_t.dtype),
            pltpu.VMEM(grad_out.shape, grad_out.dtype),
            pltpu.VMEM(logits.shape, logits.dtype),
            pltpu.SemaphoreType.DMA((2, 1 + 2 * across // LANES)),
        ],
        compiler_params=pltpu.CompilerParams(vmem_limit_bytes=58 * 1024 * 1024),
        name="finish",
    )(logits, grad_out, gate_t)


def body(histories, lengths, counts, imp_user, items, labels, w_uvqk, w_out):
    logits, grad_out, grad_gate = finish(
        *train_step(histories, lengths, counts, imp_user, items, labels, w_uvqk, w_out)
    )
    return (logits[0], grad_out, grad_gate)


def solution(mesh):
    return jax.shard_map(
        body,
        mesh=mesh,
        in_specs=(
            P(("own", "rep"), None, None),
            P(("own", "rep")),
            P(("own", "rep")),
            P(("own", "rep")),
            P(("own", "rep"), None),
            P(("own", "rep")),
            P(),
            P(),
        ),
        out_specs=(P(("own", "rep")), P(), P()),
        check_vma=False,
    )
```

```python
import functools

import jax
import jax.numpy as jnp
from jax import lax
from jax.experimental import pallas as pl
from jax.experimental.pallas import tpu as pltpu
from jax.sharding import PartitionSpec as P

D = 1024
HEADS = 4
HEAD = 128
HIST = 64
WIDTH = HEADS * HEAD
BIN = 128
STEP = 512
CORES = 2
LANES = 128
PARTS = 2
MESH = pl.DeviceIdType.MESH

EPS_NORM = 1e-06
EPS_LAYER = 1e-05


def sigmoid(v):
    return 0.5 * jnp.tanh(0.5 * v) + 0.5


def dot(a, b):
    return jnp.dot(a, b, preferred_element_type=jnp.float32)


def dot_t(a, b):
    return lax.dot_general(a, b, (((1,), (1,)), ((), ())), preferred_element_type=jnp.float32)


def step_kernel(
    nz, nr, imp_hbm, label_hbm, lengths_hbm, counts_hbm, items_hbm, w_out_hbm, w_hbm, h_hbm,
    logit_hbm, out_hbm, gate_hbm,
    user_ref, label_ref, items, w_out, w, x, slope, even, odd, sum_y, logit_ref, out_ref, gate_ref,
    users, pool_send, pool_core, pool_mine, pool_z, pool_got, pre, *rest,
):
    per_sum = 8
    sums = [rest[n * per_sum : (n + 1) * per_sum] for n in range(3)]
    (
        lengths, counts, load_sem, h_sem, w_sem, out_sem,
        user_send, user_recv, py_send, py_recv, relay_sem, pool_sem, sum_send, sum_recv,
    ) = rest[3 * per_sum :]
    own = lax.axis_index("own")
    rep = lax.axis_index("rep")
    z, c = own // CORES, own % CORES
    other = 1 - c
    slots = users.shape[1]
    side = nz * slots
    half_w = D // CORES
    part_w = half_w // 2
    blocks = slots * HIST // STEP
    step_bins = STEP // BIN
    step_slots = STEP // HIST
    linear = (even, odd)

    def block_rows(i):
        return slice(i * STEP, (i + 1) * STEP)

    def part(n):
        return slice(n * WIDTH, (n + 1) * WIDTH)

    h_loads = [
        pltpu.make_async_copy(h_hbm.at[block_rows(i)], x.at[block_rows(i)], h_sem.at[i]) for i in range(blocks)
    ]
    w_loads = [pltpu.make_async_copy(w_hbm.at[:, part(n)], w.at[:, part(n)], w_sem.at[n]) for n in range(4)]
    loads = [
        pltpu.make_async_copy(source, target, load_sem.at[k])
        for k, (source, target) in enumerate(
            (
                (lengths_hbm, lengths), (counts_hbm, counts), (w_out_hbm, w_out), (items_hbm, items),
                (imp_hbm, user_ref), (label_hbm, label_ref),
            )
        )
    ]
    h_loads[0].start()
    for load in w_loads:
        load.start()
    for load in loads[:2] + h_loads[1:] + loads[2:]:
        load.start()

    def z_id(k):
        return ((z + k) % nz * CORES + c, rep)

    def plane_id(k):
        return (own, (rep + k) % nr)

    sibling = (z * CORES + other, rep)

    def copy(source, target, send, recv, device):
        return pltpu.make_async_remote_copy(
            src_ref=source, dst_ref=target, send_sem=send, recv_sem=recv,
            device_id=device, device_id_type=MESH,
        )

    def signal(device):
        pl.semaphore_signal(barrier, inc=1, device_id=device, device_id_type=MESH)

    barrier = pltpu.get_barrier_semaphore()
    for k in range(1, nz):
        signal(z_id(k))
    for k in range(1, nr):
        signal(plane_id(k))
    signal(sibling)

    at = c * nz + z
    reach = nz // 2
    width = D // PARTS
    ends = (z_id(1), z_id(nz - 1))

    def origin(way, step):
        return (z + nz - step if way == 0 else z + step) % nz

    def hop(way, step, part):
        spot = users.at[c * nz + origin(way, step), :, part * width : (part + 1) * width]
        return copy(spot, spot, user_send, user_recv.at[(way * reach + step) * PARTS + part], ends[way])

    def landed(way, step, part):
        spot = users.at[c * nz + origin(way, step + 1), :, part * width : (part + 1) * width]
        copy(spot, spot, user_send, user_recv.at[(way * reach + step) * PARTS + part], ends[way]).wait_recv()

    def goes(way, step, part):
        return step < reach - 1 or part % 2 == way

    def pass_on(step):
        for piece in range(PARTS):
            for way in range(2):
                if goes(way, step, piece):
                    landed(way, step, piece)
                if step + 1 < reach and goes(way, step + 1, piece):
                    hop(way, step + 1, piece).start()
        user_relay(origin(0, step + 1), 0).start()
        if step + 1 < reach:
            user_relay(origin(1, step + 1), 0).start()

    def user_relay(zz, k):
        spot = users.at[c * nz + zz, :, D * k : D + WIDTH * k]
        return copy(spot, spot, relay_sem.at[2 * k], relay_sem.at[2 * k + 1], sibling)

    def all_relays(k):
        cols = slice(D * k, D + WIDTH * k)
        return copy(
            users.at[pl.ds(c * nz, nz), :, cols], users.at[pl.ds(other * nz, nz), :, cols],
            relay_sem.at[2 * k], relay_sem.at[2 * k + 1], sibling,
        )

    order = [k for near in range(1, reach) for k in (near, nz - near)] + [reach]
    some = slots // 2

    def direct(g):
        rows = slice(g * some, (g + 1) * some)
        users[at, rows, D : D + WIDTH] = sum_y[rows, :].astype(jnp.bfloat16)
        spot = users.at[at, rows, D : D + WIDTH]
        for k in order:
            copy(spot, spot, py_send, py_recv.at[g * nz + z], z_id(k)).start()

    def direct_landed(zz):
        for g in range(2):
            spot = users.at[c * nz + zz, g * some : (g + 1) * some, D : D + WIDTH]
            copy(spot, spot, py_send, py_recv.at[g * nz + zz], sibling).wait_recv()

    def project(i, n):
        linear[i % 2][:, part(n)] = dot(x[block_rows(i), :], w[:, part(n)])

    def span_of(s):
        return jnp.where(s % 2 < counts[s // 2], lengths[s], 0)

    def one_bin(i, k):
        b = i * step_bins + k
        source = linear[i % 2]
        rows = slice(k * BIN, (k + 1) * BIN)
        first, second = span_of(2 * b), span_of(2 * b + 1)
        feats = x[b * BIN : (b + 1) * BIN, :].astype(jnp.float32)
        half_scale = 0.5 * lax.rsqrt(jnp.mean(feats * feats, -1, keepdims=True) + EPS_NORM)
        row = lax.broadcasted_iota(jnp.int32, (BIN, BIN), 0)
        col = lax.broadcasted_iota(jnp.int32, (BIN, BIN), 1)
        allowed = (
            (col <= row) & ((row < HIST) | (col >= HIST)) & (col < jnp.where(col < HIST, first, HIST + second))
        )
        span = jnp.where(row < HIST, first, second)
        share = jnp.where(row % HIST < span, 1.0 / jnp.maximum(span, 1).astype(jnp.float32), 0.0)
        back = share * half_scale

        def half_of(m, h):
            at = m * WIDTH + h * HEAD
            return source[rows, at : at + HEAD] * half_scale

        attended = []
        for h in range(HEADS):
            value, query, key = [
                (half * jnp.tanh(half) + half).astype(jnp.bfloat16) for half in (half_of(m, h) for m in (1, 2, 3))
            ]
            half = dot_t(query, key) * (0.5 * HEAD ** (-0.5))
            attn = jnp.where(allowed, half * jnp.tanh(half) + half, 0.0).astype(jnp.bfloat16)
            attended.append(dot(attn, value))
        center = jnp.sum(sum(attended), -1, keepdims=True) / WIDTH
        moved = [a - center for a in attended]
        spread = jnp.sum(sum(a * a for a in moved), -1, keepdims=True) / WIDTH
        norm = lax.rsqrt(spread + EPS_LAYER)
        for h in range(HEADS):
            cols = slice(h * HEAD, (h + 1) * HEAD)
            half = half_of(0, h)
            t = jnp.tanh(half)
            normal = moved[h] * norm
            mixed = share * normal * (half * t + half)
            for j in range(2):
                s = 2 * b + j
                sum_y[s : s + 1, cols] = jnp.sum(mixed[j * HIST : (j + 1) * HIST], 0, keepdims=True)
            falls = back * normal * ((1.0 + t) * (1.0 + half * (1.0 - t)))
            slope[cols, b * BIN : (b + 1) * BIN] = falls.T.astype(jnp.bfloat16)

    def pool_x(i):
        slot = lax.broadcasted_iota(jnp.int32, (step_slots, STEP), 0)
        event = lax.broadcasted_iota(jnp.int32, (step_slots, STEP), 1) - slot * HIST
        which = lax.broadcasted_iota(jnp.int32, (step_slots, 1), 0)
        span = jnp.zeros((step_slots, 1), jnp.int32)
        for j in range(step_slots):
            span = jnp.where(which == j, span_of(i * step_slots + j), span)
        live = ((event >= 0) & (event < span)).astype(jnp.bfloat16)
        inverse = 1.0 / jnp.maximum(span, 1).astype(jnp.float32)
        return dot(live, x[block_rows(i), :]) * inverse

    h_loads[0].wait()
    for n in range(4):
        w_loads[n].wait()
        project(0, n)
    for load in loads[:3]:
        load.wait()
    for i in range(blocks):
        if i == 0:
            for load in h_loads[1:]:
                load.wait()
        for k in range(step_bins):
            if i + 1 < blocks:
                project(i + 1, k)
            one_bin(i, k)
            if k == step_bins // 2 - 1 and i >= 2:
                pass_on(2 * i - 3)
        if i == 0:
            px = jnp.concatenate([pool_x(j) for j in range(blocks)], 0)
            users[at, :, 0:D] = px.astype(jnp.bfloat16)
            pl.semaphore_wait(barrier, nz - 1 + nr - 1 + 1)
            for piece in range(PARTS):
                for way in range(2):
                    hop(way, 0, piece).start()
            user_relay(z, 0).start()
        elif i < blocks - 1:
            pass_on(2 * i - 2)
        if i == blocks // 2 - 1:
            direct(0)
    direct(1)
    user_relay(z, 1).start()
    for load in loads[3:]:
        load.wait()
    item_w = dot_t(items[...], w_out[...]).astype(jnp.bfloat16)
    all_relays(0).wait_recv()
    table_x = dot_t(users[:, :, 0:D].reshape(2 * side, D), items[...])
    for k in order:
        zz = (z + k) % nz
        direct_landed(zz)
        user_relay(zz, 1).start()
    all_relays(1).wait_recv()

    index = user_ref[...]
    source = (index % slots) // 2
    place = (source % CORES) * side + (source // CORES) * slots + index // slots * 2 + index % 2
    table = table_x + dot_t(users[:, :, D : D + WIDTH].reshape(2 * side, WIDTH), item_w)
    imps = index.shape[1]
    picked = lax.broadcasted_iota(jnp.int32, (2 * side, imps), 0) == place
    logits = jnp.sum(jnp.where(picked, table, 0.0), 0, keepdims=True)
    logit_ref[...] = logits
    logit_out = pltpu.make_async_copy(logit_ref, logit_hbm, out_sem.at[0])
    logit_out.start()
    error = sigmoid(logits) - label_ref[...].astype(jnp.float32)

    line = lax.broadcasted_iota(jnp.int32, (side, imps), 0)

    def pool_side(core):
        weight = jnp.where(line + core * side == place, error, 0.0).astype(jnp.bfloat16)
        return dot(weight, item_w).reshape(nz, slots, WIDTH)

    pool_send[...] = pool_side(other).astype(jnp.bfloat16)
    pool_copy = copy(pool_send, pool_core, pool_sem.at[0], pool_sem.at[1], sibling)
    pool_copy.start()
    pool_mine[...] = pool_side(c)
    turned = users[:, :, D : D + WIDTH].reshape(2 * side, WIDTH).astype(jnp.float32).T.astype(jnp.bfloat16)
    pool_copy.wait()
    pool_z[...] = (pool_mine[...] + pool_core[...].astype(jnp.float32)).astype(jnp.bfloat16)
    for k in range(1, nz):
        copy(pool_z.at[(z + k) % nz], pool_got.at[z], pool_sem.at[2], pool_sem.at[3], z_id(k)).start()
    pool_got[z] = pool_z[z]

    chosen = dot(turned, picked.astype(jnp.bfloat16))
    chosen = (chosen * error).astype(jnp.bfloat16)

    def columns(core, first=0, size=half_w):
        step = min(size, part_w)
        return pl.ds(pl.multiple_of(core * half_w + first, step), size)

    places = ((out_ref, 0, half_w), (gate_ref, 0, part_w), (gate_ref, part_w, part_w))
    block = WIDTH // nr
    CORE, PLANE, PIECE, BACK, WIDE, LAST = range(6)

    def sems(n, stage):
        return sum_send.at[n, stage], sum_recv.at[n, stage]

    def core_copy(n):
        return copy(sums[n][1], sums[n][2], *sems(n, CORE), sibling)

    def core_start(n, part):
        sums[n][1][...] = part.astype(jnp.bfloat16)
        core_copy(n).start()

    def plane_rows(k):
        return pl.ds(pl.multiple_of((rep + k) % nr * block, block), block)

    def core_end(n):
        mine, _, core_got, half, plane_got = sums[n][:5]
        core_copy(n).wait()
        half[...] = (mine[...] + core_got[...].astype(jnp.float32)).astype(jnp.bfloat16)
        for k in range(1, nr):
            copy(half.at[plane_rows(k)], plane_got.at[rep], *sems(n, PLANE), plane_id(k)).start()
        plane_got[rep] = half[plane_rows(0), :]

    def plane_all(n):
        return copy(sums[n][3].at[pl.ds(0, block * (nr - 1))], sums[n][4].at[pl.ds(0, nr - 1)], *sems(n, PLANE), sibling)

    def piece_spot(n, zz):
        across = places[n][2] // LANES
        tall = block * across // nz
        return (
            pl.ds(pl.multiple_of(zz // across * tall, tall), tall),
            pl.ds(pl.multiple_of(zz % across * LANES, LANES), LANES),
        )

    def plane_end(n):
        plane_got, row_sum, piece_got = sums[n][4:7]
        plane_all(n).wait_recv()
        total = plane_got[0].astype(jnp.float32)
        for k in range(1, nr):
            total += plane_got[k].astype(jnp.float32)
        row_sum[...] = total
        for k in range(1, nz):
            copy(row_sum.at[piece_spot(n, (z + k) % nz)], piece_got.at[z], *sems(n, PIECE), z_id(k)).start()
        piece_got[z] = row_sum[piece_spot(n, z)]

    def piece_all(n):
        spot = sums[n][6].at[pl.ds(0, nz - 1)]
        return copy(spot, spot, *sems(n, PIECE), sibling)

    def piece_end(n):
        piece_got, final = sums[n][6:8]
        piece_all(n).wait_recv()
        total = piece_got[0]
        for k in range(1, nz):
            total += piece_got[k]
        spot = final.at[piece_spot(n, z)]
        spot[...] = total
        for k in range(1, nz):
            copy(spot, spot, *sems(n, BACK), z_id(k)).start()

    def back_all(n):
        spot = sums[n][6].at[pl.ds(0, nz - 1)]
        return copy(spot, spot, *sems(n, BACK), sibling)

    def wide_spot(n, core, k):
        ref, first, size = places[n]
        return ref.at[plane_rows(k), columns(core, first, size)]

    def back_end(n):
        back_all(n).wait_recv()
        spot = wide_spot(n, c, 0)
        spot[...] = sums[n][7][...].astype(jnp.bfloat16)
        for k in range(1, nr):
            copy(spot, spot, *sems(n, WIDE), plane_id(k)).start()

    def wide_all(n):
        ref, first, size = places[n]
        spot = ref.at[pl.ds(0, block * (nr - 1)), columns(c, first, size)]
        return copy(spot, spot, *sems(n, WIDE), sibling)

    def last_copy(n, core):
        ref, first, size = places[n]
        spot = ref.at[:, columns(core, first, size)]
        return copy(spot, spot, *sems(n, LAST), sibling)

    def wide_end(n):
        wide_all(n).wait_recv()
        last_copy(n, c).start()

    core_start(0, dot(chosen, items[:, columns(other)]))
    sums[0][0][...] = dot(chosen, items[:, columns(c)])
    core_end(0)

    pool_spot = pool_got.at[pl.ds(0, nz - 1)]
    pool_all = copy(pool_spot, pool_spot, pool_sem.at[2], pool_sem.at[3], sibling)
    pool_all.wait_recv()
    total = pool_got[0].astype(jnp.float32)
    for k in range(1, nz):
        total += pool_got[k].astype(jnp.float32)
    pool_t = total.astype(jnp.bfloat16).astype(jnp.float32).T.astype(jnp.bfloat16)
    tokens = slots * HIST
    slot = lax.broadcasted_iota(jnp.int32, (slots, tokens), 0)
    event = lax.broadcasted_iota(jnp.int32, (slots, tokens), 1)
    holds = (event // HIST == slot).astype(jnp.bfloat16)
    pre[...] = (dot(pool_t, holds) * slope[...].astype(jnp.float32)).astype(jnp.bfloat16)
    gate_part = dot(pre[...], x[:, columns(other)])
    core_start(1, gate_part[:, 0:part_w])
    core_start(2, gate_part[:, part_w:half_w])
    plane_end(0)
    gate_part = dot(pre[...], x[:, columns(c)])
    sums[1][0][...] = gate_part[:, 0:part_w]
    core_end(1)
    sums[2][0][...] = gate_part[:, part_w:half_w]
    core_end(2)
    piece_end(0)
    plane_end(1)
    plane_end(2)
    back_end(0)
    piece_end(1)
    piece_end(2)
    back_end(1)
    wide_end(0)
    back_end(2)
    wide_end(1)
    wide_end(2)

    def strips(n):
        ref, first, size = places[n]
        target = gate_hbm if n else out_hbm
        return [
            pltpu.make_async_copy(
                ref.at[:, core * half_w + first : core * half_w + first + size],
                target.at[:, core * half_w + first : core * half_w + first + size],
                out_sem.at[1 + n * CORES + core],
            )
            for core in range(CORES)
        ]

    for n in range(3):
        last_copy(n, other).wait()
        for strip in strips(n):
            strip.start()
    spot = users.at[pl.ds(0, nz - 1), :, 0:D]
    copy(spot, spot, user_send, user_recv.at[0], sibling).wait_send()
    spot = users.at[pl.ds(0, nz - 1), :, D : D + WIDTH]
    copy(spot, spot, py_send, py_recv.at[0], sibling).wait_send()
    for k in range(2):
        all_relays(k).wait_send()
    pool_all.wait_send()
    for n in range(3):
        plane_all(n).wait_send()
        piece_all(n).wait_send()
        back_all(n).wait_send()
        wide_all(n).wait_send()
    logit_out.wait()
    for n in range(3):
        for strip in strips(n):
            strip.wait()


def train_step(histories, lengths, counts, imp_user, items, labels, w_uvqk, w_out):
    nz = lax.axis_size("own") // CORES
    nr = lax.axis_size("rep")
    slots = histories.shape[0]
    tokens = slots * HIST
    blocks = tokens // STEP
    imps = imp_user.shape[0]
    half_w = D // CORES
    bf16, f32 = jnp.bfloat16, jnp.float32
    hbm = pl.BlockSpec(memory_space=pltpu.HBM)
    dma = pltpu.SemaphoreType.DMA
    sums = []
    for size in (half_w, half_w // 2, half_w // 2):
        block = WIDTH // nr
        sums += [
            pltpu.VMEM((WIDTH, size), f32),
            pltpu.VMEM((WIDTH, size), bf16),
            pltpu.VMEM((WIDTH, size), bf16),
            pltpu.VMEM((WIDTH, size), bf16),
            pltpu.VMEM((nr, block, size), bf16),
            pltpu.VMEM((block, size), f32),
            pltpu.VMEM((nz, block * size // nz // LANES, LANES), f32),
            pltpu.VMEM((block, size), f32),
        ]
    return pl.pallas_call(
        functools.partial(step_kernel, nz, nr),
        in_specs=[hbm] * 8,
        out_specs=[hbm] * 3,
        out_shape=[
            jax.ShapeDtypeStruct((1, imps), f32),
            jax.ShapeDtypeStruct((WIDTH, D), bf16),
            jax.ShapeDtypeStruct((WIDTH, D), bf16),
        ],
        scratch_shapes=[
            pltpu.VMEM((1, imps), jnp.int32),
            pltpu.VMEM((1, imps), jnp.int32),
            pltpu.VMEM(items.shape, bf16),
            pltpu.VMEM(w_out.shape, bf16),
            pltpu.VMEM(w_uvqk.shape, bf16),
            pltpu.VMEM((tokens, D), bf16),
            pltpu.VMEM((WIDTH, tokens), bf16),
            pltpu.VMEM((STEP, 4 * WIDTH), f32),
            pltpu.VMEM((STEP, 4 * WIDTH), f32),
            pltpu.VMEM((slots, WIDTH), f32),
            pltpu.VMEM((1, imps), f32),
            pltpu.VMEM((WIDTH, D), bf16),
            pltpu.VMEM((WIDTH, D), bf16),
            pltpu.VMEM((CORES * nz, slots, D + WIDTH), bf16),
            pltpu.VMEM((nz, slots, WIDTH), bf16),
            pltpu.VMEM((nz, slots, WIDTH), bf16),
            pltpu.VMEM((nz, slots, WIDTH), f32),
            pltpu.VMEM((nz, slots, WIDTH), bf16),
            pltpu.VMEM((nz, slots, WIDTH), bf16),
            pltpu.VMEM((WIDTH, tokens), bf16),
            *sums,
            pltpu.SMEM(lengths.shape, jnp.int32),
            pltpu.SMEM(counts.shape, jnp.int32),
            dma((6,)), dma((blocks,)), dma((4,)), dma((1 + 3 * CORES,)),
            dma(()), dma((nz * PARTS,)), dma(()), dma((2 * nz,)), dma((4,)), dma((4,)),
            dma((3, 6)), dma((3, 6)),
        ],
        compiler_params=pltpu.CompilerParams(
            collective_id=0, has_side_effects=True, vmem_limit_bytes=58 * 1024 * 1024
        ),
        name="train_step",
    )(
        imp_user[None], labels[None], lengths, counts, items, w_out, w_uvqk, histories.reshape(tokens, D)
    )


def finish_kernel(logit_in, out_in, gate_in, logit_out, out_out, gate_out, turned, rows, flat, logit, sem):
    pieces = gate_in.shape[0] // LANES

    def moves(source, between, target, k):
        return (
            pltpu.make_async_copy(source, between, sem.at[0, k]),
            pltpu.make_async_copy(between, target, sem.at[1, k]),
        )

    def part(k):
        return pl.ds(k * LANES, LANES)

    gate_in_moves = [
        pltpu.make_async_copy(gate_in.at[part(k)], rows.at[part(k)], sem.at[0, k]) for k in range(pieces)
    ]
    out_moves = [
        moves(out_in.at[part(k)], flat.at[part(k)], out_out.at[part(k)], pieces + k) for k in range(pieces)
    ]
    logit_moves = moves(logit_in, logit, logit_out, 2 * pieces)
    for load in gate_in_moves:
        load.start()
    for load, _ in out_moves:
        load.start()
    logit_moves[0].start()
    for k in range(pieces):
        gate_in_moves[k].wait()
        turned[:, k * LANES : (k + 1) * LANES] = rows[part(k), :].astype(jnp.float32).T.astype(jnp.bfloat16)
        out_moves[k][0].wait()
        out_moves[k][1].start()
    last = pltpu.make_async_copy(turned, gate_out, sem.at[1, 0])
    last.start()
    logit_moves[0].wait()
    logit_moves[1].start()
    for _, store in out_moves:
        store.wait()
    logit_moves[1].wait()
    last.wait()


def finish(logits, grad_out, gate_t):
    hbm = pl.BlockSpec(memory_space=pltpu.HBM)
    across, deep = gate_t.shape
    return pl.pallas_call(
        finish_kernel,
        in_specs=[hbm] * 3,
        out_specs=[hbm] * 3,
        out_shape=[
            jax.ShapeDtypeStruct(logits.shape, logits.dtype),
            jax.ShapeDtypeStruct(grad_out.shape, grad_out.dtype),
            jax.ShapeDtypeStruct((deep, across), gate_t.dtype),
        ],
        scratch_shapes=[
            pltpu.VMEM((deep, across), gate_t.dtype),
            pltpu.VMEM((across, deep), gate_t.dtype),
            pltpu.VMEM(grad_out.shape, grad_out.dtype),
            pltpu.VMEM(logits.shape, logits.dtype),
            pltpu.SemaphoreType.DMA((2, 1 + 2 * across // LANES)),
        ],
        compiler_params=pltpu.CompilerParams(vmem_limit_bytes=58 * 1024 * 1024),
        name="finish",
    )(logits, grad_out, gate_t)


def body(histories, lengths, counts, imp_user, items, labels, w_uvqk, w_out):
    logits, grad_out, grad_gate = finish(
        *train_step(histories, lengths, counts, imp_user, items, labels, w_uvqk, w_out)
    )
    return (logits[0], grad_out, grad_gate)


def solution(mesh):
    return jax.shard_map(
        body,
        mesh=mesh,
        in_specs=(
            P(("own", "rep"), None, None),
            P(("own", "rep")),
            P(("own", "rep")),
            P(("own", "rep")),
            P(("own", "rep"), None),
            P(("own", "rep")),
            P(),
            P(),
        ),
        out_specs=(P(("own", "rep")), P(), P()),
        check_vma=False,
    )
```
